32 devices in a mesh: outer: 4 (over x, core), inner: 8 (over z, y).
Axes of the slice: x: 2, y: 2, z: 4, core: 2. Of those that a mesh axis runs over, the one named last changes fastest.
Arguments:
- tokens: bfloat16 [128, 1024, 256], P(('outer', 'inner')), may hold values from -6 to 6
- segment_ids: int32 [128, 1024], P(('outer', 'inner')), may hold values from 0 to 7, never falling along the last dimension, each value on 1 to 512 neighbouring positions
- padding_mask: int32 [128, 1024], P(('outer', 'inner')), may hold values 0 or 1
- joint_weight: bfloat16 [256, 768], P(('outer', 'inner')), may hold values from -0.375 to 0.375
- query_bias: bfloat16 [256], P(('outer', 'inner')), may hold values from -3 to 3
- value_bias: bfloat16 [256], P(('outer', 'inner')), may hold values from -3 to 3
- output_weight: bfloat16 [256, 256], P(('outer', 'inner')), may hold values from -2 to 2
- output_bias: bfloat16 [256], P(('outer', 'inner')), may hold values from -2 to 2
- first_gain: bfloat16 [256], P(('outer', 'inner')), may hold values from 0.099609375 to 1.8984375
- first_shift: bfloat16 [256], P(('outer', 'inner')), may hold values from -2 to 2
- expand_weight: bfloat16 [256, 512], P(('outer', 'inner')), may hold values from -0.375 to 0.375
- expand_bias: bfloat16 [512], P(('outer', 'inner')), may hold values from -3 to 3
- reduce_weight: bfloat16 [512, 256], P(('outer', 'inner')), may hold values from -0.25 to 0.25
- reduce_bias: bfloat16 [256], P(('outer', 'inner')), may hold values from -2 to 2
- second_gain: bfloat16 [256], P(('outer', 'inner')), may hold values from 0.099609375 to 1.8984375
- second_shift: bfloat16 [256], P(('outer', 'inner')), may hold values from -2 to 2
- cotangent: bfloat16 [128, 1024, 256], P(('outer', 'inner')), may hold values from -6 to 6
Outputs:
- layer_out: bfloat16 [128, 1024, 256], P(('outer', 'inner'))
- tokens_gradient: float32 [128, 1024, 256], P(('outer', 'inner'))
- joint_gradient: float32 [256, 768], P(('outer', 'inner'))
- query_bias_gradient: float32 [256], P(('outer', 'inner'))
- value_bias_gradient: float32 [256], P(('outer', 'inner'))
- output_gradient: float32 [256, 256], P(('outer', 'inner'))
- output_bias_gradient: float32 [256], P(('outer', 'inner'))
- first_gain_gradient: float32 [256], P(('outer', 'inner'))
- first_shift_gradient: float32 [256], P(('outer', 'inner'))
- expand_gradient: float32 [256, 512], P(('outer', 'inner'))
- expand_bias_gradient: float32 [512], P(('outer', 'inner'))
- reduce_gradient: float32 [512, 256], P(('outer', 'inner'))
- reduce_bias_gradient: float32 [256], P(('outer', 'inner'))
- second_gain_gradient: float32 [256], P(('outer', 'inner'))
- second_shift_gradient: float32 [256], P(('outer', 'inner'))
The draws below stay inside these ranges and needn't reach their ends.
Inputs may be any that keep to these rules, and one draw needn't show every extreme that they name: `segment_ids`: in each sequence the numbers never fall, each cell holds 1 to 512 tokens, and one cell of each sequence holds exactly 512.
All inputs are finite; a program needn't handle non-finite values. No bound on the sum of `padding_mask` on one device may be relied on, other than what follows from the above.
Results may differ from the reference program's by a relative error of at most 0.012.
The reference program's roundings to bfloat16 on the way count: a program that leaves them out, or rounds other values in their place, can miss the bound.
Values may be sent and summed in bfloat16 or wider, within the bound.
A program may use at most 128 MiB of HBM per device.

```python
import math
import jax
import jax.numpy as jnp
import numpy as np
from jax import lax

D = 256
HEADS = 4
FF = 512
HEAD_DIM = 64
LEN = 1024
SEGMENTS = 8
SEQS = 128


def touch_ends(values, stream_key, least, high):
    longest = values.shape.index(max(values.shape))
    spots = []
    for shift in (0, 1):
        where = [jax.random.randint(jax.random.fold_in(stream_key, axis), (), 0, length) for axis, length in enumerate(values.shape)]
        where[longest] = (where[longest] + shift) % values.shape[longest]
        spots.append(tuple(where))
    return values.at[spots[0]].set(least).at[spots[1]].set(high)


def spiked(drawn, own_key, source, target, blocks, factor):
    owner, partner = [(jnp.arange(drawn.shape[position]) // (drawn.shape[position] // blocks)).reshape([-1 if axis == position else 1 for axis in range(drawn.ndim)]) for position in (source, target)]
    chosen = jax.random.permutation(own_key, blocks)[partner]
    strong = (owner == chosen) | (owner == (partner + blocks // 2) % blocks)
    return jnp.where(strong, factor * drawn, drawn)


def block_scale(rng, dims, split, low, largest):
    def one(axis_at, blocks):
        steps = jax.random.uniform(jax.random.fold_in(jax.random.fold_in(rng, 6), axis_at), (blocks,), jnp.float32, low / len(split), largest / len(split))
        return jnp.repeat(jnp.exp(steps), dims[axis_at] // blocks).reshape((-1,) + (1,) * (len(dims) - axis_at - 1))

    level = one(*split[0])
    for cut in split[1:]:
        level = level * one(*cut)
    return level


def profile(amount, total, bound, lean):
    weights = [(1 << 20) // math.isqrt(rank ** lean) + 1 for rank in range(2, amount + 1)]
    rest, given = total - bound - (amount - 1), [1] * (amount - 1)
    while rest > 0:
        movable = [i for i in range(amount - 1) if given[i] < bound]
        pool, remaining = sum([weights[i] for i in movable]), rest
        for i in movable:
            more = min(bound - given[i], max(1, remaining * weights[i] // pool), rest)
            given[i] = given[i] + more
            rest = rest - more
    return np.array([bound] + given)


def uneven(key, count, total, most, skew):
    if count == 2:
        one = jax.random.randint(key, (), max(1, total - most), min(most, total - 1) + 1)
        return jnp.stack([one, total - one])
    sizes = jnp.asarray(profile(count, total, most, skew), jnp.int32)
    twos = (count - 1) // 2
    donor, receiver = sizes[1:1 + 2 * twos:2], sizes[2:2 + 2 * twos:2]
    slack = jnp.minimum(donor - 1, most - receiver)
    shifted = jax.random.randint(jax.random.fold_in(key, 1), (twos,), 0, 1 << 20) % (slack + 1)
    sizes = sizes.at[1:1 + 2 * twos:2].set(donor - shifted).at[2:2 + 2 * twos:2].set(receiver + shifted)
    return sizes[jax.random.permutation(jax.random.fold_in(key, 2), count)]


def gaussian(own_key, dims, scale, limit, split=(), kind=jnp.bfloat16):
    drawn = jax.random.normal(own_key, dims, jnp.float32) * scale
    if len(split) > 0:
        drawn = block_scale(own_key, dims, split, -0.22, 0.18) * drawn
    return jnp.clip(drawn, min=-limit, max=limit).astype(kind)


def bell_draw_with(key, dims, deviation, reach, split, heavy, held_as=jnp.bfloat16):
    values = deviation * jax.random.normal(key, dims, jnp.float32)
    if split:
        values = values * block_scale(key, dims, split, -0.22, 0.18)
    return jnp.clip(spiked(values, jax.random.fold_in(key, 3), *heavy), -reach, reach).astype(held_as)


def setup_inputs(seed: int = 0) -> dict:
    key_of = jax.random.split(jax.random.key(seed), 18)
    return {
        "tokens": gaussian(key_of[0], (SEQS, LEN, D), 1.0, 6.0, ((0, 32),)),
        "segment_ids": jax.vmap(lambda own: jnp.searchsorted(jnp.cumsum(uneven(own, SEGMENTS, LEN, LEN // 2, 0)), jnp.arange(LEN), side="right"))(jax.random.split(key_of[1], SEQS)).reshape((SEQS, LEN)).astype(jnp.int32),
        "padding_mask": touch_ends((jax.random.randint(key_of[2], (SEQS, LEN), 0, 8) < 7).astype(jnp.int32), jax.random.fold_in(key_of[2], 1), 0, 1),
        "joint_weight": gaussian(key_of[3], (D, 3 * D), D ** -0.5, 0.375, ((0, 32),)),
        "query_bias": gaussian(key_of[4], (D,), 0.5, 3.0, ((0, 32),)),
        "value_bias": gaussian(key_of[5], (D,), 0.5, 3.0, ((0, 32),)),
        "output_weight": gaussian(key_of[6], (D, D), (D // 32) ** -0.5, 2.0, ((0, 32),)),
        "output_bias": gaussian(key_of[7], (D,), 0.3, 2.0, ((0, 32),)),
        "first_gain": jnp.clip(1.0 + 0.18 * jax.random.normal(key_of[8], (D,), jnp.float32), 0.099609375, 1.8984375).astype(jnp.bfloat16),
        "first_shift": gaussian(key_of[9], (D,), 0.3, 2.0, ((0, 32),)),
        "expand_weight": gaussian(key_of[10], (D, FF), D ** -0.5, 0.375, ((0, 32),)),
        "expand_bias": gaussian(key_of[11], (FF,), 0.5, 3.0, ((0, 32),)),
        "reduce_weight": gaussian(key_of[12], (FF, D), FF ** -0.5, 0.25, ((0, 32),)),
        "reduce_bias": gaussian(key_of[13], (D,), 0.3, 2.0, ((0, 32),)),
        "second_gain": jnp.clip(1.0 + 0.18 * jax.random.normal(key_of[14], (D,), jnp.float32), 0.099609375, 1.8984375).astype(jnp.bfloat16),
        "second_shift": gaussian(key_of[15], (D,), 0.3, 2.0, ((0, 32),)),
        "cotangent": bell_draw_with(key_of[16], (SEQS, LEN, D), 1.0, 6.0, ((0, 32),), (0, 2, 32, 2.75)),
    }


@jax.custom_vjp
def low(v):
    return lax.optimization_barrier(v.astype(jnp.bfloat16)).astype(jnp.float32)

@jax.custom_vjp
def low_back(v):
    return v

def low_keep(v):
    return (low(v), None)

def low_pass(kept, grad):
    return (grad,)

def back_keep(v):
    return (v, None)

def back_low(kept, grad):
    return (low(grad),)
low.defvjp(low_keep, low_pass)
low_back.defvjp(back_keep, back_low)
highest = lax.Precision.HIGHEST
norm_epsilon = 1e-06
masked_value = -1e+30

def layer_norm(hidden, gain, shift):
    centred = hidden - lax.optimization_barrier(jnp.mean(hidden, axis=-1, keepdims=True))
    spread = lax.optimization_barrier(jnp.mean(centred * centred, axis=-1, keepdims=True))
    return centred * lax.rsqrt(spread + norm_epsilon) * gain + shift

def attend(joint, segment, padding):
    length = joint.shape[0]
    parts = joint.reshape(length, 3, HEADS, HEAD_DIM)
    queries = parts[:, 0]
    keys = parts[:, 1]
    values = parts[:, 2]
    scores = jnp.einsum('qhe,khe->hqk', queries, keys, precision=highest) * HEAD_DIM ** (-0.5)
    scores = low_back(scores)
    positions = jnp.arange(length)
    same = segment[:, None] == segment[None, :]
    usable = (padding[None, :] == 1) | (positions[:, None] == positions[None, :])
    allowed = same & usable
    masked = jnp.where(allowed[None], scores, masked_value)
    highest_score = lax.optimization_barrier(jnp.max(masked, axis=-1, keepdims=True))
    weights = jnp.exp(masked - highest_score)
    probs = low(weights / lax.optimization_barrier(jnp.sum(weights, axis=-1, keepdims=True)))
    mixed = jnp.einsum('hqk,khe->qhe', probs, values, precision=highest)
    return mixed.reshape(length, D)

def attend_item(item):
    return attend(item[0], item[1], item[2])

def layer(inputs, params, segment, padding):
    joint_weight, query_bias, value_bias, output_weight, output_bias, first_gain, first_shift, expand_weight, expand_bias, reduce_weight, reduce_bias, second_gain, second_shift = params
    joint_bias = jnp.concatenate([query_bias, jnp.zeros_like(query_bias), value_bias])
    joint = jnp.einsum('bld,de->ble', inputs, joint_weight, precision=highest) + joint_bias
    joint = low(low_back(joint))
    mixed = lax.map(jax.checkpoint(attend_item), (joint, segment, padding))
    mixed = low(low_back(mixed))
    branch = low_back(jnp.einsum('bld,de->ble', mixed, output_weight, precision=highest) + output_bias)
    first = layer_norm(inputs + branch, first_gain, first_shift)
    inner = low_back(jnp.einsum('bld,de->ble', low(first), expand_weight, precision=highest) + expand_bias)
    active = low(jax.nn.gelu(inner))
    second = low_back(jnp.einsum('ble,ed->bld', active, reduce_weight, precision=highest) + reduce_bias)
    return layer_norm(first + second, second_gain, second_shift)

def reference(tokens, segment_ids, padding_mask, joint_weight, query_bias, value_bias, output_weight, output_bias, first_gain, first_shift, expand_weight, expand_bias, reduce_weight, reduce_bias, second_gain, second_shift, cotangent):
    params = (joint_weight, query_bias, value_bias, output_weight, output_bias, first_gain, first_shift, expand_weight, expand_bias, reduce_weight, reduce_bias, second_gain, second_shift)
    params = tuple((item.astype(jnp.float32) for item in params))
    group = math.gcd(SEQS, max(1, 4096 // LEN))
    blocks = SEQS // group
    items = (tokens.reshape(blocks, group, LEN, D), segment_ids.reshape(blocks, group, LEN), padding_mask.reshape(blocks, group, LEN), cotangent.reshape(blocks, group, LEN, D))

    def step(totals, item):
        inputs, segment, padding, upstream = item

        def forward(values, weights):
            return layer(values, weights, segment, padding)
        result, pullback = jax.vjp(forward, inputs.astype(jnp.float32), params)
        inputs_grad, params_grad = pullback(upstream.astype(jnp.float32))
        totals = jax.tree.map(jnp.add, totals, params_grad)
        return (totals, (result.astype(jnp.bfloat16), inputs_grad))
    starts = tuple((jnp.zeros_like(item) for item in params))
    totals, (results, inputs_grads) = lax.scan(step, starts, items)
    return (results.reshape(SEQS, LEN, D), inputs_grads.reshape(SEQS, LEN, D), totals[0], totals[1], totals[2], totals[3], totals[4], totals[5], totals[6], totals[7], totals[8], totals[9], totals[10], totals[11], totals[12])
```

```python
import functools
import math

import jax
import jax.numpy as jnp
from jax import lax
from jax.experimental import pallas as pl
from jax.experimental.pallas import tpu as pltpu
from jax.sharding import PartitionSpec as P

HEADS = 4
HEAD_DIM = 64
HALF = 512
CHUNK = 256

norm_epsilon = 1e-06
mask_step = -(2.0**100)
log2_e = math.log2(math.e)
gelu_a = math.sqrt(2.0 / math.pi)
gelu_b = 0.044715

f32 = jnp.float32
bf16 = jnp.bfloat16


def nn(left, right):
    return lax.dot_general(left, right, (((1,), (0,)), ((), ())), preferred_element_type=f32)


def nt(left, right):
    return lax.dot_general(left, right, (((1,), (1,)), ((), ())), preferred_element_type=f32)


def over_features(values):
    return jnp.sum(values, axis=0, keepdims=True)


def big_cell_start(seg_ref, seq, length):
    wanted = seg_ref[seq, HALF - 1]
    low = jnp.int32(0)
    step = HALF
    while step > 1:
        step //= 2
        probe = low + step
        low = jnp.where(seg_ref[seq, probe - 1] < wanted, probe, low)
    last = jnp.minimum(low + HALF - 1, length - 1)
    return jnp.where(seg_ref[seq, last] == wanted, low, HALF)


def compute_kernel(
    seg_smem,
    tokens_ref,
    cot_ref,
    seg_ref,
    pad_ref,
    wj_ref,
    wo_ref,
    we_ref,
    wr_ref,
    bias_ref,
    out_ref,
    tg_ref,
    gj_ref,
    go_ref,
    ge_ref,
    gr_ref,
    gb_ref,
    wjt,
    wot,
    wet,
    wrt,
    bj,
    be,
    bcol,
    vrow,
    turn,
    xtok,
    xT,
    cT,
    jT,
    kaug,
    vaug,
    codeq,
    pT,
    inv,
    mixT,
    hat1,
    rinv1,
    act,
    slow,
    igr,
    flow,
    blow,
    fig,
    mgT,
    jgT,
    dgelu,
    accb,
):
    seq = pl.program_id(0)
    length, width = tokens_ref.shape[1], tokens_ref.shape[2]
    inner_width = we_ref.shape[1]
    scale = HEAD_DIM**-0.5

    @pl.when(seq == 0)
    def _():
        wide = wj_ref[...].astype(f32)
        for part in range(3):
            piece = wide[:, part * width : (part + 1) * width].T
            if part == 0:
                piece = piece * scale
            wjt[part * width : (part + 1) * width, :] = piece.astype(bf16)
        wot[...] = wo_ref[...].astype(f32).T.astype(bf16)
        wet[...] = we_ref[...].astype(f32).T.astype(bf16)
        wrt[...] = wr_ref[...].astype(f32).T.astype(bf16)
        columns = bias_ref[...].astype(f32)

        def spread(at):
            return jnp.broadcast_to(columns[:, at : at + 1], (width, 128))

        bj[0:width, :] = spread(0) * scale
        bj[width : 2 * width, :] = jnp.zeros((width, 128), f32)
        bj[2 * width : 3 * width, :] = spread(1)
        for at in range(6):
            bcol[at, :, :] = spread(2 + at)
        be[0:width, :] = spread(8)
        be[width : 2 * width, :] = spread(9)
        vrow[...] = columns.T[0:8, :]
        gj_ref[...] = jnp.zeros_like(gj_ref)
        go_ref[...] = jnp.zeros_like(go_ref)
        ge_ref[...] = jnp.zeros_like(ge_ref)
        gr_ref[...] = jnp.zeros_like(gr_ref)
        accb[...] = jnp.zeros_like(accb)

    start = big_cell_start(seg_smem, seq, length)

    def turned(ref, tile):
        lanes = slice(tile * 128, (tile + 1) * 128)
        whole = ref[0, :, lanes].astype(f32)
        turn[tile, 0:length, :] = whole
        turn[tile, length : length + HALF, :] = whole[0:HALF]

    def take(tile, rows):
        return turn[tile, pl.ds(start + rows, CHUNK), :]

    tiles = width // 128
    for tile in range(tiles):
        turned(tokens_ref, tile)
    for tile in range(tiles):
        for at in range(0, length, CHUNK):
            piece = take(tile, at)
            xtok[at : at + CHUNK, tile * 128 : (tile + 1) * 128] = piece.astype(bf16)
            xT[tile * 128 : (tile + 1) * 128, at : at + CHUNK] = piece.T.astype(bf16)
    for tile in range(tiles):
        turned(cot_ref, tile)
    for tile in range(tiles):
        for at in range(0, length, CHUNK):
            cT[tile * 128 : (tile + 1) * 128, at : at + CHUNK] = take(tile, at).T.astype(bf16)

    shift = length - start
    segs = jnp.broadcast_to(seg_ref[pl.ds(seq, 1), :].astype(f32), (8, length))
    pads = jnp.broadcast_to(pad_ref[pl.ds(seq, 1), :].astype(f32), (8, length))
    segs = pltpu.roll(segs, shift, 1)[0:1, :]
    pads = pltpu.roll(pads, shift, 1)[0:1, :]
    position = lax.broadcasted_iota(jnp.int32, (1, length), 1)
    digits = [(position // 64) % 8, (position // 8) % 8, position % 8]
    code = lax.broadcasted_iota(jnp.int32, (8, length), 0)
    hidden = (pads == 0.0).astype(f32)
    same = (segs == code.astype(f32)).astype(f32)
    parts_q = [1.0 - same]
    parts_k = [same * mask_step]
    for digit in digits:
        equal = (digit == code).astype(f32)
        parts_q.append(1.0 - equal)
        parts_k.append(equal * hidden * mask_step)
    nothing = jnp.zeros((32, length), f32)
    codeq[...] = jnp.concatenate(parts_q + [nothing], axis=0).astype(bf16)
    codek = jnp.concatenate(parts_k + [nothing] + parts_k + [nothing], axis=0).T

    lane = lax.broadcasted_iota(jnp.int32, (CHUNK, 128), 1)
    low_lanes = lane < HEAD_DIM

    for at in range(0, length, CHUNK):
        rows = slice(at, at + CHUNK)
        made = nn(wjt[...], xT[:, rows])
        for tile in range(CHUNK // 128):
            jT[:, at + tile * 128 : at + (tile + 1) * 128] = (
                made[:, tile * 128 : (tile + 1) * 128] + bj[...]
            ).astype(bf16)
        flat = nn(xtok[rows, :], wj_ref[:, width : 3 * width])
        codes = codek[rows, :]
        for head in range(HEADS):
            lanes = slice((head // 2) * 128, (head // 2 + 1) * 128)
            mine = low_lanes if head % 2 == 0 else ~low_lanes
            keys = flat[:, lanes]
            values = flat[:, width + lanes.start : width + lanes.stop] + vrow[1:2, lanes]
            kaug[head, rows, :] = jnp.where(mine, keys, codes).astype(bf16)
            vaug[head, rows, :] = jnp.where(mine, values, -1.0).astype(bf16)

    ones = jnp.ones((16, HALF), bf16)
    for head in range(HEADS):
        own = slice(head * HEAD_DIM, (head + 1) * HEAD_DIM)
        vrows = slice(2 * width + own.start, 2 * width + own.stop)
        for block in range(length // HALF):
            cols = slice(block * HALF, (block + 1) * HALF)
            place = head * (length // HALF) + block
            for at in range(0, HALF, CHUNK):
                here = slice(block * HALF + at, block * HALF + at + CHUNK)
                pair = [jT[own, here], codeq[:, here]]
                if head % 2 == 1:
                    pair = pair[::-1]
                scores = nn(kaug[head, cols, :], jnp.concatenate(pair, axis=0))
                for tile in range(0, CHUNK, 128):
                    mine = scores[:, tile : tile + 128]
                    highest = jnp.max(mine, axis=0, keepdims=True)
                    pT[place, :, at + tile : at + tile + 128] = jnp.exp2(
                        (mine - highest) * log2_e
                    ).astype(bf16)
            mixed = nn(jnp.concatenate([jT[vrows, cols], ones], axis=0), pT[place])
            inverse = 1.0 / mixed[HEAD_DIM : HEAD_DIM + 1, :]
            inv[head : head + 1, cols] = inverse
            mixT[own, cols] = (mixed[0:HEAD_DIM, :] * inverse).astype(bf16)

    def add_sums(row, values):
        accb[row : row + values.shape[0], :] += values

    def unit(hidden):
        centred = hidden - over_features(hidden) * (1.0 / width)
        inverse = lax.rsqrt(over_features(centred * centred) * (1.0 / width) + norm_epsilon)
        return centred * inverse, inverse

    def unit_back(inside, hat, inverse):
        return inverse * (
            inside
            - over_features(inside) * (1.0 / width)
            - hat * (over_features(inside * hat) * (1.0 / width))
        )

    halves = [slice(t, t + 128) for t in range(0, CHUNK, 128)]
    for at in range(0, length, CHUNK):
        rows = slice(at, at + CHUNK)
        branch = nn(wot[...], mixT[:, rows])
        firsts = []
        for half in halves:
            here = slice(at + half.start, at + half.stop)
            hat, inverse = unit(xT[:, here].astype(f32) + branch[:, half] + bcol[0])
            hat1[:, here] = hat
            rinv1[0:1, here] = inverse
            first = hat * bcol[1] + bcol[2]
            flow[:, here] = first.astype(bf16)
            firsts.append(first)
        inner = nn(wet[...], flow[:, rows])
        for half in halves:
            here = slice(at + half.start, at + half.stop)
            for r in range(0, inner_width, 64):
                u = inner[r : r + 64, half] + be[r : r + 64, :]
                square = u * u
                t = jnp.tanh(u * (gelu_a + (gelu_a * gelu_b) * square))
                h = 0.5 + 0.5 * t
                value = u * h
                act[r : r + 64, here] = value.astype(bf16)
                dgelu[r : r + 64, half] = h + value * (1.0 - h) * (
                    2.0 * gelu_a + (6.0 * gelu_a * gelu_b) * square
                )
        second = nn(wrt[...], act[:, rows])
        grads = []
        for k, half in enumerate(halves):
            here = slice(at + half.start, at + half.stop)
            hat, inverse = unit(firsts[k] + second[:, half] + bcol[3])
            result = (hat * bcol[4] + bcol[5]).T
            for tile in range(tiles):
                piece = result[:, tile * 128 : (tile + 1) * 128]
                turn[tile, HALF + here.start : HALF + here.stop, :] = piece
                if here.start >= HALF:
                    turn[tile, here.start - HALF : here.stop - HALF, :] = piece
            upstream = cT[:, here].astype(f32)
            add_sums(0, upstream * hat)
            add_sums(width, upstream)
            back = unit_back(upstream * bcol[4], hat, inverse)
            low = back.astype(bf16)
            slow[:, here] = low
            add_sums(2 * width, low.astype(f32))
            grads.append(back)
        active_grad = nn(wr_ref[...], slow[:, rows])
        for half in halves:
            here = slice(at + half.start, at + half.stop)
            for r in range(0, inner_width, 64):
                low = (active_grad[r : r + 64, half] * dgelu[r : r + 64, half]).astype(bf16)
                igr[r : r + 64, here] = low
                add_sums(3 * width + r, low.astype(f32))
        deeper = nn(we_ref[...], igr[:, rows])
        for k, half in enumerate(halves):
            here = slice(at + half.start, at + half.stop)
            first_grad = grads[k] + deeper[:, half]
            hat = hat1[:, here]
            base = 3 * width + inner_width
            add_sums(base, first_grad * hat)
            add_sums(base + width, first_grad)
            back = unit_back(first_grad * bcol[1], hat, rinv1[0:1, here])
            fig[:, here] = back
            low = back.astype(bf16)
            blow[:, here] = low
            add_sums(base + 2 * width, low.astype(f32))
        mgT[:, rows] = nn(wo_ref[...], blow[:, rows])

    def untake(tile, at):
        return turn[tile, pl.ds(HALF - start + at, CHUNK), :]

    for tile in range(tiles):
        for at in range(0, length, CHUNK):
            out_ref[0, at : at + CHUNK, tile * 128 : (tile + 1) * 128] = untake(tile, at).astype(
                bf16
            )

    gr_ref[...] += nt(act[...], slow[...])
    ge_ref[...] += nt(flow[...], igr[...])
    go_ref[...] += nt(mixT[...], blow[...])

    for head in range(HEADS):
        own = slice(head * HEAD_DIM, (head + 1) * HEAD_DIM)
        for block in range(length // HALF):
            cols = slice(block * HALF, (block + 1) * HALF)
            place = head * (length // HALF) + block
            grown = mgT[own, cols].astype(bf16).astype(f32)
            inverse = inv[head : head + 1, cols]
            grown = grown * inverse
            dots = over_features(grown * mixT[own, cols].astype(f32))
            high = dots.astype(bf16).astype(f32)
            row = lax.broadcasted_iota(jnp.int32, (16, HALF), 0)
            extra = jnp.where(row == 0, high, jnp.where(row == 1, dots - high, 0.0))
            extra = jnp.concatenate([extra, jnp.zeros((HEAD_DIM - 16, HALF), f32)], axis=0)
            grown = grown.astype(bf16)
            pair = [grown, extra.astype(bf16)]
            if head % 2 == 1:
                pair = pair[::-1]
            upstream = jnp.concatenate(pair, axis=0)
            dsT = (
                pT[place].astype(f32) * nn(vaug[head, cols, :], upstream)
            ).astype(bf16)
            jgT[2 * width + own.start : 2 * width + own.stop, cols] = nt(grown, pT[place]).astype(
                bf16
            )
            keysT = jT[width + own.start : width + own.stop, cols]
            jgT[own, cols] = (nn(keysT, dsT) * scale).astype(bf16)
            jgT[width + own.start : width + own.stop, cols] = nt(jT[own, cols], dsT).astype(bf16)

    gj_ref[...] += nt(xT[...], jgT[...])
    base = 6 * width + inner_width
    for at in range(0, length, 128):
        here = slice(at, at + 128)
        add_sums(base, jgT[0:width, here].astype(f32))
        add_sums(base + width, jgT[2 * width : 3 * width, here].astype(f32))
    for at in range(0, length, CHUNK):
        rows = slice(at, at + CHUNK)
        result = (nn(wj_ref[...], jgT[:, rows]) + fig[:, rows]).T
        for tile in range(tiles):
            piece = result[:, tile * 128 : (tile + 1) * 128]
            turn[tile, HALF + at : HALF + at + CHUNK, :] = piece
            if at >= HALF:
                turn[tile, at - HALF : at - HALF + CHUNK, :] = piece
    for tile in range(tiles):
        for at in range(0, length, CHUNK):
            tg_ref[0, at : at + CHUNK, tile * 128 : (tile + 1) * 128] = untake(tile, at)

    @pl.when(seq == pl.num_programs(0) - 1)
    def _():
        sums = jnp.sum(accb[...], axis=1, keepdims=True)
        gb_ref[...] = jnp.broadcast_to(sums, gb_ref.shape)


def run_compute(tokens, segment_ids, padding_mask, cotangent, wj, wo, we, wr, biases):
    count, length, width = tokens.shape
    inner_width = we.shape[1]
    sums = 8 * width + inner_width
    vmem = pl.BlockSpec(memory_space=pltpu.VMEM)

    def whole(shape):
        return pl.BlockSpec(shape, lambda i: (0,) * len(shape))

    per_seq = pl.BlockSpec((1, length, width), lambda i: (i, 0, 0))
    blocks = HEADS * (length // HALF)
    scratch = [
        pltpu.VMEM((3 * width, width), bf16),
        pltpu.VMEM((width, width), bf16),
        pltpu.VMEM((inner_width, width), bf16),
        pltpu.VMEM((width, inner_width), bf16),
        pltpu.VMEM((3 * width, 128), f32),
        pltpu.VMEM((inner_width, 128), f32),
        pltpu.VMEM((6, width, 128), f32),
        pltpu.VMEM((8, width), f32),
        pltpu.VMEM((width // 128, length + HALF, 128), f32),
        pltpu.VMEM((length, width), bf16),
        pltpu.VMEM((width, length), bf16),
        pltpu.VMEM((width, length), bf16),
        pltpu.VMEM((3 * width, length), bf16),
        pltpu.VMEM((HEADS, length, 128), bf16),
        pltpu.VMEM((HEADS, length, 128), bf16),
        pltpu.VMEM((HEAD_DIM, length), bf16),
        pltpu.VMEM((blocks, HALF, HALF), bf16),
        pltpu.VMEM((8, length), f32),
        pltpu.VMEM((width, length), bf16),
        pltpu.VMEM((width, length), f32),
        pltpu.VMEM((8, length), f32),
        pltpu.VMEM((inner_width, length), bf16),
        pltpu.VMEM((width, length), bf16),
        pltpu.VMEM((inner_width, length), bf16),
        pltpu.VMEM((width, length), bf16),
        pltpu.VMEM((width, length), bf16),
        pltpu.VMEM((width, length), f32),
        pltpu.VMEM((width, length), f32),
        pltpu.VMEM((3 * width, length), bf16),
        pltpu.VMEM((inner_width, CHUNK), f32),
        pltpu.VMEM((sums, 128), f32),
    ]
    shape = jax.ShapeDtypeStruct
    return pl.pallas_call(
        compute_kernel,
        grid=(count,),
        in_specs=[
            pl.BlockSpec(memory_space=pltpu.SMEM),
            per_seq,
            per_seq,
            whole(segment_ids.shape),
            whole(padding_mask.shape),
            whole(wj.shape),
            whole(wo.shape),
            whole(we.shape),
            whole(wr.shape),
            whole(biases.shape),
        ],
        out_specs=[
            per_seq,
            per_seq,
            whole(wj.shape),
            whole(wo.shape),
            whole(we.shape),
            whole(wr.shape),
            whole((sums, 128)),
        ],
        out_shape=[
            shape(tokens.shape, bf16),
            shape(tokens.shape, f32),
            shape(wj.shape, f32),
            shape(wo.shape, f32),
            shape(we.shape, f32),
            shape(wr.shape, f32),
            shape((sums, 128), f32),
        ],
        scratch_shapes=scratch,
        compiler_params=pltpu.CompilerParams(
            dimension_semantics=("arbitrary",), vmem_limit_bytes=60 * 1024 * 1024
        ),
        name="layer",
    )(
        segment_ids,
        tokens,
        cotangent,
        segment_ids,
        padding_mask,
        wj,
        wo,
        we,
        wr,
        biases,
    )


def on_device(
    tokens,
    segment_ids,
    padding_mask,
    joint_weight,
    query_bias,
    value_bias,
    output_weight,
    output_bias,
    first_gain,
    first_shift,
    expand_weight,
    expand_bias,
    reduce_weight,
    reduce_bias,
    second_gain,
    second_shift,
    cotangent,
):
    axes = ("outer", "inner")
    vectors = (
        query_bias,
        value_bias,
        output_bias,
        first_gain,
        first_shift,
        reduce_bias,
        second_gain,
        second_shift,
    )
    shards = (joint_weight, output_weight, expand_weight, reduce_weight) + vectors + (expand_bias,)
    flat = jnp.concatenate([item.reshape(-1) for item in shards])
    gathered = lax.all_gather(flat, axes, axis=0, tiled=False)
    devices = gathered.shape[0]
    at = 0
    full = []
    for item in shards:
        piece = gathered[:, at : at + item.size]
        at += item.size
        full.append(piece.reshape((devices * item.shape[0],) + item.shape[1:]))
    width = tokens.shape[2]
    columns = jnp.stack(full[4:12] + [full[12][:width], full[12][width:]], axis=1)
    columns = jnp.pad(columns, ((0, 0), (0, 128 - columns.shape[1])))
    layer_out, tokens_grad, gj, go, ge, gr, gb = run_compute(
        tokens, segment_ids, padding_mask, cotangent, *full[:4], columns
    )
    sums = gb[:, 0]
    inner_width = full[2].shape[1]
    names = {}
    spot = 0
    for name, size in (
        ("second_gain", width),
        ("second_shift", width),
        ("reduce_bias", width),
        ("expand_bias", inner_width),
        ("first_gain", width),
        ("first_shift", width),
        ("output_bias", width),
        ("query_bias", width),
        ("value_bias", width),
    ):
        names[name] = sums[spot : spot + size]
        spot += size
    grads = (
        gj,
        names["query_bias"],
        names["value_bias"],
        go,
        names["output_bias"],
        names["first_gain"],
        names["first_shift"],
        ge,
        names["expand_bias"],
        gr,
        names["reduce_bias"],
        names["second_gain"],
        names["second_shift"],
    )
    packed = jnp.concatenate([item.reshape(devices, -1) for item in grads], axis=1)
    owned = lax.psum_scatter(packed, axes, scatter_dimension=0, tiled=True).reshape(-1)
    outs = []
    at = 0
    for item in grads:
        size = item.size // devices
        outs.append(owned[at : at + size].reshape((item.shape[0] // devices,) + item.shape[1:]))
        at += size
    return (layer_out, tokens_grad, *outs)


def solution(mesh):
    rows = P(("outer", "inner"))
    rows2 = P(("outer", "inner"), None)
    rows3 = P(("outer", "inner"), None, None)
    weights = (rows2, rows, rows, rows2, rows, rows, rows, rows2, rows, rows2, rows, rows, rows)
    return jax.shard_map(
        on_device,
        mesh=mesh,
        in_specs=(rows3, rows2, rows2) + weights + (rows3,),
        out_specs=(rows3, rows3) + weights,
        check_vma=False,
    )
```

```python
import functools
import math

import jax
import jax.numpy as jnp
from jax import lax
from jax.experimental import pallas as pl
from jax.experimental.pallas import tpu as pltpu
from jax.sharding import PartitionSpec as P

HEADS = 4
HEAD_DIM = 64
HALF = 512
CHUNK = 256

norm_epsilon = 1e-06
mask_step = -(2.0**100)
log2_e = math.log2(math.e)
gelu_a = math.sqrt(2.0 / math.pi)
gelu_b = 0.044715

f32 = jnp.float32
bf16 = jnp.bfloat16


def nn(left, right):
    return lax.dot_general(left, right, (((1,), (0,)), ((), ())), preferred_element_type=f32)


def nt(left, right):
    return lax.dot_general(left, right, (((1,), (1,)), ((), ())), preferred_element_type=f32)


def over_features(values):
    return jnp.sum(values, axis=0, keepdims=True)


def big_cell_start(seg_ref, seq, length):
    wanted = seg_ref[seq, HALF - 1]
    low = jnp.int32(0)
    step = HALF
    while step > 1:
        step //= 2
        probe = low + step
        low = jnp.where(seg_ref[seq, probe - 1] < wanted, probe, low)
    last = jnp.minimum(low + HALF - 1, length - 1)
    return jnp.where(seg_ref[seq, last] == wanted, low, HALF)


def compute_kernel(
    devices,
    seg_smem,
    tokens_ref,
    cot_ref,
    seg_ref,
    pad_ref,
    wj_ref,
    wo_ref,
    we_ref,
    wr_ref,
    bias_ref,
    out_ref,
    tg_ref,
    gj_ref,
    go_ref,
    ge_ref,
    gr_ref,
    gb_ref,
    wjt,
    wot,
    wet,
    wrt,
    bj,
    be,
    bcol,
    vrow,
    turn,
    xtok,
    xT,
    cT,
    jT,
    kaug,
    vaug,
    codeq,
    pT,
    inv,
    mixT,
    hat1,
    rinv1,
    act,
    slow,
    igr,
    flow,
    blow,
    fig,
    mgT,
    jgT,
    dgelu,
    accb,
):
    seq = pl.program_id(0)
    length, width = tokens_ref.shape[1], tokens_ref.shape[2]
    inner_width = we_ref.shape[1]
    scale = HEAD_DIM**-0.5

    @pl.when(seq == 0)
    def _():
        wide = wj_ref[...].astype(f32)
        for part in range(3):
            piece = wide[:, part * width : (part + 1) * width].T
            if part == 0:
                piece = piece * scale
            wjt[part * width : (part + 1) * width, :] = piece.astype(bf16)
        wot[...] = wo_ref[...].astype(f32).T.astype(bf16)
        wet[...] = we_ref[...].astype(f32).T.astype(bf16)
        wrt[...] = wr_ref[...].astype(f32).T.astype(bf16)
        columns = bias_ref[...]

        def spread(at):
            return jnp.broadcast_to(columns[:, at : at + 1], (width, 128))

        bj[0:width, :] = spread(0) * scale
        bj[width : 2 * width, :] = jnp.zeros((width, 128), f32)
        bj[2 * width : 3 * width, :] = spread(1)
        for at in range(6):
            bcol[at, :, :] = spread(2 + at)
        halves = [spread(8), spread(9)]
        share = width // devices
        be[...] = jnp.concatenate(
            [halves[k % 2][k // 2 * share : (k // 2 + 1) * share] for k in range(2 * devices)], axis=0
        )
        vrow[...] = columns.T[0:8, :]
        gj_ref[...] = jnp.zeros_like(gj_ref)
        go_ref[...] = jnp.zeros_like(go_ref)
        ge_ref[...] = jnp.zeros_like(ge_ref)
        gr_ref[...] = jnp.zeros_like(gr_ref)
        accb[...] = jnp.zeros_like(accb)

    start = big_cell_start(seg_smem, seq, length)

    def turned(ref, tile):
        lanes = slice(tile * 128, (tile + 1) * 128)
        whole = ref[0, :, lanes].astype(f32)
        turn[tile, 0:length, :] = whole
        turn[tile, length : length + HALF, :] = whole[0:HALF]

    def take(tile, rows):
        return turn[tile, pl.ds(start + rows, CHUNK), :]

    tiles = width // 128
    for tile in range(tiles):
        turned(tokens_ref, tile)
    for tile in range(tiles):
        for at in range(0, length, CHUNK):
            piece = take(tile, at)
            xtok[at : at + CHUNK, tile * 128 : (tile + 1) * 128] = piece.astype(bf16)
            xT[tile * 128 : (tile + 1) * 128, at : at + CHUNK] = piece.T.astype(bf16)
    for tile in range(tiles):
        turned(cot_ref, tile)
    for tile in range(tiles):
        for at in range(0, length, CHUNK):
            cT[tile * 128 : (tile + 1) * 128, at : at + CHUNK] = take(tile, at).T.astype(bf16)

    shift = length - start
    segs = jnp.broadcast_to(seg_ref[pl.ds(seq, 1), :].astype(f32), (8, length))
    pads = jnp.broadcast_to(pad_ref[pl.ds(seq, 1), :].astype(f32), (8, length))
    segs = pltpu.roll(segs, shift, 1)[0:1, :]
    pads = pltpu.roll(pads, shift, 1)[0:1, :]
    position = lax.broadcasted_iota(jnp.int32, (1, length), 1)
    digits = [(position // 64) % 8, (position // 8) % 8, position % 8]
    code = lax.broadcasted_iota(jnp.int32, (8, length), 0)
    hidden = (pads == 0.0).astype(f32)
    same = (segs == code.astype(f32)).astype(f32)
    parts_q = [1.0 - same]
    parts_k = [same * mask_step]
    for digit in digits:
        equal = (digit == code).astype(f32)
        parts_q.append(1.0 - equal)
        parts_k.append(equal * hidden * mask_step)
    nothing = jnp.zeros((32, length), f32)
    codeq[...] = jnp.concatenate(parts_q + [nothing], axis=0).astype(bf16)
    codek = jnp.concatenate(parts_k + [nothing] + parts_k + [nothing], axis=0).T

    lane = lax.broadcasted_iota(jnp.int32, (CHUNK, 128), 1)
    low_lanes = lane < HEAD_DIM

    for at in range(0, length, CHUNK):
        rows = slice(at, at + CHUNK)
        made = nn(wjt[...], xT[:, rows])
        for tile in range(CHUNK // 128):
            jT[:, at + tile * 128 : at + (tile + 1) * 128] = (
                made[:, tile * 128 : (tile + 1) * 128] + bj[...]
            ).astype(bf16)
        flat = nn(xtok[rows, :], wj_ref[:, width : 3 * width])
        codes = codek[rows, :]
        for head in range(HEADS):
            lanes = slice((head // 2) * 128, (head // 2 + 1) * 128)
            mine = low_lanes if head % 2 == 0 else ~low_lanes
            keys = flat[:, lanes]
            values = flat[:, width + lanes.start : width + lanes.stop] + vrow[1:2, lanes]
            kaug[head, rows, :] = jnp.where(mine, keys, codes).astype(bf16)
            vaug[head, rows, :] = jnp.where(mine, values, -1.0).astype(bf16)

    ones = jnp.ones((16, HALF), bf16)
    for head in range(HEADS):
        own = slice(head * HEAD_DIM, (head + 1) * HEAD_DIM)
        vrows = slice(2 * width + own.start, 2 * width + own.stop)
        for block in range(length // HALF):
            cols = slice(block * HALF, (block + 1) * HALF)
            place = head * (length // HALF) + block
            for at in range(0, HALF, CHUNK):
                here = slice(block * HALF + at, block * HALF + at + CHUNK)
                pair = [jT[own, here], codeq[:, here]]
                if head % 2 == 1:
                    pair = pair[::-1]
                scores = nn(kaug[head, cols, :], jnp.concatenate(pair, axis=0))
                for tile in range(0, CHUNK, 128):
                    mine = scores[:, tile : tile + 128]
                    highest = jnp.max(mine, axis=0, keepdims=True)
                    pT[place, :, at + tile : at + tile + 128] = jnp.exp2(
                        (mine - highest) * log2_e
                    ).astype(bf16)
            mixed = nn(jnp.concatenate([jT[vrows, cols], ones], axis=0), pT[place])
            inverse = 1.0 / mixed[HEAD_DIM : HEAD_DIM + 1, :]
            inv[head : head + 1, cols] = inverse
            mixT[own, cols] = (mixed[0:HEAD_DIM, :] * inverse).astype(bf16)

    def add_sums(row, values):
        accb[row : row + values.shape[0], :] += values

    def unit(hidden):
        centred = hidden - over_features(hidden) * (1.0 / width)
        inverse = lax.rsqrt(over_features(centred * centred) * (1.0 / width) + norm_epsilon)
        return centred * inverse, inverse

    def unit_back(inside, hat, inverse):
        return inverse * (
            inside
            - over_features(inside) * (1.0 / width)
            - hat * (over_features(inside * hat) * (1.0 / width))
        )

    halves = [slice(t, t + 128) for t in range(0, CHUNK, 128)]
    for at in range(0, length, CHUNK):
        rows = slice(at, at + CHUNK)
        branch = nn(wot[...], mixT[:, rows])
        firsts = []
        for half in halves:
            here = slice(at + half.start, at + half.stop)
            hat, inverse = unit(xT[:, here].astype(f32) + branch[:, half] + bcol[0])
            hat1[:, here] = hat
            rinv1[0:1, here] = inverse
            first = hat * bcol[1] + bcol[2]
            flow[:, here] = first.astype(bf16)
            firsts.append(first)
        inner = nn(wet[...], flow[:, rows])
        for half in halves:
            here = slice(at + half.start, at + half.stop)
            for r in range(0, inner_width, 64):
                u = inner[r : r + 64, half] + be[r : r + 64, :]
                square = u * u
                t = jnp.tanh(u * (gelu_a + (gelu_a * gelu_b) * square))
                h = 0.5 + 0.5 * t
                value = u * h
                act[r : r + 64, here] = value.astype(bf16)
                dgelu[r : r + 64, half] = h + value * (1.0 - h) * (
                    2.0 * gelu_a + (6.0 * gelu_a * gelu_b) * square
                )
        second = nn(wrt[...], act[:, rows])
        grads = []
        for k, half in enumerate(halves):
            here = slice(at + half.start, at + half.stop)
            hat, inverse = unit(firsts[k] + second[:, half] + bcol[3])
            result = (hat * bcol[4] + bcol[5]).T
            for tile in range(tiles):
                piece = result[:, tile * 128 : (tile + 1) * 128]
                turn[tile, HALF + here.start : HALF + here.stop, :] = piece
                if here.start >= HALF:
                    turn[tile, here.start - HALF : here.stop - HALF, :] = piece
            upstream = cT[:, here].astype(f32)
            add_sums(0, upstream * hat)
            add_sums(width, upstream)
            back = unit_back(upstream * bcol[4], hat, inverse)
            low = back.astype(bf16)
            slow[:, here] = low
            add_sums(2 * width, low.astype(f32))
            grads.append(back)
        active_grad = nn(wr_ref[...], slow[:, rows])
        for half in halves:
            here = slice(at + half.start, at + half.stop)
            for r in range(0, inner_width, 64):
                low = (active_grad[r : r + 64, half] * dgelu[r : r + 64, half]).astype(bf16)
                igr[r : r + 64, here] = low
                add_sums(3 * width + r, low.astype(f32))
        deeper = nn(we_ref[...], igr[:, rows])
        for k, half in enumerate(halves):
            here = slice(at + half.start, at + half.stop)
            first_grad = grads[k] + deeper[:, half]
            hat = hat1[:, here]
            base = 3 * width + inner_width
            add_sums(base, first_grad * hat)
            add_sums(base + width, first_grad)
            back = unit_back(first_grad * bcol[1], hat, rinv1[0:1, here])
            fig[:, here] = back
            low = back.astype(bf16)
            blow[:, here] = low
            add_sums(base + 2 * width, low.astype(f32))
        mgT[:, rows] = nn(wo_ref[...], blow[:, rows])

    def untake(tile, at):
        return turn[tile, pl.ds(HALF - start + at, CHUNK), :]

    for tile in range(tiles):
        for at in range(0, length, CHUNK):
            out_ref[0, at : at + CHUNK, tile * 128 : (tile + 1) * 128] = untake(tile, at).astype(
                bf16
            )

    gr_ref[...] += nt(act[...], slow[...])
    ge_ref[...] += nt(flow[...], igr[...])
    go_ref[...] += nt(mixT[...], blow[...])

    for head in range(HEADS):
        own = slice(head * HEAD_DIM, (head + 1) * HEAD_DIM)
        for block in range(length // HALF):
            cols = slice(block * HALF, (block + 1) * HALF)
            place = head * (length // HALF) + block
            grown = mgT[own, cols].astype(bf16).astype(f32)
            inverse = inv[head : head + 1, cols]
            grown = grown * inverse
            dots = over_features(grown * mixT[own, cols].astype(f32))
            high = dots.astype(bf16).astype(f32)
            row = lax.broadcasted_iota(jnp.int32, (16, HALF), 0)
            extra = jnp.where(row == 0, high, jnp.where(row == 1, dots - high, 0.0))
            extra = jnp.concatenate([extra, jnp.zeros((HEAD_DIM - 16, HALF), f32)], axis=0)
            grown = grown.astype(bf16)
            pair = [grown, extra.astype(bf16)]
            if head % 2 == 1:
                pair = pair[::-1]
            upstream = jnp.concatenate(pair, axis=0)
            dsT = (
                pT[place].astype(f32) * nn(vaug[head, cols, :], upstream)
            ).astype(bf16)
            jgT[2 * width + own.start : 2 * width + own.stop, cols] = nt(grown, pT[place]).astype(
                bf16
            )
            keysT = jT[width + own.start : width + own.stop, cols]
            jgT[own, cols] = (nn(keysT, dsT) * scale).astype(bf16)
            jgT[width + own.start : width + own.stop, cols] = nt(jT[own, cols], dsT).astype(bf16)

    gj_ref[...] += nt(xT[...], jgT[...])
    base = 6 * width + inner_width
    for at in range(0, length, 128):
        here = slice(at, at + 128)
        add_sums(base, jgT[0:width, here].astype(f32))
        add_sums(base + width, jgT[2 * width : 3 * width, here].astype(f32))
    for at in range(0, length, CHUNK):
        rows = slice(at, at + CHUNK)
        result = (nn(wj_ref[...], jgT[:, rows]) + fig[:, rows]).T
        for tile in range(tiles):
            piece = result[:, tile * 128 : (tile + 1) * 128]
            turn[tile, HALF + at : HALF + at + CHUNK, :] = piece
            if at >= HALF:
                turn[tile, at - HALF : at - HALF + CHUNK, :] = piece
    for tile in range(tiles):
        for at in range(0, length, CHUNK):
            tg_ref[0, at : at + CHUNK, tile * 128 : (tile + 1) * 128] = untake(tile, at)

    @pl.when(seq == pl.num_programs(0) - 1)
    def _():
        sums = jnp.sum(accb[...], axis=1, keepdims=True)
        wide = jnp.broadcast_to(sums[3 * width : 3 * width + inner_width], (inner_width, 128))
        share = width // devices
        hidden_sums = [
            jnp.concatenate(
                [wide[k * share : (k + 1) * share] for k in range(first, 2 * devices, 2)], axis=0
            )
            for first in range(2)
        ]
        later = 3 * width + inner_width
        places = [later + 3 * width, later + 4 * width, later + 2 * width, later, later + width]
        places += [2 * width, 0, width]
        lanes = lax.broadcasted_iota(jnp.int32, (width, 128), 1)
        columns = jnp.zeros((width, 128), f32)
        for at, place in enumerate(places):
            columns = jnp.where(lanes == at, sums[place : place + width], columns)
        for at, item in enumerate(hidden_sums):
            columns = jnp.where(lanes == len(places) + at, item, columns)
        gb_ref[...] = columns


def run_compute(
    tokens, segment_ids, padding_mask, cotangent, wj, wo, we, wr, biases, devices
):
    count, length, width = tokens.shape
    inner_width = we.shape[1]
    sums = 8 * width + inner_width
    vmem = pl.BlockSpec(memory_space=pltpu.VMEM)

    def whole(shape):
        return pl.BlockSpec(shape, lambda i: (0,) * len(shape))

    per_seq = pl.BlockSpec((1, length, width), lambda i: (i, 0, 0))
    blocks = HEADS * (length // HALF)
    scratch = [
        pltpu.VMEM((3 * width, width), bf16),
        pltpu.VMEM((width, width), bf16),
        pltpu.VMEM((inner_width, width), bf16),
        pltpu.VMEM((width, inner_width), bf16),
        pltpu.VMEM((3 * width, 128), f32),
        pltpu.VMEM((inner_width, 128), f32),
        pltpu.VMEM((6, width, 128), f32),
        pltpu.VMEM((8, width), f32),
        pltpu.VMEM((width // 128, length + HALF, 128), f32),
        pltpu.VMEM((length, width), bf16),
        pltpu.VMEM((width, length), bf16),
        pltpu.VMEM((width, length), bf16),
        pltpu.VMEM((3 * width, length), bf16),
        pltpu.VMEM((HEADS, length, 128), bf16),
        pltpu.VMEM((HEADS, length, 128), bf16),
        pltpu.VMEM((HEAD_DIM, length), bf16),
        pltpu.VMEM((blocks, HALF, HALF), bf16),
        pltpu.VMEM((8, length), f32),
        pltpu.VMEM((width, length), bf16),
        pltpu.VMEM((width, length), f32),
        pltpu.VMEM((8, length), f32),
        pltpu.VMEM((inner_width, length), bf16),
        pltpu.VMEM((width, length), bf16),
        pltpu.VMEM((inner_width, length), bf16),
        pltpu.VMEM((width, length), bf16),
        pltpu.VMEM((width, length), bf16),
        pltpu.VMEM((width, length), f32),
        pltpu.VMEM((width, length), f32),
        pltpu.VMEM((3 * width, length), bf16),
        pltpu.VMEM((inner_width, CHUNK), f32),
        pltpu.VMEM((sums, 128), f32),
    ]
    shape = jax.ShapeDtypeStruct
    return pl.pallas_call(
        functools.partial(compute_kernel, devices),
        grid=(count,),
        in_specs=[
            pl.BlockSpec(memory_space=pltpu.SMEM),
            per_seq,
            per_seq,
            whole(segment_ids.shape),
            whole(padding_mask.shape),
            whole(wj.shape),
            whole(wo.shape),
            whole(we.shape),
            whole(wr.shape),
            whole(biases.shape),
        ],
        out_specs=[
            per_seq,
            per_seq,
            whole(wj.shape),
            whole(wo.shape),
            whole(we.shape),
            whole(wr.shape),
            whole(biases.shape),
        ],
        out_shape=[
            shape(tokens.shape, bf16),
            shape(tokens.shape, f32),
            shape(wj.shape, f32),
            shape(wo.shape, f32),
            shape(we.shape, f32),
            shape(wr.shape, f32),
            shape(biases.shape, f32),
        ],
        scratch_shapes=scratch,
        compiler_params=pltpu.CompilerParams(
            dimension_semantics=("arbitrary",), vmem_limit_bytes=60 * 1024 * 1024
        ),
        name="layer",
    )(
        segment_ids,
        tokens,
        cotangent,
        segment_ids,
        padding_mask,
        wj,
        wo,
        we,
        wr,
        biases,
    )


MESH = pl.DeviceIdType.MESH
VECTORS = 8


def copy_to(source, target, send, receive, outer, inner):
    return pltpu.make_async_remote_copy(
        src_ref=source,
        dst_ref=target,
        send_sem=send,
        recv_sem=receive,
        device_id=(outer, inner),
        device_id_type=MESH,
    )


def rounded_up(amount, to):
    return (amount + to - 1) // to * to


class Peers:
    def __init__(self, outers, inners):
        self.outers, self.inners = outers, inners
        self.outer = lax.axis_index("outer")
        self.inner = lax.axis_index("inner")
        self.core = lax.rem(self.outer, 2)
        self.chip = lax.div(self.outer, 2)
        self.chips = outers // 2

    def along_inner(self):
        for step in range(1, self.inners):
            yield lax.rem(self.inner + step, self.inners)

    def along_chips(self):
        for step in range(1, self.chips):
            yield lax.rem(self.chip + step, self.chips)

    def greet(self):
        barrier = pltpu.get_barrier_semaphore()
        others = [(self.outer, at) for at in self.along_inner()]
        others += [(at * 2 + self.core, self.inner) for at in self.along_chips()]
        others += [(self.chip * 2 + 1 - self.core, self.inner)]
        for other in others:
            pl.semaphore_signal(barrier, inc=1, device_id=other, device_id_type=MESH)
        pl.semaphore_wait(barrier, len(others))


def gather(peers, held, send, receive):
    mine = held.at[peers.core, peers.chip, peers.inner]
    sent = []

    def pass_on(slot, semaphores, outer, inner):
        core, chip, at = slot
        copy = copy_to(
            held.at[core, chip, at],
            held.at[core, chip, at],
            semaphores,
            receive.at[core, chip, at],
            outer,
            inner,
        )
        copy.start()
        sent.append(copy)

    def arrived(core, chip, at):
        block = held.at[core, chip, at]
        copy_to(
            block, block, send.at[0], receive.at[core, chip, at], peers.outer, peers.inner
        ).wait_recv()

    core, chip, inner = peers.core, peers.chip, peers.inner
    mate = chip * 2 + 1 - core
    counter = iter(range(10000))
    for at in peers.along_inner():
        pass_on((core, chip, inner), send.at[next(counter)], peers.outer, at)
    order = [inner] + list(peers.along_inner())
    for k, at in enumerate(order):
        if k > 0:
            arrived(core, chip, at)
        for other in peers.along_chips():
            pass_on((core, chip, at), send.at[next(counter)], other * 2 + core, inner)
        pass_on((core, chip, at), send.at[next(counter)], mate, inner)
    for at in order:
        for other in peers.along_chips():
            arrived(core, other, at)
            pass_on((core, other, at), send.at[next(counter)], mate, inner)
    for at in order:
        for other in [chip] + list(peers.along_chips()):
            arrived(1 - core, other, at)
    for copy in sent:
        copy.wait_send()


def gather_sends(outers, inners):
    chips = outers // 2
    return (inners - 1) + inners * (chips - 1) + inners * chips


def column_blocks(values):
    return [values[:, at : at + 128] for at in range(0, values.shape[1], 128)]


def padded_rows(pieces, rows):
    have = sum(piece.shape[0] for piece in pieces)
    if rows > have:
        pieces = pieces + [jnp.zeros((rows - have, 128), f32)]
    return jnp.concatenate(pieces, axis=0)


def gather_kernel(outers, inners, shapes, *refs):
    (wj, wo, we, wr), refs = refs[:4], refs[4:]
    vectors, refs = refs[: VECTORS + 1], refs[VECTORS + 1 :]
    (wj_out, wo_out, we_out, wr_out, cols_out), refs = refs[:5], refs[5:]
    held, send, receive = refs
    peers = Peers(outers, inners)
    rows = wj.shape[0]
    lines = [ref[...].astype(f32).reshape(1, ref.shape[0]) for ref in vectors]
    lines = lines[:-1] + [lines[-1][:, :rows], lines[-1][:, rows:]]
    lines.append(jnp.zeros((128 - len(lines), rows), f32))
    columns = jnp.concatenate(lines, axis=0).T
    pieces = [columns]
    for ref in (wj, wo, we, wr):
        pieces += column_blocks(ref[...].astype(f32))
    held[peers.core, peers.chip, peers.inner] = padded_rows(pieces, held.shape[3]).astype(bf16)
    peers.greet()
    gather(peers, held, send, receive)
    at = 0
    for ref, source in ((cols_out, None), (wj_out, wj), (wo_out, wo), (we_out, we), (wr_out, wr)):
        depth = rows if source is None else source.shape[0]
        for column in range(0, ref.shape[1], 128):
            stack = []
            for device in range(outers * inners):
                outer, inner = device // inners, device % inners
                block = held[outer % 2, outer // 2, inner].astype(f32)
                stack.append(block[at : at + depth])
            ref[:, column : column + 128] = jnp.concatenate(stack, axis=0).astype(ref.dtype)
            at += depth


def run_gather(outers, inners, shards):
    devices = outers * inners
    rows = shards[0].shape[0]
    total = rows + sum(item.size // 128 for item in shards[:4])
    total = rounded_up(total, 16)
    vmem = pl.BlockSpec(memory_space=pltpu.VMEM)
    shape = jax.ShapeDtypeStruct
    outs = [shape((item.shape[0] * devices, item.shape[1]), bf16) for item in shards[:4]]
    outs.append(shape((rows * devices, 128), f32))
    return pl.pallas_call(
        functools.partial(gather_kernel, outers, inners, None),
        in_specs=[vmem] * len(shards),
        out_specs=[vmem] * len(outs),
        out_shape=outs,
        scratch_shapes=[
            pltpu.VMEM((2, outers // 2, inners, total, 128), bf16),
            pltpu.SemaphoreType.DMA((gather_sends(outers, inners),)),
            pltpu.SemaphoreType.DMA((2, outers // 2, inners)),
        ],
        compiler_params=pltpu.CompilerParams(
            collective_id=0, has_side_effects=True, vmem_limit_bytes=40 * 1024 * 1024
        ),
        name="gather_weights",
    )(*shards)


def reduce_kernel(outers, inners, cols, gj, go, ge, gr, fin, *scratch):
    packed, from_mate, mid, from_chips, last, from_inner, send, receive = scratch
    peers = Peers(outers, inners)
    devices = outers * inners
    core, chip, inner = peers.core, peers.chip, peers.inner
    peers.greet()
    for device in range(devices):
        outer = device // inners
        pieces = []
        for ref in (cols, gj, go, ge, gr):
            depth = ref.shape[0] // devices
            pieces += column_blocks(ref[device * depth : (device + 1) * depth, :])
        packed[outer % 2, outer // 2, device % inners] = padded_rows(pieces, packed.shape[3])
    mate = chip * 2 + 1 - core
    first = copy_to(packed.at[1 - core], from_mate, send.at[0], receive.at[0], mate, inner)
    first.start()
    first.wait()
    chips = peers.chips
    copies = []
    for k, other in enumerate(peers.along_chips()):
        for at in range(inners):
            mid[other, at] = (packed[core, other, at] + from_mate[other, at]).astype(bf16)
        copy = copy_to(
            mid.at[other],
            from_chips.at[k],
            send.at[1 + k],
            receive.at[1 + k],
            other * 2 + core,
            inner,
        )
        copy.start()
        copies.append(copy)
    for copy in copies:
        copy.wait()
    copies = []
    for k, at in enumerate(peers.along_inner()):
        total = packed[core, chip, at] + from_mate[chip, at]
        for other in range(chips - 1):
            total += from_chips[other, at].astype(f32)
        last[at] = total.astype(bf16)
        copy = copy_to(
            last.at[at],
            from_inner.at[k],
            send.at[chips + k],
            receive.at[chips + k],
            peers.outer,
            at,
        )
        copy.start()
        copies.append(copy)
    total = packed[core, chip, inner] + from_mate[chip, inner]
    for other in range(chips - 1):
        total += from_chips[other, inner].astype(f32)
    for k, copy in enumerate(copies):
        copy.wait()
        total += from_inner[k].astype(f32)
    fin[...] = total


def run_reduce(outers, inners, grads):
    devices = outers * inners
    rows = rounded_up(sum(item.size // 128 // devices for item in grads), 16)
    chips = outers // 2
    vmem = pl.BlockSpec(memory_space=pltpu.VMEM)
    return pl.pallas_call(
        functools.partial(reduce_kernel, outers, inners),
        in_specs=[vmem] * 5,
        out_specs=vmem,
        out_shape=jax.ShapeDtypeStruct((rows, 128), f32),
        scratch_shapes=[
            pltpu.VMEM((2, chips, inners, rows, 128), f32),
            pltpu.VMEM((chips, inners, rows, 128), f32),
            pltpu.VMEM((chips, inners, rows, 128), bf16),
            pltpu.VMEM((max(chips - 1, 1), inners, rows, 128), bf16),
            pltpu.VMEM((inners, rows, 128), bf16),
            pltpu.VMEM((inners - 1, rows, 128), bf16),
            pltpu.SemaphoreType.DMA((chips + inners,)),
            pltpu.SemaphoreType.DMA((chips + inners,)),
        ],
        compiler_params=pltpu.CompilerParams(
            collective_id=1, has_side_effects=True, vmem_limit_bytes=40 * 1024 * 1024
        ),
        name="reduce_gradients",
    )(*grads)


def hand_out_kernel(fin, *outs):
    matrices, vectors = outs[:4], outs[4:]
    rows = vectors[0].shape[0]
    lines = fin[0:rows, :].T
    for at, ref in enumerate(vectors[:-1]):
        ref[...] = lines[at, :]
    vectors[-1][...] = jnp.concatenate([lines[VECTORS, :], lines[VECTORS + 1, :]])
    at = rows
    for ref in matrices:
        depth = ref.shape[0]
        for column in range(0, ref.shape[1], 128):
            ref[:, column : column + 128] = fin[at : at + depth, :]
            at += depth


def hand_out(fin, shards):
    vmem = pl.BlockSpec(memory_space=pltpu.VMEM)
    return pl.pallas_call(
        hand_out_kernel,
        in_specs=[vmem],
        out_specs=[vmem] * len(shards),
        out_shape=[jax.ShapeDtypeStruct(item.shape, f32) for item in shards],
        name="hand_out",
    )(fin)


def on_device(
    outers,
    inners,
    tokens,
    segment_ids,
    padding_mask,
    joint_weight,
    query_bias,
    value_bias,
    output_weight,
    output_bias,
    first_gain,
    first_shift,
    expand_weight,
    expand_bias,
    reduce_weight,
    reduce_bias,
    second_gain,
    second_shift,
    cotangent,
):
    shards = (
        joint_weight,
        output_weight,
        expand_weight,
        reduce_weight,
        query_bias,
        value_bias,
        output_bias,
        first_gain,
        first_shift,
        reduce_bias,
        second_gain,
        second_shift,
        expand_bias,
    )
    wj, wo, we, wr, columns = run_gather(outers, inners, shards)
    layer_out, tokens_grad, *grads = run_compute(
        tokens, segment_ids, padding_mask, cotangent, wj, wo, we, wr, columns, outers * inners
    )
    owned = hand_out(run_reduce(outers, inners, (grads[4], *grads[:4])), shards)
    gj, go, ge, gr, query, value, out, gain1, shift1, reduce, gain2, shift2, expand = owned
    return (
        layer_out,
        tokens_grad,
        gj,
        query,
        value,
        go,
        out,
        gain1,
        shift1,
        ge,
        expand,
        gr,
        reduce,
        gain2,
        shift2,
    )


def solution(mesh):
    rows = P(("outer", "inner"))
    rows2 = P(("outer", "inner"), None)
    rows3 = P(("outer", "inner"), None, None)
    weights = (rows2, rows, rows, rows2, rows, rows, rows, rows2, rows, rows2, rows, rows, rows)
    return jax.shard_map(
        functools.partial(on_device, mesh.shape["outer"], mesh.shape["inner"]),
        mesh=mesh,
        in_specs=(rows3, rows2, rows2) + weights + (rows3,),
        out_specs=(rows3, rows3) + weights,
        check_vma=False,
    )
```

```python
import functools
import math

import jax
import jax.numpy as jnp
from jax import lax
from jax.experimental import pallas as pl
from jax.experimental.pallas import tpu as pltpu
from jax.sharding import PartitionSpec as P

HEADS = 4
HEAD_DIM = 64
HALF = 512
CHUNK = 256
VECTORS = 8
MESH = pl.DeviceIdType.MESH

norm_epsilon = 1e-06
mask_step = -(2.0**100)
log2_e = math.log2(math.e)
gelu_a = math.sqrt(2.0 / math.pi)
gelu_b = 0.044715

f32 = jnp.float32
bf16 = jnp.bfloat16


def nn(left, right):
    return lax.dot_general(left, right, (((1,), (0,)), ((), ())), preferred_element_type=f32)


def nt(left, right):
    return lax.dot_general(left, right, (((1,), (1,)), ((), ())), preferred_element_type=f32)


def over_features(values):
    return jnp.sum(values, axis=0, keepdims=True)


def column_blocks(values):
    return [values[:, at : at + 128] for at in range(0, values.shape[1], 128)]


def padded_rows(pieces, rows):
    have = sum(piece.shape[0] for piece in pieces)
    if rows > have:
        pieces = pieces + [jnp.zeros((rows - have, 128), f32)]
    return jnp.concatenate(pieces, axis=0)


def rounded_up(amount, to):
    return (amount + to - 1) // to * to


def big_cell_start(seg_ref, seq, length):
    wanted = seg_ref[seq, HALF - 1]
    low = jnp.int32(0)
    step = HALF
    while step > 1:
        step //= 2
        probe = low + step
        low = jnp.where(seg_ref[seq, probe - 1] < wanted, probe, low)
    last = jnp.minimum(low + HALF - 1, length - 1)
    return jnp.where(seg_ref[seq, last] == wanted, low, HALF)


def copy_to(source, target, send, receive, outer, inner):
    return pltpu.make_async_remote_copy(
        src_ref=source,
        dst_ref=target,
        send_sem=send,
        recv_sem=receive,
        device_id=(outer, inner),
        device_id_type=MESH,
    )


class Peers:
    def __init__(self, outers, inners):
        self.outers, self.inners = outers, inners
        self.outer = lax.axis_index("outer")
        self.inner = lax.axis_index("inner")
        self.core = lax.rem(self.outer, 2)
        self.chip = lax.div(self.outer, 2)
        self.chips = outers // 2
        self.mate = self.chip * 2 + 1 - self.core

    def along_inner(self):
        return [lax.rem(self.inner + step, self.inners) for step in range(1, self.inners)]

    def along_chips(self):
        return [lax.rem(self.chip + step, self.chips) for step in range(1, self.chips)]

    def greet(self):
        barrier = pltpu.get_barrier_semaphore()
        others = [(self.outer, at) for at in self.along_inner()]
        others += [(at * 2 + self.core, self.inner) for at in self.along_chips()]
        others += [(self.mate, self.inner)]
        for other in others:
            pl.semaphore_signal(barrier, inc=1, device_id=other, device_id_type=MESH)
        pl.semaphore_wait(barrier, len(others))


class Gather:
    def __init__(self, peers, held, send, receive):
        self.peers, self.held, self.send, self.receive = peers, held, send, receive
        self.sent = []

    def pass_on(self, core, chip, at, outer, inner):
        block = self.held.at[core, chip, at]
        copy = copy_to(
            block,
            block,
            self.send.at[len(self.sent)],
            self.receive.at[core, chip, at],
            outer,
            inner,
        )
        copy.start()
        self.sent.append(copy)

    def arrived(self, core, chip, at):
        block = self.held.at[core, chip, at]
        peers = self.peers
        copy_to(
            block,
            block,
            self.send.at[0],
            self.receive.at[core, chip, at],
            peers.outer,
            peers.inner,
        ).wait_recv()

    def spread(self, at):
        peers = self.peers
        for other in peers.along_chips():
            self.pass_on(peers.core, peers.chip, at, other * 2 + peers.core, peers.inner)
        self.pass_on(peers.core, peers.chip, at, peers.mate, peers.inner)

    def first(self):
        peers = self.peers
        for at in peers.along_inner():
            self.pass_on(peers.core, peers.chip, peers.inner, peers.outer, at)
        self.spread(peers.inner)

    def second(self):
        peers = self.peers
        for at in peers.along_inner():
            self.arrived(peers.core, peers.chip, at)
            self.spread(at)

    def third(self):
        peers = self.peers
        for at in [peers.inner] + peers.along_inner():
            for other in peers.along_chips():
                self.arrived(peers.core, other, at)
                self.pass_on(peers.core, other, at, peers.mate, peers.inner)

    def finish(self):
        peers = self.peers
        for at in [peers.inner] + peers.along_inner():
            for other in [peers.chip] + peers.along_chips():
                self.arrived(1 - peers.core, other, at)
        for copy in self.sent:
            copy.wait_send()


def gather_sends(outers, inners):
    chips = outers // 2
    return (inners - 1) + inners * (chips - 1) + inners * chips


class Reduce:
    def __init__(self, peers, packed, from_mate, mid, from_chips, last, from_inner, send, receive):
        self.peers, self.packed, self.from_mate = peers, packed, from_mate
        self.mid, self.from_chips, self.last = mid, from_chips, last
        self.from_inner, self.send, self.receive = from_inner, send, receive

    def to_mate(self):
        peers = self.peers
        return copy_to(
            self.packed.at[1 - peers.core],
            self.from_mate,
            self.send.at[0],
            self.receive.at[0],
            peers.mate,
            peers.inner,
        )

    def to_chips(self):
        peers = self.peers
        return [
            copy_to(
                self.mid.at[k],
                self.from_chips.at[k],
                self.send.at[1 + k],
                self.receive.at[1 + k],
                other * 2 + peers.core,
                peers.inner,
            )
            for k, other in enumerate(peers.along_chips())
        ]

    def to_inner(self):
        peers = self.peers
        return [
            copy_to(
                self.last.at[k],
                self.from_inner.at[k],
                self.send.at[peers.chips + k],
                self.receive.at[peers.chips + k],
                peers.outer,
                at,
            )
            for k, at in enumerate(peers.along_inner())
        ]

    def first(self):
        self.to_mate().start()

    def second(self):
        peers = self.peers
        self.to_mate().wait()
        for k, (other, copy) in enumerate(zip(peers.along_chips(), self.to_chips())):
            for at in range(peers.inners):
                total = self.packed[peers.core, other, at] + self.from_mate[other, at]
                self.mid[k, at] = total.astype(bf16)
            copy.start()

    def own(self, at):
        peers = self.peers
        total = self.packed[peers.core, peers.chip, at] + self.from_mate[peers.chip, at]
        for k in range(peers.chips - 1):
            total += self.from_chips[k, at].astype(f32)
        return total

    def third(self):
        for copy in self.to_chips():
            copy.wait()
        for k, (at, copy) in enumerate(zip(self.peers.along_inner(), self.to_inner())):
            self.last[k] = self.own(at).astype(bf16)
            copy.start()

    def finish(self):
        total = self.own(self.peers.inner)
        for k, copy in enumerate(self.to_inner()):
            copy.wait()
            total += self.from_inner[k].astype(f32)
        return total


def reduce_scratch(outers, inners, rows):
    chips = outers // 2
    return [
        pltpu.VMEM((2, chips, inners, rows, 128), f32),
        pltpu.VMEM((chips, inners, rows, 128), f32),
        pltpu.VMEM((max(chips - 1, 1), inners, rows, 128), bf16),
        pltpu.VMEM((max(chips - 1, 1), inners, rows, 128), bf16),
        pltpu.VMEM((inners - 1, rows, 128), bf16),
        pltpu.VMEM((inners - 1, rows, 128), bf16),
        pltpu.SemaphoreType.DMA((chips + inners,)),
        pltpu.SemaphoreType.DMA((chips + inners,)),
    ]


REDUCE_SCRATCH = 8


def unit(hidden, width):
    centred = hidden - over_features(hidden) * (1.0 / width)
    inverse = lax.rsqrt(over_features(centred * centred) * (1.0 / width) + norm_epsilon)
    return centred * inverse, inverse


def unit_back(inside, hat, inverse, width):
    return inverse * (
        inside
        - over_features(inside) * (1.0 / width)
        - hat * (over_features(inside * hat) * (1.0 / width))
    )


def layer_kernel(outers, inners, *refs):
    refs = list(refs)

    def grab(amount):
        taken = refs[:amount]
        del refs[:amount]
        return taken

    seg_smem, tokens_hbm, cot_hbm, seg_hbm, pad_hbm = grab(5)
    shard_hbm = grab(4 + VECTORS + 1)
    out_hbm, tg_hbm, fin_a, fin_b = grab(4)
    shards = grab(4 + VECTORS + 1)
    land_x, land_c, segv, padv = grab(4)
    wj, wo, we, wr, wjt, wot, wet, wrt, bj, be, bcol, vrow = grab(12)
    turn, xtok, xT, cT, codek, codeq = grab(6)
    qkT, vT, qtok, kaug, vtok, pT, inv, mixT = grab(8)
    hat1, rinv1, act, slow, igr, flow, blow, dgelu = grab(8)
    fig, dots = grab(2)
    doT, dotok = cT, xtok
    gj, go, ge, gr, accb, accv = grab(6)
    held_a, send_a, receive_a, held_b, send_b, receive_b = grab(6)
    reduce_a, reduce_b = grab(REDUCE_SCRATCH), grab(REDUCE_SCRATCH)
    shard_sem, land_sem, out_sem, tg_sem = grab(4)

    count, length, width = tokens_hbm.shape
    inner_width = we.shape[1]
    devices = outers * inners
    share = width // devices
    scale = HEAD_DIM**-0.5
    tiles = width // 128
    blocks = length // HALF
    peers = Peers(outers, inners)

    def land(seq):
        slot = seq % 2
        return [
            pltpu.make_async_copy(tokens_hbm.at[seq], land_x.at[slot], land_sem.at[0, slot]),
            pltpu.make_async_copy(cot_hbm.at[seq], land_c.at[slot], land_sem.at[1, slot]),
        ]

    small = [
        pltpu.make_async_copy(source, target, shard_sem.at[k])
        for k, (source, target) in enumerate(
            zip(shard_hbm + [seg_hbm, pad_hbm], shards + [segv, padv])
        )
    ]
    for copy in small:
        copy.start()
    for seq in range(min(2, count)):
        for copy in land(seq):
            copy.start()
    for copy in small:
        copy.wait()

    lines = [ref[...].astype(f32).reshape(1, ref.shape[0]) for ref in shards[4:]]
    lines = lines[:-1] + [lines[-1][:, :share], lines[-1][:, share:]]
    lines.append(jnp.zeros((128 - len(lines), share), f32))
    pieces = [jnp.concatenate(lines, axis=0).T] + column_blocks(shards[0][...].astype(f32))
    here = (peers.core, peers.chip, peers.inner)
    held_a[here] = padded_rows(pieces, held_a.shape[3]).astype(bf16)
    pieces = []
    for ref in shards[1:4]:
        pieces += column_blocks(ref[...].astype(f32))
    held_b[here] = padded_rows(pieces, held_b.shape[3]).astype(bf16)
    peers.greet()
    gather_a = Gather(peers, held_a, send_a, receive_a)
    gather_b = Gather(peers, held_b, send_b, receive_b)
    gather_a.first()
    gather_b.first()

    identity = (
        lax.broadcasted_iota(jnp.int32, (CHUNK, CHUNK), 0)
        == lax.broadcasted_iota(jnp.int32, (CHUNK, CHUNK), 1)
    )
    identity = identity.astype(f32).astype(bf16)

    def prepare(seq):
        for copy in land(seq):
            copy.wait()
        start = big_cell_start(seg_smem, seq, length)
        slot = seq % 2

        def turned(tile, whole):
            turn[tile, 0:length, :] = whole
            turn[tile, length : length + HALF, :] = whole[0:HALF]

        def take(tile, at):
            return turn[tile, pl.ds(start + at, CHUNK), :]

        for source, target in ((land_x, xT), (land_c, cT)):
            for tile in range(tiles):
                turned(tile, source[slot, :, tile * 128 : (tile + 1) * 128].astype(f32))
            for at in range(0, length, CHUNK):
                piece = jnp.concatenate([take(tile, at) for tile in range(tiles)], axis=1)
                piece = piece.astype(bf16)
                if target is xT:
                    xtok[seq, at : at + CHUNK, :] = piece
                target[seq, :, at : at + CHUNK] = nt(identity, piece).astype(bf16)
        if seq + 2 < count:
            for copy in land(seq + 2):
                copy.start()

        position = lax.broadcasted_iota(jnp.int32, (1, length), 1)
        code = lax.broadcasted_iota(jnp.int32, (8, length), 0)
        hidden = (padv[seq : seq + 1, :] != 1).astype(f32)
        same = (segv[seq : seq + 1, :] == code).astype(f32)
        parts_q = [1.0 - same]
        parts_k = [same * mask_step]
        for digit in ((position // 64) % 8, (position // 8) % 8, position % 8):
            equal = (digit == code).astype(f32)
            parts_q.append(1.0 - equal)
            parts_k.append(equal * hidden * mask_step)
        both = jnp.concatenate(parts_k + parts_q + parts_k + parts_q, axis=0).astype(bf16)
        for at in range(0, length, CHUNK):
            flat = nt(identity, both[:, at : at + CHUNK])
            turn[2, at : at + CHUNK, :] = flat
            if at < HALF:
                turn[2, length + at : length + at + CHUNK, :] = flat
        nothing = jnp.zeros((32, CHUNK), f32)
        for at in range(0, length, CHUNK):
            piece = take(2, at).astype(bf16)
            codek[seq, at : at + CHUNK, :] = piece
            across = nt(identity[0:128, 0:128], piece)
            codeq[seq, :, at : at + CHUNK] = jnp.concatenate(
                [across[32:64], nothing], axis=0
            ).astype(bf16)

    steps = [
        [gather_a.second],
        [gather_a.third, gather_b.second],
        [gather_b.third],
    ]
    for seq in range(count):
        prepare(seq)
        if seq < len(steps):
            for step in steps[seq]:
                step()
    for step in sum(steps[count:], []):
        step()
    gather_a.finish()
    gather_b.finish()

    def stacked(held, at, depth):
        stack = []
        for device in range(devices):
            outer, inner = device // inners, device % inners
            stack.append(held[outer % 2, outer // 2, inner].astype(f32)[at : at + depth])
        return jnp.concatenate(stack, axis=0)

    columns = stacked(held_a, 0, share)
    for held, at, matrices in (
        (held_a, share, ((wj, wjt, shards[0]),)),
        (held_b, 0, ((wo, wot, shards[1]), (we, wet, shards[2]), (wr, wrt, shards[3]))),
    ):
        for straight, across, source in matrices:
            depth = source.shape[0]
            for column in range(0, straight.shape[1], 128):
                whole = stacked(held, at, depth)
                straight[:, column : column + 128] = whole.astype(bf16)
                if across is wjt and column < width:
                    whole = whole * scale
                across[column : column + 128, :] = whole.T.astype(bf16)
                at += depth

    def spread(at):
        return jnp.broadcast_to(columns[:, at : at + 1], (width, 128))

    bj[0:width, :] = spread(0) * scale
    bj[width : 2 * width, :] = jnp.zeros((width, 128), f32)
    bj[2 * width : 3 * width, :] = spread(1)
    for at in range(6):
        bcol[at, :, :] = spread(2 + at)
    halves = [spread(8), spread(9)]
    be[...] = jnp.concatenate(
        [halves[k % 2][k // 2 * share : (k // 2 + 1) * share] for k in range(2 * devices)], axis=0
    )
    vrow[...] = columns.T[0:8, :]
    for ref in (gj, go, ge, gr, accb, accv):
        ref[...] = jnp.zeros_like(ref)

    lane = lax.broadcasted_iota(jnp.int32, (CHUNK, 128), 1)
    low_lanes = lane < HEAD_DIM
    halves = [slice(t, t + 128) for t in range(0, CHUNK, 128)]
    ones = jnp.ones((16, HALF), bf16)

    def add_sums(row, values):
        accb[row : row + values.shape[0], :] += values

    def out_copy(seq):
        slot = lax.rem(seq, 2)
        return pltpu.make_async_copy(land_x.at[slot], out_hbm.at[seq], out_sem.at[slot])

    def forward(seq, carry):
        for at in range(0, length, CHUNK):
            rows = slice(at, at + CHUNK)
            made = nn(wjt[...], xT[seq, :, rows])
            for half in halves:
                there = slice(at + half.start, at + half.stop)
                low = (made[:, half] + bj[...]).astype(bf16)
                qkT[seq, :, there] = low[0 : 2 * width]
                vT[:, there] = low[2 * width : 3 * width]
            flat = nn(xtok[seq, rows, :], wj[...])
            qtok[seq, rows, :] = ((flat[:, 0:width] + vrow[0:1, :]) * scale).astype(bf16)
            vtok[seq, rows, :] = (flat[:, 2 * width : 3 * width] + vrow[1:2, :]).astype(bf16)
            codes = codek[seq, rows, :].astype(f32)
            for head in range(HEADS):
                lanes = slice((head // 2) * 128, (head // 2 + 1) * 128)
                mine = low_lanes if head % 2 == 0 else ~low_lanes
                keys = flat[:, width + lanes.start : width + lanes.stop]
                kaug[head, rows, :] = jnp.where(mine, keys, codes).astype(bf16)

        for head in range(HEADS):
            own = slice(head * HEAD_DIM, (head + 1) * HEAD_DIM)
            for block in range(blocks):
                cols = slice(block * HALF, (block + 1) * HALF)
                place = head * blocks + block
                for at in range(0, HALF, CHUNK):
                    there = slice(block * HALF + at, block * HALF + at + CHUNK)
                    pair = [qkT[seq, own, there], codeq[seq, :, there]]
                    if head % 2 == 1:
                        pair = pair[::-1]
                    scores = nn(kaug[head, cols, :], jnp.concatenate(pair, axis=0))
                    for tile in range(0, CHUNK, 128):
                        mine = scores[:, tile : tile + 128]
                        highest = jnp.max(mine, axis=0, keepdims=True)
                        pT[seq, place, :, at + tile : at + tile + 128] = jnp.exp2(
                            (mine - highest) * log2_e
                        ).astype(bf16)
                mixed = nn(jnp.concatenate([vT[own, cols], ones], axis=0), pT[seq, place])
                inverse = 1.0 / mixed[HEAD_DIM : HEAD_DIM + 1, :]
                inv[head : head + 1, cols] = inverse
                mixT[own, cols] = (mixed[0:HEAD_DIM, :] * inverse).astype(bf16)

        @pl.when(seq >= 2)
        def _():
            out_copy(seq - 2).wait()

        slot = lax.rem(seq, 2)
        for at in range(0, length, CHUNK):
            rows = slice(at, at + CHUNK)
            branch = nn(wot[...], mixT[:, rows])
            firsts = []
            for half in halves:
                there = slice(at + half.start, at + half.stop)
                hat, inverse = unit(
                    xT[seq, :, there].astype(f32) + branch[:, half] + bcol[0], width
                )
                hat1[:, half] = hat
                rinv1[0:1, half] = inverse
                first = hat * bcol[1] + bcol[2]
                flow[:, there] = first.astype(bf16)
                firsts.append(first)
            inner = nn(wet[...], flow[:, rows])
            for half in halves:
                there = slice(at + half.start, at + half.stop)
                for r in range(0, inner_width, 64):
                    u = inner[r : r + 64, half] + be[r : r + 64, :]
                    square = u * u
                    t = jnp.tanh(u * (gelu_a + (gelu_a * gelu_b) * square))
                    h = 0.5 + 0.5 * t
                    value = u * h
                    act[r : r + 64, there] = value.astype(bf16)
                    dgelu[r : r + 64, half] = h + value * (1.0 - h) * (
                        2.0 * gelu_a + (6.0 * gelu_a * gelu_b) * square
                    )
            second = nn(wrt[...], act[:, rows])
            grads = []
            results = []
            for k, half in enumerate(halves):
                there = slice(at + half.start, at + half.stop)
                hat, inverse = unit(firsts[k] + second[:, half] + bcol[3], width)
                results.append((hat * bcol[4] + bcol[5]).astype(bf16))
                upstream = cT[seq, :, there].astype(f32)
                add_sums(0, upstream * hat)
                add_sums(width, upstream)
                back = unit_back(upstream * bcol[4], hat, inverse, width)
                low = back.astype(bf16)
                slow[:, there] = low
                add_sums(2 * width, low.astype(f32))
                grads.append(back)
            land_x[slot, rows, :] = nt(identity, jnp.concatenate(results, axis=1)).astype(bf16)
            active_grad = nn(wr[...], slow[:, rows])
            for half in halves:
                there = slice(at + half.start, at + half.stop)
                for r in range(0, inner_width, 64):
                    low = (active_grad[r : r + 64, half] * dgelu[r : r + 64, half]).astype(bf16)
                    igr[r : r + 64, there] = low
                    add_sums(3 * width + r, low.astype(f32))
            deeper = nn(we[...], igr[:, rows])
            for k, half in enumerate(halves):
                there = slice(at + half.start, at + half.stop)
                first_grad = grads[k] + deeper[:, half]
                hat = hat1[:, half]
                base = 3 * width + inner_width
                add_sums(base, first_grad * hat)
                add_sums(base + width, first_grad)
                back = unit_back(first_grad * bcol[1], hat, rinv1[0:1, half], width)
                fig[seq, :, there] = back
                low = back.astype(bf16)
                blow[:, there] = low
                add_sums(base + 2 * width, low.astype(f32))
            grown = nn(wo[...], blow[:, rows]).astype(bf16).astype(f32)
            scaled = []
            for head in range(HEADS):
                own = slice(head * HEAD_DIM, (head + 1) * HEAD_DIM)
                piece = grown[own, :] * inv[head : head + 1, rows]
                total = over_features(piece * mixT[own, rows].astype(f32))
                high = total.astype(bf16).astype(f32)
                dots[seq, 2 * head : 2 * head + 1, rows] = high
                dots[seq, 2 * head + 1 : 2 * head + 2, rows] = total - high
                scaled.append(piece.astype(bf16))
            scaled = jnp.concatenate(scaled, axis=0)
            doT[seq, :, rows] = scaled
            dotok[seq, rows, :] = nt(identity, scaled).astype(bf16)
        out_copy(seq).start()
        gr[...] += nt(act[...], slow[...])
        ge[...] += nt(flow[...], igr[...])
        go[...] += nt(mixT[...], blow[...])
        return carry

    lax.fori_loop(0, count, forward, 0)

    def pack(reduce, sources):
        for device in range(devices):
            outer = device // inners
            pieces = []
            for ref in sources:
                depth = ref.shape[0] // devices
                pieces += column_blocks(ref[device * depth : (device + 1) * depth, :])
            packed = reduce.packed
            packed[outer % 2, outer // 2, device % inners] = padded_rows(pieces, packed.shape[3])

    sum_a, sum_b = Reduce(peers, *reduce_a), Reduce(peers, *reduce_b)
    pack(sum_a, (go, ge, gr))
    sum_a.first()

    low_half = lax.broadcasted_iota(jnp.int32, (HALF, 128), 1) < HEAD_DIM
    keep = [low_half.astype(f32).astype(bf16), (~low_half).astype(f32).astype(bf16)]
    fill = [-keep[1], -keep[0]]
    extra_row = lax.broadcasted_iota(jnp.int32, (16, HALF), 0)

    def backward(seq, carry):
        for pair in range(HEADS // 2):
            lanes = slice(pair * 128, (pair + 1) * 128)
            for block in range(blocks):
                cols = slice(block * HALF, (block + 1) * HALF)
                keys, values = [], []
                for odd in range(2):
                    head = pair * 2 + odd
                    own = slice(head * HEAD_DIM, (head + 1) * HEAD_DIM)
                    place = head * blocks + block
                    high = dots[seq, 2 * head : 2 * head + 1, cols]
                    rest = dots[seq, 2 * head + 1 : 2 * head + 2, cols]
                    extra = jnp.where(extra_row == 0, high, jnp.where(extra_row == 1, rest, 0.0))
                    extra = jnp.concatenate([extra, jnp.zeros((HEAD_DIM - 16, HALF), f32)], axis=0)
                    stack = [doT[seq, own, cols], extra.astype(bf16)]
                    if odd:
                        stack = stack[::-1]
                    side = vtok[seq, cols, lanes] * keep[odd] + fill[odd]
                    grads = nn(side, jnp.concatenate(stack, axis=0))
                    dsT = (pT[seq, place].astype(f32) * grads).astype(bf16)
                    values.append(nn(pT[seq, place], dotok[seq, cols, lanes]))
                    keys.append(nn(dsT, qtok[seq, cols, lanes]))
                    key_rows = slice(width + own.start, width + own.stop)
                    qkT[seq, own, cols] = (nn(qkT[seq, key_rows, cols], dsT) * scale).astype(bf16)
                qtok[seq, cols, lanes] = jnp.where(low_half, keys[0], keys[1]).astype(bf16)
                dotok[seq, cols, lanes] = jnp.where(low_half, values[0], values[1]).astype(bf16)
        turned = xT[seq]
        gj[:, 0:width] += nt(turned, qkT[seq, 0:width, :])
        gj[:, width : 2 * width] += nn(turned, qtok[seq])
        gj[:, 2 * width : 3 * width] += nn(turned, dotok[seq])
        base = 6 * width + inner_width
        for at in range(0, length, 128):
            add_sums(base, qkT[seq, 0:width, at : at + 128].astype(f32))
        total = accv[...]
        for at in range(0, length, 128):
            part = dotok[seq, at : at + 128, :].astype(f32)
            total += jnp.sum(part.reshape(16, 8, width), axis=0)
        accv[...] = total

        @pl.when(seq == 0)
        def _():
            sum_a.second()

        if count > 1:

            @pl.when(seq == 1)
            def _():
                sum_a.third()

        return carry

    lax.fori_loop(0, count, backward, 0)
    if count == 1:
        sum_a.third()

    sums = jnp.sum(accb[...], axis=1, keepdims=True)
    wide = jnp.broadcast_to(sums[3 * width : 3 * width + inner_width], (inner_width, 128))
    hidden_sums = [
        jnp.concatenate(
            [wide[k * share : (k + 1) * share] for k in range(first, 2 * devices, 2)], axis=0
        )
        for first in range(2)
    ]
    later = 3 * width + inner_width
    places = {0: later + 3 * width, 2: later + 2 * width, 3: later, 4: later + width}
    places.update({5: 2 * width, 6: 0, 7: width})
    lanes = lax.broadcasted_iota(jnp.int32, (width, 128), 1)
    value_sums = jnp.broadcast_to(jnp.sum(accv[...], axis=0, keepdims=True), (128, width)).T
    columns = jnp.where(lanes == 1, value_sums, 0.0)
    for at, place in places.items():
        columns = jnp.where(lanes == at, sums[place : place + width], columns)
    for at, item in enumerate(hidden_sums):
        columns = jnp.where(lanes == VECTORS + at, item, columns)
    bcol[0] = columns
    pack(sum_b, (bcol.at[0], gj))
    sum_b.first()

    def tg_copies(seq):
        slot = lax.rem(seq, 2)
        return [
            pltpu.make_async_copy(
                turn.at[slot * 2 + tile, pl.ds(0, length)],
                tg_hbm.at[seq, tile],
                tg_sem.at[slot, tile],
            )
            for tile in range(tiles)
        ]

    def inputs_back(seq, carry):
        @pl.when(seq >= 2)
        def _():
            for copy in tg_copies(seq - 2):
                copy.wait()

        slot = lax.rem(seq, 2)
        for at in range(0, length, CHUNK):
            rows = slice(at, at + CHUNK)
            result = (
                nn(wj[:, 0:width], qkT[seq, 0:width, rows])
                + nt(wj[:, width : 2 * width], qtok[seq, rows, :])
                + nt(wj[:, 2 * width : 3 * width], dotok[seq, rows, :])
                + fig[seq, :, rows]
            ).T
            for tile in range(tiles):
                turn[slot * 2 + tile, rows, :] = result[:, tile * 128 : (tile + 1) * 128]
        for copy in tg_copies(seq):
            copy.start()

        @pl.when(seq == 0)
        def _():
            sum_b.second()

        if count > 2:

            @pl.when(seq == 2)
            def _():
                sum_b.third()

        return carry

    lax.fori_loop(0, count, inputs_back, 0)
    if count <= 2:
        sum_b.third()
    fin_a[...] = sum_a.finish()
    fin_b[...] = sum_b.finish()
    for seq in range(max(count - 2, 0), count):
        out_copy(seq).wait()
        for copy in tg_copies(seq):
            copy.wait()


def run_layer(outers, inners, tokens, segment_ids, padding_mask, cotangent, shards):
    count, length, width = tokens.shape
    devices = outers * inners
    share = width // devices
    inner_width = shards[2].shape[1]
    tiles = width // 128
    chips = outers // 2
    blocks = length // HALF

    def rows_of(items):
        return sum(item.size // 128 for item in items)

    held_a = rounded_up(share + rows_of(shards[:1]), 16)
    held_b = rounded_up(rows_of(shards[1:4]), 16)
    sends = gather_sends(outers, inners)
    dma = pltpu.SemaphoreType.DMA
    vmem = pltpu.VMEM
    shape = jax.ShapeDtypeStruct
    scratch = [vmem(item.shape, bf16) for item in shards]
    scratch += [
        vmem((2, length, width), bf16),
        vmem((2, length, width), bf16),
        vmem((count, length), jnp.int32),
        vmem((count, length), jnp.int32),
        vmem((width, 3 * width), bf16),
        vmem((width, width), bf16),
        vmem((width, inner_width), bf16),
        vmem((inner_width, width), bf16),
        vmem((3 * width, width), bf16),
        vmem((width, width), bf16),
        vmem((inner_width, width), bf16),
        vmem((width, inner_width), bf16),
        vmem((3 * width, 128), f32),
        vmem((inner_width, 128), f32),
        vmem((6, width, 128), f32),
        vmem((8, width), f32),
        vmem((2 * tiles, length + HALF, 128), f32),
        vmem((count, length, width), bf16),
        vmem((count, width, length), bf16),
        vmem((count, width, length), bf16),
        vmem((count, length, 128), bf16),
        vmem((count, HEAD_DIM, length), bf16),
        vmem((count, 2 * width, length), bf16),
        vmem((width, length), bf16),
        vmem((count, length, width), bf16),
        vmem((HEADS, length, 128), bf16),
        vmem((count, length, width), bf16),
        vmem((count, HEADS * blocks, HALF, HALF), bf16),
        vmem((8, length), f32),
        vmem((width, length), bf16),
        vmem((width, CHUNK), f32),
        vmem((8, CHUNK), f32),
        vmem((inner_width, length), bf16),
        vmem((width, length), bf16),
        vmem((inner_width, length), bf16),
        vmem((width, length), bf16),
        vmem((width, length), bf16),
        vmem((inner_width, CHUNK), f32),
        vmem((count, width, length), f32),
        vmem((count, 8, length), f32),
        vmem((width, 3 * width), f32),
        vmem((width, width), f32),
        vmem((width, inner_width), f32),
        vmem((inner_width, width), f32),
        vmem((7 * width + inner_width, 128), f32),
        vmem((8, width), f32),
        vmem((2, chips, inners, held_a, 128), bf16),
        dma((sends,)),
        dma((2, chips, inners)),
        vmem((2, chips, inners, held_b, 128), bf16),
        dma((sends,)),
        dma((2, chips, inners)),
    ]
    scratch += reduce_scratch(outers, inners, held_b)
    scratch += reduce_scratch(outers, inners, held_a)
    scratch += [dma((len(shards) + 2,)), dma((2, 2)), dma((2,)), dma((2, tiles))]
    hbm = pl.BlockSpec(memory_space=pl.ANY)
    return pl.pallas_call(
        functools.partial(layer_kernel, outers, inners),
        in_specs=[pl.BlockSpec(memory_space=pltpu.SMEM)] + [hbm] * (4 + len(shards)),
        out_specs=[hbm, hbm] + [pl.BlockSpec(memory_space=pltpu.VMEM)] * 2,
        out_shape=[
            shape(tokens.shape, bf16),
            shape((count, tiles, length, 128), f32),
            shape((held_b, 128), f32),
            shape((held_a, 128), f32),
        ],
        scratch_shapes=scratch,
        compiler_params=pltpu.CompilerParams(
            collective_id=0, has_side_effects=True, vmem_limit_bytes=64 * 1024 * 1024 - 65536
        ),
        name="layer",
    )(segment_ids, tokens, cotangent, segment_ids, padding_mask, *shards)


def finish_kernel(seg_smem, out_turned, tg_turned, fin_a, fin_b, *refs):
    layer_out, tokens_grad, matrices, vectors = refs[0], refs[1], refs[2:6], refs[6:-1]
    turn = refs[-1]
    seq = pl.program_id(0)
    length, width = layer_out.shape[1], layer_out.shape[2]
    start = big_cell_start(seg_smem, seq, length)
    for tile in range(width // 128):
        lanes = slice(tile * 128, (tile + 1) * 128)
        for k, target in enumerate((layer_out, tokens_grad)):
            if k == 0:
                whole = out_turned[0, :, lanes].astype(f32)
            else:
                whole = tg_turned[0, tile]
            turn[k, tile, 0:HALF] = whole[length - HALF : length]
            turn[k, tile, HALF : HALF + length] = whole
            for at in range(0, length, CHUNK):
                piece = turn[k, tile, pl.ds(HALF - start + at, CHUNK), :]
                target[0, at : at + CHUNK, lanes] = piece.astype(target.dtype)

    @pl.when(seq == 0)
    def _():
        rows = vectors[0].shape[0]
        lines = fin_b[0:rows, :].T
        for at, ref in enumerate(vectors[:-1]):
            ref[...] = lines[at, :]
        vectors[-1][...] = jnp.concatenate([lines[VECTORS, :], lines[VECTORS + 1, :]])
        for source, at, targets in ((fin_b, rows, matrices[:1]), (fin_a, 0, matrices[1:])):
            for ref in targets:
                depth = ref.shape[0]
                for column in range(0, ref.shape[1], 128):
                    ref[:, column : column + 128] = source[at : at + depth, :]
                    at += depth


def finish(segment_ids, out_turned, tg_turned, fin_a, fin_b, shards):
    count, length, width = out_turned.shape
    tiles = width // 128

    def whole(shape):
        return pl.BlockSpec(shape, lambda i: (0,) * len(shape))

    per_seq = pl.BlockSpec((1, length, width), lambda i: (i, 0, 0))
    shape = jax.ShapeDtypeStruct
    return pl.pallas_call(
        finish_kernel,
        grid=(count,),
        in_specs=[
            pl.BlockSpec(memory_space=pltpu.SMEM),
            per_seq,
            pl.BlockSpec((1, tiles, length, 128), lambda i: (i, 0, 0, 0)),
            whole(fin_a.shape),
            whole(fin_b.shape),
        ],
        out_specs=[per_seq, per_seq] + [whole(item.shape) for item in shards],
        out_shape=[shape(out_turned.shape, bf16), shape(out_turned.shape, f32)]
        + [shape(item.shape, f32) for item in shards],
        scratch_shapes=[pltpu.VMEM((2, tiles, length + HALF, 128), f32)],
        compiler_params=pltpu.CompilerParams(
            dimension_semantics=("arbitrary",), vmem_limit_bytes=60 * 1024 * 1024
        ),
        name="finish",
    )(segment_ids, out_turned, tg_turned, fin_a, fin_b)


def on_device(
    outers,
    inners,
    tokens,
    segment_ids,
    padding_mask,
    joint_weight,
    query_bias,
    value_bias,
    output_weight,
    output_bias,
    first_gain,
    first_shift,
    expand_weight,
    expand_bias,
    reduce_weight,
    reduce_bias,
    second_gain,
    second_shift,
    cotangent,
):
    shards = (
        joint_weight,
        output_weight,
        expand_weight,
        reduce_weight,
        query_bias,
        value_bias,
        output_bias,
        first_gain,
        first_shift,
        reduce_bias,
        second_gain,
        second_shift,
        expand_bias,
    )
    turned = run_layer(outers, inners, tokens, segment_ids, padding_mask, cotangent, shards)
    layer_out, tokens_grad, *owned = finish(segment_ids, *turned, shards)
    gj, go, ge, gr, query, value, out, gain1, shift1, reduce, gain2, shift2, expand = owned
    return (
        layer_out,
        tokens_grad,
        gj,
        query,
        value,
        go,
        out,
        gain1,
        shift1,
        ge,
        expand,
        gr,
        reduce,
        gain2,
        shift2,
    )


def solution(mesh):
    rows = P(("outer", "inner"))
    rows2 = P(("outer", "inner"), None)
    rows3 = P(("outer", "inner"), None, None)
    weights = (rows2, rows, rows, rows2, rows, rows, rows, rows2, rows, rows2, rows, rows, rows)
    return jax.shard_map(
        functools.partial(on_device, mesh.shape["outer"], mesh.shape["inner"]),
        mesh=mesh,
        in_specs=(rows3, rows2, rows2) + weights + (rows3,),
        out_specs=(rows3, rows3) + weights,
        check_vma=False,
    )
```

```python
import functools
import math

import jax
import jax.numpy as jnp
from jax import lax
from jax.experimental import pallas as pl
from jax.experimental.pallas import tpu as pltpu
from jax.sharding import PartitionSpec as P

HEADS = 4
HEAD_DIM = 64
HALF = 512
CHUNK = 256
VECTORS = 8
MESH = pl.DeviceIdType.MESH

norm_epsilon = 1e-06
mask_step = -(2.0**100)
log2_e = math.log2(math.e)
gelu_a = math.sqrt(2.0 / math.pi)
gelu_b = 0.044715

f32 = jnp.float32
bf16 = jnp.bfloat16


def nn(left, right):
    return lax.dot_general(left, right, (((1,), (0,)), ((), ())), preferred_element_type=f32)


def nt(left, right):
    return lax.dot_general(left, right, (((1,), (1,)), ((), ())), preferred_element_type=f32)


def over_features(values):
    return jnp.sum(values, axis=0, keepdims=True)


def column_blocks(values):
    return [values[:, at : at + 128] for at in range(0, values.shape[1], 128)]


def padded_rows(pieces, rows):
    have = sum(piece.shape[0] for piece in pieces)
    if rows > have:
        pieces = pieces + [jnp.zeros((rows - have, 128), f32)]
    return jnp.concatenate(pieces, axis=0)


def rounded_up(amount, to):
    return (amount + to - 1) // to * to


def big_cell_start(seg_ref, seq, length):
    wanted = seg_ref[seq, HALF - 1]
    low = jnp.int32(0)
    step = HALF
    while step > 1:
        step //= 2
        probe = low + step
        low = jnp.where(seg_ref[seq, probe - 1] < wanted, probe, low)
    last = jnp.minimum(low + HALF - 1, length - 1)
    return jnp.where(seg_ref[seq, last] == wanted, low, HALF)


def copy_to(source, target, send, receive, outer, inner):
    return pltpu.make_async_remote_copy(
        src_ref=source,
        dst_ref=target,
        send_sem=send,
        recv_sem=receive,
        device_id=(outer, inner),
        device_id_type=MESH,
    )


class Peers:
    def __init__(self, outers, inners):
        self.outers, self.inners = outers, inners
        self.outer = lax.axis_index("outer")
        self.inner = lax.axis_index("inner")
        self.core = lax.rem(self.outer, 2)
        self.chip = lax.div(self.outer, 2)
        self.chips = outers // 2
        self.mate = self.chip * 2 + 1 - self.core

    def along_inner(self):
        return [lax.rem(self.inner + step, self.inners) for step in range(1, self.inners)]

    def along_chips(self):
        return [lax.rem(self.chip + step, self.chips) for step in range(1, self.chips)]

    def greet(self):
        barrier = pltpu.get_barrier_semaphore()
        others = [(self.outer, at) for at in self.along_inner()]
        others += [(at * 2 + self.core, self.inner) for at in self.along_chips()]
        others += [(self.mate, self.inner)]
        for other in others:
            pl.semaphore_signal(barrier, inc=1, device_id=other, device_id_type=MESH)
        pl.semaphore_wait(barrier, len(others))


class Gather:
    def __init__(self, peers, held, send, receive):
        self.peers, self.held, self.send, self.receive = peers, held, send, receive
        self.sent = []

    def pass_on(self, core, chip, at, outer, inner):
        block = self.held.at[core, chip, at]
        copy = copy_to(
            block,
            block,
            self.send.at[len(self.sent)],
            self.receive.at[core, chip, at],
            outer,
            inner,
        )
        copy.start()
        self.sent.append(copy)

    def arrived(self, core, chip, at):
        block = self.held.at[core, chip, at]
        peers = self.peers
        copy_to(
            block,
            block,
            self.send.at[0],
            self.receive.at[core, chip, at],
            peers.outer,
            peers.inner,
        ).wait_recv()

    def spread(self, at):
        peers = self.peers
        for other in peers.along_chips():
            self.pass_on(peers.core, peers.chip, at, other * 2 + peers.core, peers.inner)
        self.pass_on(peers.core, peers.chip, at, peers.mate, peers.inner)

    def first(self):
        peers = self.peers
        for at in peers.along_inner():
            self.pass_on(peers.core, peers.chip, peers.inner, peers.outer, at)
        self.spread(peers.inner)

    def second(self):
        peers = self.peers
        for at in peers.along_inner():
            self.arrived(peers.core, peers.chip, at)
            self.spread(at)

    def third(self):
        peers = self.peers
        for at in [peers.inner] + peers.along_inner():
            for other in peers.along_chips():
                self.arrived(peers.core, other, at)
                self.pass_on(peers.core, other, at, peers.mate, peers.inner)

    def finish(self):
        peers = self.peers
        for at in [peers.inner] + peers.along_inner():
            for other in [peers.chip] + peers.along_chips():
                self.arrived(1 - peers.core, other, at)
        for copy in self.sent:
            copy.wait_send()


def gather_sends(outers, inners):
    chips = outers // 2
    return (inners - 1) + inners * (chips - 1) + inners * chips


class Reduce:
    def __init__(self, peers, packed, from_mate, mid, from_chips, last, from_inner, send, receive):
        self.peers, self.packed, self.from_mate = peers, packed, from_mate
        self.mid, self.from_chips, self.last = mid, from_chips, last
        self.from_inner, self.send, self.receive = from_inner, send, receive

    def to_mate(self):
        peers = self.peers
        return copy_to(
            self.packed.at[1 - peers.core],
            self.from_mate,
            self.send.at[0],
            self.receive.at[0],
            peers.mate,
            peers.inner,
        )

    def to_chips(self):
        peers = self.peers
        return [
            copy_to(
                self.mid.at[k],
                self.from_chips.at[k],
                self.send.at[1 + k],
                self.receive.at[1 + k],
                other * 2 + peers.core,
                peers.inner,
            )
            for k, other in enumerate(peers.along_chips())
        ]

    def to_inner(self):
        peers = self.peers
        return [
            copy_to(
                self.last.at[k],
                self.from_inner.at[k],
                self.send.at[peers.chips + k],
                self.receive.at[peers.chips + k],
                peers.outer,
                at,
            )
            for k, at in enumerate(peers.along_inner())
        ]

    def first(self):
        self.to_mate().start()

    def second(self):
        peers = self.peers
        self.to_mate().wait()
        for k, (other, copy) in enumerate(zip(peers.along_chips(), self.to_chips())):
            for at in range(peers.inners):
                total = self.packed[peers.core, other, at] + self.from_mate[other, at]
                self.mid[k, at] = total.astype(bf16)
            copy.start()

    def own(self, at):
        peers = self.peers
        total = self.packed[peers.core, peers.chip, at] + self.from_mate[peers.chip, at]
        for k in range(peers.chips - 1):
            total += self.from_chips[k, at].astype(f32)
        return total

    def third(self):
        for copy in self.to_chips():
            copy.wait()
        for k, (at, copy) in enumerate(zip(self.peers.along_inner(), self.to_inner())):
            self.last[k] = self.own(at).astype(bf16)
            copy.start()

    def finish(self):
        total = self.own(self.peers.inner)
        for k, copy in enumerate(self.to_inner()):
            copy.wait()
            total += self.from_inner[k].astype(f32)
        return total


def reduce_scratch(outers, inners, rows):
    chips = outers // 2
    return [
        pltpu.VMEM((2, chips, inners, rows, 128), f32),
        pltpu.VMEM((chips, inners, rows, 128), f32),
        pltpu.VMEM((max(chips - 1, 1), inners, rows, 128), bf16),
        pltpu.VMEM((max(chips - 1, 1), inners, rows, 128), bf16),
        pltpu.VMEM((inners - 1, rows, 128), bf16),
        pltpu.VMEM((inners - 1, rows, 128), bf16),
        pltpu.SemaphoreType.DMA((chips + inners,)),
        pltpu.SemaphoreType.DMA((chips + inners,)),
    ]


REDUCE_SCRATCH = 8


def unit(hidden, width):
    centred = hidden - over_features(hidden) * (1.0 / width)
    inverse = lax.rsqrt(over_features(centred * centred) * (1.0 / width) + norm_epsilon)
    return centred * inverse, inverse


def unit_back(inside, hat, inverse, width):
    return inverse * (
        inside
        - over_features(inside) * (1.0 / width)
        - hat * (over_features(inside * hat) * (1.0 / width))
    )


def layer_kernel(outers, inners, *refs):
    refs = list(refs)

    def grab(amount):
        taken = refs[:amount]
        del refs[:amount]
        return taken

    seg_smem, tokens_hbm, cot_hbm, seg_hbm, pad_hbm = grab(5)
    shard_hbm = grab(4 + VECTORS + 1)
    out_hbm, tg_hbm, fin_a, fin_b = grab(4)
    shards = grab(4 + VECTORS + 1)
    land_x, land_c, segv, padv = grab(4)
    wj, wo, we, wr, wjt, wot, wet, wrt, bj, be, bcol, vrow = grab(12)
    turn, xtok, xT, cT, codek, codeq = grab(6)
    qkT, vT, qtok, kaug, vtok, pT, inv, mixT = grab(8)
    hat1, rinv1, act, slow, igr, flow, blow, dgelu, dsT = grab(9)
    (dots,) = grab(1)
    doT, dotok = cT, xtok
    gj, go, ge, gr, accb, accc = grab(6)
    held_a, send_a, receive_a, held_b, send_b, receive_b = grab(6)
    reduce_a, reduce_b = grab(REDUCE_SCRATCH), grab(REDUCE_SCRATCH)
    shard_sem, land_sem, out_sem, tg_sem = grab(4)

    count, length, width = tokens_hbm.shape
    inner_width = we.shape[1]
    devices = outers * inners
    share = width // devices
    scale = HEAD_DIM**-0.5
    tiles = width // 128
    blocks = length // HALF
    peers = Peers(outers, inners)

    def land(seq):
        slot = seq % 2
        return [
            pltpu.make_async_copy(tokens_hbm.at[seq], land_x.at[slot], land_sem.at[0, slot]),
            pltpu.make_async_copy(cot_hbm.at[seq], land_c.at[slot], land_sem.at[1, slot]),
        ]

    small = [
        pltpu.make_async_copy(source, target, shard_sem.at[k])
        for k, (source, target) in enumerate(
            zip(shard_hbm + [seg_hbm, pad_hbm], shards + [segv, padv])
        )
    ]
    for copy in small:
        copy.start()
    for seq in range(min(2, count)):
        for copy in land(seq):
            copy.start()
    for copy in small:
        copy.wait()

    lines = [ref[...].astype(f32).reshape(1, ref.shape[0]) for ref in shards[4:]]
    lines = lines[:-1] + [lines[-1][:, :share], lines[-1][:, share:]]
    lines.append(jnp.zeros((128 - len(lines), share), f32))
    pieces = [jnp.concatenate(lines, axis=0).T] + column_blocks(shards[0][...].astype(f32))
    here = (peers.core, peers.chip, peers.inner)
    held_a[here] = padded_rows(pieces, held_a.shape[3]).astype(bf16)
    pieces = []
    for ref in shards[1:4]:
        pieces += column_blocks(ref[...].astype(f32))
    held_b[here] = padded_rows(pieces, held_b.shape[3]).astype(bf16)
    peers.greet()
    gather_a = Gather(peers, held_a, send_a, receive_a)
    gather_b = Gather(peers, held_b, send_b, receive_b)
    gather_a.first()
    gather_b.first()

    identity = (
        lax.broadcasted_iota(jnp.int32, (CHUNK, CHUNK), 0)
        == lax.broadcasted_iota(jnp.int32, (CHUNK, CHUNK), 1)
    )
    identity = identity.astype(f32).astype(bf16)

    for ref in [mixT, act, flow] + [xT.at[seq] for seq in range(count)]:
        ref[ref.shape[0] - 16 : ref.shape[0], :] = jnp.ones((16, length), bf16)
    for ref in (gj, go, ge, gr, accb, accc):
        ref[...] = jnp.zeros_like(ref)
    some_ones = jnp.ones((16, CHUNK), bf16)

    def prepare(seq):
        for copy in land(seq):
            copy.wait()
        start = big_cell_start(seg_smem, seq, length)
        slot = seq % 2

        def turned(tile, whole):
            turn[tile, 0:length, :] = whole
            turn[tile, length : length + HALF, :] = whole[0:HALF]

        def take(tile, at):
            return turn[tile, pl.ds(start + at, CHUNK), :]

        for source, target in ((land_x, xT), (land_c, cT)):
            for tile in range(tiles):
                turned(tile, source[slot, :, tile * 128 : (tile + 1) * 128].astype(f32))
            for at in range(0, length, CHUNK):
                piece = jnp.concatenate([take(tile, at) for tile in range(tiles)], axis=1)
                piece = piece.astype(bf16)
                if target is xT:
                    xtok[seq, at : at + CHUNK, :] = piece
                else:
                    accc[...] += nn(some_ones, piece)
                target[seq, 0:width, at : at + CHUNK] = nt(identity, piece).astype(bf16)
        if seq + 2 < count:
            for copy in land(seq + 2):
                copy.start()

        position = lax.broadcasted_iota(jnp.int32, (1, length), 1)
        code = lax.broadcasted_iota(jnp.int32, (8, length), 0)
        hidden = (padv[seq : seq + 1, :] != 1).astype(f32)
        same = (segv[seq : seq + 1, :] == code).astype(f32)
        parts_q = [1.0 - same]
        parts_k = [same * mask_step]
        for digit in ((position // 64) % 8, (position // 8) % 8, position % 8):
            equal = (digit == code).astype(f32)
            parts_q.append(1.0 - equal)
            parts_k.append(equal * hidden * mask_step)
        both = jnp.concatenate(parts_k + parts_q + parts_k + parts_q, axis=0).astype(bf16)
        for at in range(0, length, CHUNK):
            flat = nt(identity, both[:, at : at + CHUNK])
            turn[2, at : at + CHUNK, :] = flat
            if at < HALF:
                turn[2, length + at : length + at + CHUNK, :] = flat
        nothing = jnp.zeros((32, CHUNK), f32)
        for at in range(0, length, CHUNK):
            piece = take(2, at).astype(bf16)
            codek[seq, at : at + CHUNK, :] = piece
            across = nt(identity[0:128, 0:128], piece)
            codeq[seq, :, at : at + CHUNK] = jnp.concatenate(
                [across[32:64], nothing], axis=0
            ).astype(bf16)

    steps = [
        [gather_a.second],
        [gather_a.third, gather_b.second],
        [gather_b.third],
    ]
    for seq in range(count):
        prepare(seq)
        if seq < len(steps):
            for step in steps[seq]:
                step()
    for step in sum(steps[count:], []):
        step()
    gather_a.finish()
    gather_b.finish()

    def stacked(held, at, depth):
        stack = []
        for device in range(devices):
            outer, inner = device // inners, device % inners
            stack.append(held[outer % 2, outer // 2, inner].astype(f32)[at : at + depth])
        return jnp.concatenate(stack, axis=0)

    columns = stacked(held_a, 0, share)
    for held, at, matrices in (
        (held_a, share, ((wj, wjt, shards[0]),)),
        (held_b, 0, ((wo, wot, shards[1]), (we, wet, shards[2]), (wr, wrt, shards[3]))),
    ):
        for straight, across, source in matrices:
            depth = source.shape[0]
            for column in range(0, straight.shape[1], 128):
                whole = stacked(held, at, depth)
                straight[:, column : column + 128] = whole.astype(bf16)
                if across is wjt and column < width:
                    whole = whole * scale
                across[column : column + 128, :] = whole.T.astype(bf16)
                at += depth

    def spread(at):
        return jnp.broadcast_to(columns[:, at : at + 1], (width, 128))

    bj[0:width, :] = spread(0) * scale
    bj[width : 2 * width, :] = jnp.zeros((width, 128), f32)
    bj[2 * width : 3 * width, :] = spread(1)
    for at in range(6):
        bcol[at, :, :] = spread(2 + at)
    halves = [spread(8), spread(9)]
    be[...] = jnp.concatenate(
        [halves[k % 2][k // 2 * share : (k // 2 + 1) * share] for k in range(2 * devices)], axis=0
    )
    vrow[...] = columns.T[0:8, :]

    lane = lax.broadcasted_iota(jnp.int32, (CHUNK, 128), 1)
    low_lanes = lane < HEAD_DIM
    halves = [slice(t, t + 128) for t in range(0, CHUNK, 128)]
    ones = jnp.ones((16, HALF), bf16)

    def add_sums(row, values):
        accb[row : row + values.shape[0], :] += values

    def out_copy(seq):
        slot = lax.rem(seq, 2)
        return pltpu.make_async_copy(land_x.at[slot], out_hbm.at[seq], out_sem.at[slot])

    def attend(seq):
        for at in range(0, length, CHUNK):
            rows = slice(at, at + CHUNK)
            made = nn(wjt[...], xT[seq, 0:width, rows])
            flat = nn(xtok[seq, rows, :], wj[...])
            for half in halves:
                there = slice(at + half.start, at + half.stop)
                low = (made[:, half] + bj[...]).astype(bf16)
                qkT[seq, :, there] = low[0 : 2 * width]
                vT[:, there] = low[2 * width : 3 * width]
            qtok[seq, rows, :] = ((flat[:, 0:width] + vrow[0:1, :]) * scale).astype(bf16)
            vtok[seq, rows, :] = (flat[:, 2 * width : 3 * width] + vrow[1:2, :]).astype(bf16)
            codes = codek[seq, rows, :].astype(f32)
            for head in range(HEADS):
                lanes = slice((head // 2) * 128, (head // 2 + 1) * 128)
                mine = low_lanes if head % 2 == 0 else ~low_lanes
                keys = flat[:, width + lanes.start : width + lanes.stop]
                kaug[head, rows, :] = jnp.where(mine, keys, codes).astype(bf16)

        def scores_of(head, block, at):
            own = slice(head * HEAD_DIM, (head + 1) * HEAD_DIM)
            cols = slice(block * HALF, (block + 1) * HALF)
            there = slice(block * HALF + at, block * HALF + at + CHUNK)
            pair = [qkT[seq, own, there], codeq[seq, :, there]]
            if head % 2 == 1:
                pair = pair[::-1]
            return nn(kaug[head, cols, :], jnp.concatenate(pair, axis=0))

        units = [
            (head, block, at)
            for head in range(HEADS)
            for block in range(blocks)
            for at in range(0, HALF, CHUNK)
        ]
        coming = scores_of(*units[0])
        for k, (head, block, at) in enumerate(units):
            scores = coming
            if k + 1 < len(units):
                coming = scores_of(*units[k + 1])
            own = slice(head * HEAD_DIM, (head + 1) * HEAD_DIM)
            place = head * blocks + block
            for tile in range(0, CHUNK, 128):
                mine = scores[:, tile : tile + 128]
                highest = jnp.max(mine, axis=0, keepdims=True)
                pT[seq, place, :, at + tile : at + tile + 128] = jnp.exp2(
                    (mine - highest) * log2_e
                ).astype(bf16)
            cols = slice(block * HALF, (block + 1) * HALF)
            there = slice(cols.start + at, cols.start + at + CHUNK)
            mixed = nn(
                jnp.concatenate([vT[own, cols], ones], axis=0), pT[seq, place, :, at : at + CHUNK]
            )
            inverse = 1.0 / mixed[HEAD_DIM : HEAD_DIM + 1, :]
            inv[head : head + 1, there] = inverse
            mixT[own, there] = (mixed[0:HEAD_DIM, :] * inverse).astype(bf16)

    def dense(seq):
        slot = lax.rem(seq, 2)
        for at in range(0, length, CHUNK):
            side = (at // CHUNK) % 2
            rows = slice(at, at + CHUNK)
            branch = nn(wot[...], mixT[0:width, rows])
            firsts = []
            for half in halves:
                there = slice(at + half.start, at + half.stop)
                hat, inverse = unit(
                    xT[seq, 0:width, there].astype(f32) + branch[:, half] + bcol[0], width
                )
                hat1[side, :, half] = hat
                rinv1[side, 0:1, half] = inverse
                first = hat * bcol[1] + bcol[2]
                flow[0:width, there] = first.astype(bf16)
                firsts.append(first)
                yield
            inner = nn(wet[...], flow[0:width, rows])
            for half in halves:
                there = slice(at + half.start, at + half.stop)
                for r in range(0, inner_width, 64):
                    u = inner[r : r + 64, half] + be[r : r + 64, :]
                    square = u * u
                    t = jnp.tanh(u * (gelu_a + (gelu_a * gelu_b) * square))
                    h = 0.5 + 0.5 * t
                    value = u * h
                    act[r : r + 64, there] = value.astype(bf16)
                    dgelu[side, r : r + 64, half] = h + value * (1.0 - h) * (
                        2.0 * gelu_a + (6.0 * gelu_a * gelu_b) * square
                    )
                    if r % 256 == 192:
                        yield
            second = nn(wrt[...], act[0:inner_width, rows])
            grads, results, gains = [], [], []
            for k, half in enumerate(halves):
                there = slice(at + half.start, at + half.stop)
                hat, inverse = unit(firsts[k] + second[:, half] + bcol[3], width)
                results.append((hat * bcol[4] + bcol[5]).astype(bf16))
                upstream = cT[seq, :, there].astype(f32)
                gains.append(upstream * hat)
                back = unit_back(upstream * bcol[4], hat, inverse, width)
                slow[:, there] = back.astype(bf16)
                grads.append(back)
                yield
            add_sums(0, gains[0] + gains[1])
            active_grad = nn(wr[...], slow[:, rows])
            land_x[slot, rows, :] = nt(identity, jnp.concatenate(results, axis=1)).astype(bf16)
            for half in halves:
                there = slice(at + half.start, at + half.stop)
                for r in range(0, inner_width, 64):
                    igr[r : r + 64, there] = (
                        active_grad[r : r + 64, half] * dgelu[side, r : r + 64, half]
                    ).astype(bf16)
                yield
            deeper = nn(we[...], igr[:, rows])
            gains, shifts = [], []
            for k, half in enumerate(halves):
                there = slice(at + half.start, at + half.stop)
                first_grad = grads[k] + deeper[:, half]
                hat = hat1[side, :, half]
                gains.append(first_grad * hat)
                shifts.append(first_grad)
                back = unit_back(first_grad * bcol[1], hat, rinv1[side, 0:1, half], width)
                blow[seq, :, there] = back.astype(bf16)
                yield
            add_sums(width, gains[0] + gains[1])
            add_sums(2 * width, shifts[0] + shifts[1])
            grown = nn(wo[...], blow[seq, :, rows]).astype(bf16).astype(f32)
            scaled = []
            for head in range(HEADS):
                own = slice(head * HEAD_DIM, (head + 1) * HEAD_DIM)
                piece = grown[own, :] * inv[head : head + 1, rows]
                total = over_features(piece * mixT[own, rows].astype(f32))
                high = total.astype(bf16).astype(f32)
                dots[seq, 2 * head : 2 * head + 1, rows] = high
                dots[seq, 2 * head + 1 : 2 * head + 2, rows] = total - high
                scaled.append(piece.astype(bf16))
            scaled = jnp.concatenate(scaled, axis=0)
            doT[seq, :, rows] = scaled
            dotok[seq, rows, :] = nt(identity, scaled).astype(bf16)
            yield
        gr[...] += nt(act[...], slow[...])
        yield
        ge[...] += nt(flow[...], igr[...])
        yield
        go[...] += nt(mixT[...], blow[seq])
        yield

    low_half = lax.broadcasted_iota(jnp.int32, (HALF, 128), 1) < HEAD_DIM
    keep = [low_half.astype(f32).astype(bf16), (~low_half).astype(f32).astype(bf16)]
    fill = [-keep[1], -keep[0]]
    extra_row = lax.broadcasted_iota(jnp.int32, (16, HALF), 0)

    def attend_back(seq):
        for pair in range(HEADS // 2):
            lanes = slice(pair * 128, (pair + 1) * 128)
            for block in range(blocks):
                cols = slice(block * HALF, (block + 1) * HALF)
                keys, values = [], []
                for odd in range(2):
                    head = pair * 2 + odd
                    own = slice(head * HEAD_DIM, (head + 1) * HEAD_DIM)
                    place = head * blocks + block
                    high = dots[seq, 2 * head : 2 * head + 1, cols]
                    rest = dots[seq, 2 * head + 1 : 2 * head + 2, cols]
                    extra = jnp.where(extra_row == 0, high, jnp.where(extra_row == 1, rest, 0.0))
                    extra = jnp.concatenate([extra, jnp.zeros((HEAD_DIM - 16, HALF), f32)], axis=0)
                    stack = [doT[seq, own, cols], extra.astype(bf16)]
                    if odd:
                        stack = stack[::-1]
                    stack = jnp.concatenate(stack, axis=0)
                    side = vtok[seq, cols, lanes] * keep[odd] + fill[odd]
                    for at in range(0, HALF, CHUNK):
                        part = slice(at, at + CHUNK)
                        grads = nn(side, stack[:, part])
                        dsT[odd, :, part] = (
                            pT[seq, place, :, part].astype(f32) * grads
                        ).astype(bf16)
                        yield
                    values.append(nn(pT[seq, place], dotok[seq, cols, lanes]))
                    yield
                    keys.append(nn(dsT[odd], qtok[seq, cols, lanes]))
                    yield
                    key_rows = slice(width + own.start, width + own.stop)
                    qkT[seq, own, cols] = (nn(qkT[seq, key_rows, cols], dsT[odd]) * scale).astype(
                        bf16
                    )
                    yield
                qtok[seq, cols, lanes] = jnp.where(low_half, keys[0], keys[1]).astype(bf16)
                dotok[seq, cols, lanes] = jnp.where(low_half, values[0], values[1]).astype(bf16)
        turned = xT[seq]
        gj[:, 0:width] += nt(turned, qkT[seq, 0:width, :])
        yield
        gj[:, width : 2 * width] += nn(turned, qtok[seq])
        yield
        gj[:, 2 * width : 3 * width] += nn(turned, dotok[seq])
        yield

    def together(*parts):
        parts = list(parts)
        while parts:
            for part in list(parts):
                if next(part, parts) is parts:
                    parts.remove(part)

    attend(0)
    together(dense(0))
    out_copy(0).start()

    def middle(seq, carry):
        attend(seq)

        @pl.when(seq >= 2)
        def _():
            out_copy(seq - 2).wait()

        together(dense(seq), attend_back(seq - 1))
        out_copy(seq).start()
        return carry

    lax.fori_loop(1, count, middle, 0)

    def pack(reduce, sources):
        for device in range(devices):
            outer = device // inners
            pieces = []
            for ref in sources:
                depth = ref.shape[0] // devices
                pieces += column_blocks(ref[device * depth : (device + 1) * depth, :])
            packed = reduce.packed
            packed[outer % 2, outer // 2, device % inners] = padded_rows(pieces, packed.shape[3])

    sum_a, sum_b = Reduce(peers, *reduce_a), Reduce(peers, *reduce_b)
    pack(sum_a, (go.at[0:width], ge.at[0:width], gr.at[0:inner_width]))
    sum_a.first()

    last = attend_back(count - 1)
    for k, step in enumerate(last):
        if k == 14:
            sum_a.second()
        if k == 30:
            sum_a.third()

    rows = [
        gj[width : width + 1, 0:width],
        gj[width : width + 1, 2 * width : 3 * width],
        go[width : width + 1, :],
        jnp.zeros((2, width), f32),
        gr[inner_width : inner_width + 1, :],
        jnp.zeros((1, width), f32),
        accc[0:1, :],
    ]
    missing = 128 - sum(row.shape[0] for row in rows)
    columns = jnp.concatenate(rows + [jnp.zeros((missing, width), f32)], axis=0).T
    lanes = lax.broadcasted_iota(jnp.int32, (width, 128), 1)
    for at, place in ((6, 0), (3, width), (4, 2 * width)):
        total = jnp.sum(accb[place : place + width, :], axis=1, keepdims=True)
        columns = jnp.where(lanes == at, total, columns)
    wide = jnp.broadcast_to(ge[width : width + 1, :], (128, inner_width)).T
    for first in range(2):
        item = [wide[k * share : (k + 1) * share] for k in range(first, 2 * devices, 2)]
        columns = jnp.where(lanes == VECTORS + first, jnp.concatenate(item, axis=0), columns)
    bcol[0] = columns
    pack(sum_b, (bcol.at[0], gj.at[0:width]))
    sum_b.first()

    def tg_copies(seq):
        slot = lax.rem(seq, 2)
        return [
            pltpu.make_async_copy(
                turn.at[slot * 2 + tile, pl.ds(0, length)],
                tg_hbm.at[seq, tile],
                tg_sem.at[slot, tile],
            )
            for tile in range(tiles)
        ]

    def inputs_back(seq, carry):
        @pl.when(seq >= 2)
        def _():
            for copy in tg_copies(seq - 2):
                copy.wait()

        slot = lax.rem(seq, 2)
        for at in range(0, length, CHUNK):
            rows = slice(at, at + CHUNK)
            across = nt(identity, qkT[seq, 0:width, rows]).astype(bf16)
            result = (
                nt(across, wj[:, 0:width])
                + nn(qtok[seq, rows, :], wjt[width : 2 * width, :])
                + nn(dotok[seq, rows, :], wjt[2 * width : 3 * width, :])
                + nt(identity, blow[seq, :, rows])
            )
            for tile in range(tiles):
                turn[slot * 2 + tile, rows, :] = result[:, tile * 128 : (tile + 1) * 128]
        for copy in tg_copies(seq):
            copy.start()

        @pl.when(seq == 0)
        def _():
            sum_b.second()

        if count > 2:

            @pl.when(seq == 2)
            def _():
                sum_b.third()

        return carry

    lax.fori_loop(0, count, inputs_back, 0)
    if count <= 2:
        sum_b.third()
    fin_a[...] = sum_a.finish()
    fin_b[...] = sum_b.finish()
    for seq in range(max(count - 2, 0), count):
        out_copy(seq).wait()
        for copy in tg_copies(seq):
            copy.wait()


def run_layer(outers, inners, tokens, segment_ids, padding_mask, cotangent, shards):
    count, length, width = tokens.shape
    devices = outers * inners
    share = width // devices
    inner_width = shards[2].shape[1]
    tiles = width // 128
    chips = outers // 2
    blocks = length // HALF

    def rows_of(items):
        return sum(item.size // 128 for item in items)

    held_a = rounded_up(share + rows_of(shards[:1]), 16)
    held_b = rounded_up(rows_of(shards[1:4]), 16)
    sends = gather_sends(outers, inners)
    dma = pltpu.SemaphoreType.DMA
    vmem = pltpu.VMEM
    shape = jax.ShapeDtypeStruct
    scratch = [vmem(item.shape, bf16) for item in shards]
    scratch += [
        vmem((2, length, width), bf16),
        vmem((2, length, width), bf16),
        vmem((count, length), jnp.int32),
        vmem((count, length), jnp.int32),
        vmem((width, 3 * width), bf16),
        vmem((width, width), bf16),
        vmem((width, inner_width), bf16),
        vmem((inner_width, width), bf16),
        vmem((3 * width, width), bf16),
        vmem((width, width), bf16),
        vmem((inner_width, width), bf16),
        vmem((width, inner_width), bf16),
        vmem((3 * width, 128), f32),
        vmem((inner_width, 128), f32),
        vmem((6, width, 128), f32),
        vmem((8, width), f32),
        vmem((2 * tiles, length + HALF, 128), f32),
        vmem((count, length, width), bf16),
        vmem((count, width + 16, length), bf16),
        vmem((count, width, length), bf16),
        vmem((count, length, 128), bf16),
        vmem((count, HEAD_DIM, length), bf16),
        vmem((count, 2 * width, length), bf16),
        vmem((width, length), bf16),
        vmem((count, length, width), bf16),
        vmem((HEADS, length, 128), bf16),
        vmem((count, length, width), bf16),
        vmem((count, HEADS * blocks, HALF, HALF), bf16),
        vmem((8, length), f32),
        vmem((width + 16, length), bf16),
        vmem((2, width, CHUNK), f32),
        vmem((2, 8, CHUNK), f32),
        vmem((inner_width + 16, length), bf16),
        vmem((width, length), bf16),
        vmem((inner_width, length), bf16),
        vmem((width + 16, length), bf16),
        vmem((count, width, length), bf16),
        vmem((2, inner_width, CHUNK), f32),
        vmem((2, HALF, HALF), bf16),
        vmem((count, 8, length), f32),
        vmem((width + 16, 3 * width), f32),
        vmem((width + 16, width), f32),
        vmem((width + 16, inner_width), f32),
        vmem((inner_width + 16, width), f32),
        vmem((3 * width, 128), f32),
        vmem((16, width), f32),
        vmem((2, chips, inners, held_a, 128), bf16),
        dma((sends,)),
        dma((2, chips, inners)),
        vmem((2, chips, inners, held_b, 128), bf16),
        dma((sends,)),
        dma((2, chips, inners)),
    ]
    scratch += reduce_scratch(outers, inners, held_b)
    scratch += reduce_scratch(outers, inners, held_a)
    scratch += [dma((len(shards) + 2,)), dma((2, 2)), dma((2,)), dma((2, tiles))]
    hbm = pl.BlockSpec(memory_space=pl.ANY)
    return pl.pallas_call(
        functools.partial(layer_kernel, outers, inners),
        in_specs=[pl.BlockSpec(memory_space=pltpu.SMEM)] + [hbm] * (4 + len(shards)),
        out_specs=[hbm, hbm] + [pl.BlockSpec(memory_space=pltpu.VMEM)] * 2,
        out_shape=[
            shape(tokens.shape, bf16),
            shape((count, tiles, length, 128), f32),
            shape((held_b, 128), f32),
            shape((held_a, 128), f32),
        ],
        scratch_shapes=scratch,
        compiler_params=pltpu.CompilerParams(
            collective_id=0, has_side_effects=True, vmem_limit_bytes=64 * 1024 * 1024 - 65536
        ),
        name="layer",
    )(segment_ids, tokens, cotangent, segment_ids, padding_mask, *shards)


def finish_kernel(seg_smem, out_turned, tg_turned, fin_a, fin_b, *refs):
    layer_out, tokens_grad, matrices, vectors = refs[0], refs[1], refs[2:6], refs[6:-1]
    turn = refs[-1]
    seq = pl.program_id(0)
    length, width = layer_out.shape[1], layer_out.shape[2]
    start = big_cell_start(seg_smem, seq, length)
    for tile in range(width // 128):
        lanes = slice(tile * 128, (tile + 1) * 128)
        for k, target in enumerate((layer_out, tokens_grad)):
            if k == 0:
                whole = out_turned[0, :, lanes].astype(f32)
            else:
                whole = tg_turned[0, tile]
            turn[k, tile, 0:HALF] = whole[length - HALF : length]
            turn[k, tile, HALF : HALF + length] = whole
            for at in range(0, length, CHUNK):
                piece = turn[k, tile, pl.ds(HALF - start + at, CHUNK), :]
                target[0, at : at + CHUNK, lanes] = piece.astype(target.dtype)

    @pl.when(seq == 0)
    def _():
        rows = vectors[0].shape[0]
        lines = fin_b[0:rows, :].T
        for at, ref in enumerate(vectors[:-1]):
            ref[...] = lines[at, :]
        vectors[-1][...] = jnp.concatenate([lines[VECTORS, :], lines[VECTORS + 1, :]])
        for source, at, targets in ((fin_b, rows, matrices[:1]), (fin_a, 0, matrices[1:])):
            for ref in targets:
                depth = ref.shape[0]
                for column in range(0, ref.shape[1], 128):
                    ref[:, column : column + 128] = source[at : at + depth, :]
                    at += depth


def finish(segment_ids, out_turned, tg_turned, fin_a, fin_b, shards):
    count, length, width = out_turned.shape
    tiles = width // 128

    def whole(shape):
        return pl.BlockSpec(shape, lambda i: (0,) * len(shape))

    per_seq = pl.BlockSpec((1, length, width), lambda i: (i, 0, 0))
    shape = jax.ShapeDtypeStruct
    return pl.pallas_call(
        finish_kernel,
        grid=(count,),
        in_specs=[
            pl.BlockSpec(memory_space=pltpu.SMEM),
            per_seq,
            pl.BlockSpec((1, tiles, length, 128), lambda i: (i, 0, 0, 0)),
            whole(fin_a.shape),
            whole(fin_b.shape),
        ],
        out_specs=[per_seq, per_seq] + [whole(item.shape) for item in shards],
        out_shape=[shape(out_turned.shape, bf16), shape(out_turned.shape, f32)]
        + [shape(item.shape, f32) for item in shards],
        scratch_shapes=[pltpu.VMEM((2, tiles, length + HALF, 128), f32)],
        compiler_params=pltpu.CompilerParams(
            dimension_semantics=("arbitrary",), vmem_limit_bytes=60 * 1024 * 1024
        ),
        name="finish",
    )(segment_ids, out_turned, tg_turned, fin_a, fin_b)


def on_device(
    outers,
    inners,
    tokens,
    segment_ids,
    padding_mask,
    joint_weight,
    query_bias,
    value_bias,
    output_weight,
    output_bias,
    first_gain,
    first_shift,
    expand_weight,
    expand_bias,
    reduce_weight,
    reduce_bias,
    second_gain,
    second_shift,
    cotangent,
):
    shards = (
        joint_weight,
        output_weight,
        expand_weight,
        reduce_weight,
        query_bias,
        value_bias,
        output_bias,
        first_gain,
        first_shift,
        reduce_bias,
        second_gain,
        second_shift,
        expand_bias,
    )
    turned = run_layer(outers, inners, tokens, segment_ids, padding_mask, cotangent, shards)
    layer_out, tokens_grad, *owned = finish(segment_ids, *turned, shards)
    gj, go, ge, gr, query, value, out, gain1, shift1, reduce, gain2, shift2, expand = owned
    return (
        layer_out,
        tokens_grad,
        gj,
        query,
        value,
        go,
        out,
        gain1,
        shift1,
        ge,
        expand,
        gr,
        reduce,
        gain2,
        shift2,
    )


def solution(mesh):
    rows = P(("outer", "inner"))
    rows2 = P(("outer", "inner"), None)
    rows3 = P(("outer", "inner"), None, None)
    weights = (rows2, rows, rows, rows2, rows, rows, rows, rows2, rows, rows2, rows, rows, rows)
    return jax.shard_map(
        functools.partial(on_device, mesh.shape["outer"], mesh.shape["inner"]),
        mesh=mesh,
        in_specs=(rows3, rows2, rows2) + weights + (rows3,),
        out_specs=(rows3, rows3) + weights,
        check_vma=False,
    )
```

```python
import functools
import math

import jax
import jax.numpy as jnp
from jax import lax
from jax.experimental import pallas as pl
from jax.experimental.pallas import tpu as pltpu
from jax.sharding import PartitionSpec as P

HEADS = 4
HEAD_DIM = 64
HALF = 512
CHUNK = 256
VECTORS = 8
MESH = pl.DeviceIdType.MESH

norm_epsilon = 1e-06
mask_step = -(2.0**100)
log2_e = math.log2(math.e)
gelu_a = math.sqrt(2.0 / math.pi)
gelu_b = 0.044715

f32 = jnp.float32
bf16 = jnp.bfloat16


def nn(left, right):
    return lax.dot_general(left, right, (((1,), (0,)), ((), ())), preferred_element_type=f32)


def nt(left, right):
    return lax.dot_general(left, right, (((1,), (1,)), ((), ())), preferred_element_type=f32)


def over_features(values):
    return jnp.sum(values, axis=0, keepdims=True)


def column_blocks(values):
    return [values[:, at : at + 128] for at in range(0, values.shape[1], 128)]


def padded_rows(pieces, rows):
    have = sum(piece.shape[0] for piece in pieces)
    if rows > have:
        pieces = pieces + [jnp.zeros((rows - have, 128), f32)]
    return jnp.concatenate(pieces, axis=0)


def rounded_up(amount, to):
    return (amount + to - 1) // to * to


def big_cell_start(seg_ref, seq, length):
    wanted = seg_ref[seq, HALF - 1]
    low = jnp.int32(0)
    step = HALF
    while step > 1:
        step //= 2
        probe = low + step
        low = jnp.where(seg_ref[seq, probe - 1] < wanted, probe, low)
    last = jnp.minimum(low + HALF - 1, length - 1)
    return jnp.where(seg_ref[seq, last] == wanted, low, HALF)


def copy_to(source, target, send, receive, outer, inner):
    return pltpu.make_async_remote_copy(
        src_ref=source,
        dst_ref=target,
        send_sem=send,
        recv_sem=receive,
        device_id=(outer, inner),
        device_id_type=MESH,
    )


class Peers:
    def __init__(self, outers, inners):
        self.outers, self.inners = outers, inners
        self.outer = lax.axis_index("outer")
        self.inner = lax.axis_index("inner")
        self.core = lax.rem(self.outer, 2)
        self.chip = lax.div(self.outer, 2)
        self.chips = outers // 2
        self.mate = self.chip * 2 + 1 - self.core

    def along_inner(self):
        return [lax.rem(self.inner + step, self.inners) for step in range(1, self.inners)]

    def along_chips(self):
        return [lax.rem(self.chip + step, self.chips) for step in range(1, self.chips)]

    def greet(self):
        barrier = pltpu.get_barrier_semaphore()
        others = [(self.outer, at) for at in self.along_inner()]
        others += [(at * 2 + self.core, self.inner) for at in self.along_chips()]
        others += [(self.mate, self.inner)]
        for other in others:
            pl.semaphore_signal(barrier, inc=1, device_id=other, device_id_type=MESH)
        pl.semaphore_wait(barrier, len(others))


class Gather:
    def __init__(self, peers, held, send, receive):
        self.peers, self.held, self.send, self.receive = peers, held, send, receive

    def one(self, at, spot, outer, inner):
        peers = self.peers
        block = self.held.at[peers.core, peers.chip, at]
        return copy_to(block, block, self.send.at[spot], self.receive.at[at], outer, inner)

    def block(self, core, chip, spot, signal, outer):
        peers = self.peers
        block = self.held.at[core, chip]
        signal = self.receive.at[peers.inners + signal]
        return copy_to(block, block, self.send.at[spot], signal, outer, peers.inner)

    def to_inner(self):
        peers = self.peers
        return [
            self.one(peers.inner, k, peers.outer, at) for k, at in enumerate(peers.along_inner())
        ]

    def to_chips(self):
        peers = self.peers
        return [
            self.block(peers.core, peers.chip, peers.inners + k, peers.chip, other * 2 + peers.core)
            for k, other in enumerate(peers.along_chips())
        ]

    def to_mate(self, k):
        peers = self.peers
        chip = ([peers.chip] + peers.along_chips())[k]
        spot = peers.inners + peers.chips + k
        return self.block(peers.core, chip, spot, peers.chips + chip, peers.mate)

    def first(self):
        for copy in self.to_inner():
            copy.start()

    def second(self):
        peers = self.peers
        for at in peers.along_inner():
            self.one(at, 0, peers.outer, peers.inner).wait_recv()
        for copy in self.to_chips() + [self.to_mate(0)]:
            copy.start()

    def third(self):
        peers = self.peers
        for k, other in enumerate(peers.along_chips()):
            self.block(peers.core, other, 0, other, peers.outer).wait_recv()
            self.to_mate(k + 1).start()

    def finish(self):
        peers = self.peers
        for chip in [peers.chip] + peers.along_chips():
            self.block(1 - peers.core, chip, 0, peers.chips + chip, peers.outer).wait_recv()
        for copy in (
            self.to_inner() + self.to_chips() + [self.to_mate(k) for k in range(peers.chips)]
        ):
            copy.wait_send()


class Reduce:
    def __init__(self, peers, packed, from_mate, mid, from_chips, last, from_inner, send, receive):
        self.peers, self.packed, self.from_mate = peers, packed, from_mate
        self.mid, self.from_chips, self.last = mid, from_chips, last
        self.from_inner, self.send, self.receive = from_inner, send, receive

    def to_mate(self):
        peers = self.peers
        return copy_to(
            self.packed.at[1 - peers.core],
            self.from_mate,
            self.send.at[0],
            self.receive.at[0],
            peers.mate,
            peers.inner,
        )

    def to_chips(self):
        peers = self.peers
        return [
            copy_to(
                self.mid.at[k],
                self.from_chips.at[k],
                self.send.at[1 + k],
                self.receive.at[1 + k],
                other * 2 + peers.core,
                peers.inner,
            )
            for k, other in enumerate(peers.along_chips())
        ]

    def to_inner(self):
        peers = self.peers
        return [
            copy_to(
                self.last.at[k],
                self.from_inner.at[k],
                self.send.at[peers.chips + k],
                self.receive.at[peers.chips + k],
                peers.outer,
                at,
            )
            for k, at in enumerate(peers.along_inner())
        ]

    def first(self):
        self.to_mate().start()

    def second(self):
        peers = self.peers
        self.to_mate().wait()
        for k, (other, copy) in enumerate(zip(peers.along_chips(), self.to_chips())):
            for at in range(peers.inners):
                total = self.packed[peers.core, other, at] + self.from_mate[other, at]
                self.mid[k, at] = total.astype(bf16)
            copy.start()

    def own(self, at):
        peers = self.peers
        total = self.packed[peers.core, peers.chip, at] + self.from_mate[peers.chip, at]
        for k in range(peers.chips - 1):
            total += self.from_chips[k, at].astype(f32)
        return total

    def third(self):
        for copy in self.to_chips():
            copy.wait()
        for k, (at, copy) in enumerate(zip(self.peers.along_inner(), self.to_inner())):
            self.last[k] = self.own(at).astype(bf16)
            copy.start()

    def finish(self):
        total = self.own(self.peers.inner)
        for k, copy in enumerate(self.to_inner()):
            copy.wait()
            total += self.from_inner[k].astype(f32)
        return total


def reduce_scratch(outers, inners, rows):
    chips = outers // 2
    return [
        pltpu.VMEM((2, chips, inners, rows, 128), f32),
        pltpu.VMEM((chips, inners, rows, 128), f32),
        pltpu.VMEM((max(chips - 1, 1), inners, rows, 128), bf16),
        pltpu.VMEM((max(chips - 1, 1), inners, rows, 128), bf16),
        pltpu.VMEM((inners - 1, rows, 128), bf16),
        pltpu.VMEM((inners - 1, rows, 128), bf16),
        pltpu.SemaphoreType.DMA((chips + inners,)),
        pltpu.SemaphoreType.DMA((chips + inners,)),
    ]


REDUCE_SCRATCH = 8


def unit(hidden, width):
    centred = hidden - over_features(hidden) * (1.0 / width)
    inverse = lax.rsqrt(over_features(centred * centred) * (1.0 / width) + norm_epsilon)
    return centred * inverse, inverse


def unit_back(inside, hat, inverse, width):
    return inverse * (
        inside
        - over_features(inside) * (1.0 / width)
        - hat * (over_features(inside * hat) * (1.0 / width))
    )


def layer_kernel(outers, inners, *refs):
    refs = list(refs)

    def grab(amount):
        taken = refs[:amount]
        del refs[:amount]
        return taken

    seg_smem, tokens_hbm, cot_hbm, seg_hbm, pad_hbm = grab(5)
    shard_hbm = grab(4 + VECTORS + 1)
    out_hbm, tg_hbm, fin_a, fin_b = grab(4)
    shards = grab(4 + VECTORS + 1)
    land_x, land_c, segv, padv = grab(4)
    wj, wo, we, wr, wjt, wot, wet, wrt, bj, be, bcol, vrow = grab(12)
    turn, xtok, xT, cT, codek, codeq = grab(6)
    qkT, vT, kaug, vtok, pT, inv, mixT = grab(7)
    hat1, rinv1, act, slow, igr, flow, blow, dgelu, dsT = grab(9)
    (dots,) = grab(1)
    doT = cT
    gj, go, ge, gr, accb, accc = grab(6)
    held_a, send_a, receive_a, held_b, send_b, receive_b = grab(6)
    reduce_a, reduce_b = grab(REDUCE_SCRATCH), grab(REDUCE_SCRATCH)
    shard_sem, land_sem, out_sem, tg_sem = grab(4)

    count, length, width = tokens_hbm.shape
    inner_width = we.shape[1]
    devices = outers * inners
    share = width // devices
    scale = HEAD_DIM**-0.5
    tiles = width // 128
    blocks = length // HALF
    peers = Peers(outers, inners)

    def land(seq):
        slot = lax.rem(seq, 2)
        return [
            pltpu.make_async_copy(tokens_hbm.at[seq], land_x.at[slot], land_sem.at[0, slot]),
            pltpu.make_async_copy(cot_hbm.at[seq], land_c.at[slot], land_sem.at[1, slot]),
        ]

    small = [
        pltpu.make_async_copy(source, target, shard_sem.at[k])
        for k, (source, target) in enumerate(
            zip(shard_hbm + [seg_hbm, pad_hbm], shards + [segv, padv])
        )
    ]
    for copy in small:
        copy.start()
    for seq in range(min(2, count)):
        for copy in land(jnp.int32(seq)):
            copy.start()
    for copy in small:
        copy.wait()

    lines = [ref[...].astype(f32).reshape(1, ref.shape[0]) for ref in shards[4:]]
    lines = lines[:-1] + [lines[-1][:, :share], lines[-1][:, share:]]
    lines.append(jnp.zeros((128 - len(lines), share), f32))
    pieces = [jnp.concatenate(lines, axis=0).T] + column_blocks(shards[0][...].astype(f32))
    here = (peers.core, peers.chip, peers.inner)
    held_a[here] = padded_rows(pieces, held_a.shape[3]).astype(bf16)
    pieces = []
    for ref in shards[1:4]:
        pieces += column_blocks(ref[...].astype(f32))
    held_b[here] = padded_rows(pieces, held_b.shape[3]).astype(bf16)
    peers.greet()
    gather_a = Gather(peers, held_a, send_a, receive_a)
    gather_b = Gather(peers, held_b, send_b, receive_b)
    gather_a.first()

    identity = (
        lax.broadcasted_iota(jnp.int32, (CHUNK, CHUNK), 0)
        == lax.broadcasted_iota(jnp.int32, (CHUNK, CHUNK), 1)
    )
    identity = identity.astype(f32).astype(bf16)

    for ref in [mixT, act, flow] + [xT.at[seq] for seq in range(count)]:
        ref[ref.shape[0] - 16 : ref.shape[0], :] = jnp.ones((16, length), bf16)
    for ref in (gj, go, ge, gr, accb, accc):
        ref[...] = jnp.zeros_like(ref)
    some_ones = jnp.ones((16, CHUNK), bf16)

    def chunks(body):
        def step(index, carry):
            body(index, pl.multiple_of(index * CHUNK, CHUNK))
            return carry

        lax.fori_loop(0, length // CHUNK, step, 0)

    def tokens_at(at, offset=0, size=CHUNK):
        return pl.ds(pl.multiple_of(at + offset, 128), size)

    def prepare(seq):
        for copy in land(seq):
            copy.wait()
        start = big_cell_start(seg_smem, seq, length)
        slot = lax.rem(seq, 2)

        def take(tile, at):
            return turn[tile, pl.ds(start + at, CHUNK), :]

        for k, source in enumerate((land_x, land_c)):

            def lay(index, at):
                for tile in range(tiles):
                    lanes = slice(tile * 128, (tile + 1) * 128)
                    piece = source[slot, tokens_at(at), lanes].astype(f32)
                    turn[2 * k + tile, tokens_at(at), :] = piece

                    @pl.when(index < HALF // CHUNK)
                    def _():
                        turn[2 * k + tile, tokens_at(at, length), :] = piece

            chunks(lay)

        def bring(index, at):
            for k, target in enumerate((xT, cT)):
                piece = jnp.concatenate([take(2 * k + tile, at) for tile in range(tiles)], axis=1)
                piece = piece.astype(bf16)
                if k == 0:
                    xtok[seq, tokens_at(at), :] = piece
                else:
                    accc[...] += nn(some_ones, piece)
                target[seq, 0:width, tokens_at(at)] = nt(identity, piece).astype(bf16)

        chunks(bring)

        @pl.when(seq + 2 < count)
        def _():
            for copy in land(seq + 2):
                copy.start()

        def mark(index, at):
            position = at + lax.broadcasted_iota(jnp.int32, (1, CHUNK), 1)
            code = lax.broadcasted_iota(jnp.int32, (8, CHUNK), 0)
            hidden = (padv[pl.ds(seq, 1), tokens_at(at)] != 1).astype(f32)
            same = (segv[pl.ds(seq, 1), tokens_at(at)] == code).astype(f32)
            parts_q = [1.0 - same]
            parts_k = [same * mask_step]
            for digit in ((position // 64) % 8, (position // 8) % 8, position % 8):
                equal = (digit == code).astype(f32)
                parts_q.append(1.0 - equal)
                parts_k.append(equal * hidden * mask_step)
            both = jnp.concatenate(parts_k + parts_q + parts_k + parts_q, axis=0).astype(bf16)
            flat = nt(identity, both)
            turn[0, tokens_at(at), :] = flat

            @pl.when(index < HALF // CHUNK)
            def _():
                turn[0, tokens_at(at, length), :] = flat

        chunks(mark)
        nothing = jnp.zeros((32, CHUNK), f32)

        def bring_marks(index, at):
            piece = take(0, at).astype(bf16)
            codek[seq, tokens_at(at), :] = piece
            across = nt(identity[0:128, 0:128], piece)
            codeq[seq, :, tokens_at(at)] = jnp.concatenate([across[32:64], nothing], axis=0).astype(
                bf16
            )

        chunks(bring_marks)

    def prepare_step(seq, carry):
        prepare(seq)

        @pl.when(seq == 0)
        def _():
            gather_a.second()
            gather_b.first()

        if count > 1:

            @pl.when(seq == 1)
            def _():
                gather_a.third()

        if count > 2:

            @pl.when(seq == 2)
            def _():
                gather_b.second()

        return carry

    lax.fori_loop(0, count, prepare_step, 0)
    if count <= 1:
        gather_a.third()
    if count <= 2:
        gather_b.second()
    gather_a.finish()
    gather_b.third()

    def stacked(held, at, depth):
        stack = []
        for device in range(devices):
            outer, inner = device // inners, device % inners
            stack.append(held[outer % 2, outer // 2, inner].astype(f32)[at : at + depth])
        return jnp.concatenate(stack, axis=0)

    columns = stacked(held_a, 0, share)
    def unpack(held, at, matrices):
        for straight, across, source in matrices:
            depth = source.shape[0]
            for column in range(0, straight.shape[1], 128):
                whole = stacked(held, at, depth)
                straight[:, column : column + 128] = whole.astype(bf16)
                if across is wjt and column < width:
                    whole = whole * scale
                across[column : column + 128, :] = whole.T.astype(bf16)
                at += depth

    unpack(held_a, share, ((wj, wjt, shards[0]),))

    def spread(at):
        return jnp.broadcast_to(columns[:, at : at + 1], (width, 128))

    bj[0:width, :] = spread(0) * scale
    bj[width : 2 * width, :] = jnp.zeros((width, 128), f32)
    bj[2 * width : 3 * width, :] = spread(1)
    for at in range(6):
        bcol[at, :, :] = spread(2 + at)
    halves = [spread(8), spread(9)]
    be[...] = jnp.concatenate(
        [halves[k % 2][k // 2 * share : (k // 2 + 1) * share] for k in range(2 * devices)], axis=0
    )
    vrow[...] = columns.T[0:8, :]

    lane = lax.broadcasted_iota(jnp.int32, (CHUNK, 128), 1)
    low_lanes = lane < HEAD_DIM
    halves = [slice(t, t + 128) for t in range(0, CHUNK, 128)]
    ones = jnp.ones((16, HALF), bf16)

    def add_sums(row, values):
        accb[row : row + values.shape[0], :] += values

    def out_copy(seq):
        slot = lax.rem(seq, 2)
        return pltpu.make_async_copy(land_x.at[slot], out_hbm.at[seq], out_sem.at[slot])

    def attend(seq):
        def project(index, at):
            made = nn(wjt[...], xT[seq, 0:width, tokens_at(at)])
            flat = nn(xtok[seq, tokens_at(at), :], wj[:, width : 3 * width])
            for half in halves:
                there = tokens_at(at, half.start, 128)
                low = (made[:, half] + bj[...]).astype(bf16)
                qkT[seq, :, there] = low[0 : 2 * width]
                vT[:, there] = low[2 * width : 3 * width]
            vtok[seq, tokens_at(at), :] = (flat[:, width : 2 * width] + vrow[1:2, :]).astype(bf16)
            codes = codek[seq, tokens_at(at), :].astype(f32)
            for head in range(HEADS):
                lanes = slice((head // 2) * 128, (head // 2 + 1) * 128)
                mine = low_lanes if head % 2 == 0 else ~low_lanes
                kaug[head, tokens_at(at), :] = jnp.where(mine, flat[:, lanes], codes).astype(bf16)

        chunks(project)

        def pair_of(index, carry):
            pair, block = index // blocks, lax.rem(index, blocks)
            first = block * HALF
            units = [(odd, at) for odd in range(2) for at in range(0, HALF, CHUNK)]

            def features(odd):
                return pl.ds(pl.multiple_of(pair * 128 + odd * HEAD_DIM, HEAD_DIM), HEAD_DIM)

            def scores_of(odd, at):
                there = tokens_at(first, at)
                parts = [qkT[seq, features(odd), there], codeq[seq, :, there]]
                if odd:
                    parts = parts[::-1]
                keys = kaug[pair * 2 + odd, tokens_at(first, 0, HALF), :]
                return nn(keys, jnp.concatenate(parts, axis=0))

            coming = scores_of(*units[0])
            for k, (odd, at) in enumerate(units):
                scores = coming
                if k + 1 < len(units):
                    coming = scores_of(*units[k + 1])
                place = (pair * 2 + odd) * blocks + block
                for tile in range(0, CHUNK, 128):
                    mine = scores[:, tile : tile + 128]
                    highest = jnp.max(mine, axis=0, keepdims=True)
                    pT[seq, place, :, at + tile : at + tile + 128] = jnp.exp2(
                        (mine - highest) * log2_e
                    ).astype(bf16)
                there = tokens_at(first, at)
                values = vT[features(odd), tokens_at(first, 0, HALF)]
                mixed = nn(
                    jnp.concatenate([values, ones], axis=0), pT[seq, place, :, at : at + CHUNK]
                )
                inverse = 1.0 / mixed[HEAD_DIM : HEAD_DIM + 1, :]
                inv[pair * 2 + odd, 0:1, there] = inverse
                mixT[features(odd), there] = (mixed[0:HEAD_DIM, :] * inverse).astype(bf16)
            return carry

        lax.fori_loop(0, HEADS // 2 * blocks, pair_of, 0)

    def dense(seq, at):
        slot = lax.rem(seq, 2)
        rows = tokens_at(at)
        branch = nn(wot[...], mixT[0:width, rows])
        firsts = []
        for half in halves:
            there = tokens_at(at, half.start, 128)
            hat, inverse = unit(
                xT[seq, 0:width, there].astype(f32) + branch[:, half] + bcol[0], width
            )
            hat1[:, half] = hat
            rinv1[0:1, half] = inverse
            first = hat * bcol[1] + bcol[2]
            flow[0:width, there] = first.astype(bf16)
            firsts.append(first)
            yield
        inner = nn(wet[...], flow[0:width, rows])
        for half in halves:
            there = tokens_at(at, half.start, 128)
            for r in range(0, inner_width, 32):
                u = inner[r : r + 32, half] + be[r : r + 32, :]
                square = u * u
                t = jnp.tanh(u * (gelu_a + (gelu_a * gelu_b) * square))
                h = 0.5 + 0.5 * t
                value = u * h
                act[r : r + 32, there] = value.astype(bf16)
                dgelu[r : r + 32, half] = h + value * (1.0 - h) * (
                    2.0 * gelu_a + (6.0 * gelu_a * gelu_b) * square
                )
                if r % 256 == 224:
                    yield
        second = nn(wrt[...], act[0:inner_width, rows])
        grads, results, gains = [], [], []
        for k, half in enumerate(halves):
            there = tokens_at(at, half.start, 128)
            hat, inverse = unit(firsts[k] + second[:, half] + bcol[3], width)
            results.append((hat * bcol[4] + bcol[5]).astype(bf16))
            upstream = cT[seq, :, there].astype(f32)
            gains.append(upstream * hat)
            back = unit_back(upstream * bcol[4], hat, inverse, width)
            slow[:, there] = back.astype(bf16)
            grads.append(back)
            yield
        add_sums(0, gains[0] + gains[1])
        active_grad = nn(wr[...], slow[:, rows])
        land_x[slot, rows, :] = nt(identity, jnp.concatenate(results, axis=1)).astype(bf16)
        for half in halves:
            there = tokens_at(at, half.start, 128)
            for r in range(0, inner_width, 32):
                igr[r : r + 32, there] = (
                    active_grad[r : r + 32, half] * dgelu[r : r + 32, half]
                ).astype(bf16)
            yield
        deeper = nn(we[...], igr[:, rows])
        gains, shifts = [], []
        for k, half in enumerate(halves):
            there = tokens_at(at, half.start, 128)
            first_grad = grads[k] + deeper[:, half]
            hat = hat1[:, half]
            gains.append(first_grad * hat)
            shifts.append(first_grad)
            back = unit_back(first_grad * bcol[1], hat, rinv1[0:1, half], width)
            blow[seq, :, there] = back.astype(bf16)
            yield
        add_sums(width, gains[0] + gains[1])
        add_sums(2 * width, shifts[0] + shifts[1])
        grown = nn(wo[...], blow[seq, :, rows]).astype(bf16).astype(f32)
        for head in range(HEADS):
            own = slice(head * HEAD_DIM, (head + 1) * HEAD_DIM)
            piece = grown[own, :] * inv[head, 0:1, rows]
            total = over_features(piece * mixT[own, rows].astype(f32))
            high = total.astype(bf16).astype(f32)
            dots[seq, head, 0:1, rows] = high
            dots[seq, head, 1:2, rows] = total - high
            doT[seq, own, rows] = piece.astype(bf16)
        yield

    def weight_sums(seq):
        gr[...] += nt(act[...], slow[...])
        ge[...] += nt(flow[...], igr[...])
        go[...] += nt(mixT[...], blow[seq])

    low_half = lax.broadcasted_iota(jnp.int32, (HALF, 128), 1) < HEAD_DIM
    keep = [low_half.astype(f32).astype(bf16), (~low_half).astype(f32).astype(bf16)]
    fill = [-keep[1], -keep[0]]
    extra_row = lax.broadcasted_iota(jnp.int32, (16, HALF), 0)

    def attend_back(seq, index):
        pair, block = index // blocks, lax.rem(index, blocks)
        first = block * HALF
        lanes = pl.ds(pl.multiple_of(pair * 128, 128), 128)
        cols = tokens_at(first, 0, HALF)
        for odd in range(2):
            head = pair * 2 + odd
            own = pl.ds(pl.multiple_of(pair * 128 + odd * HEAD_DIM, HEAD_DIM), HEAD_DIM)
            key_rows = pl.ds(
                pl.multiple_of(width + pair * 128 + odd * HEAD_DIM, HEAD_DIM), HEAD_DIM
            )
            place = head * blocks + block
            high, rest = dots[seq, head, 0:1, cols], dots[seq, head, 1:2, cols]
            extra = jnp.where(extra_row == 0, high, jnp.where(extra_row == 1, rest, 0.0))
            extra = jnp.concatenate([extra, jnp.zeros((HEAD_DIM - 16, HALF), f32)], axis=0)
            grown = doT[seq, own, cols]
            stack = [grown, extra.astype(bf16)]
            if odd:
                stack = stack[::-1]
            stack = jnp.concatenate(stack, axis=0)
            side = vtok[seq, cols, lanes] * keep[odd] + fill[odd]
            for at in range(0, HALF, CHUNK):
                part = slice(at, at + CHUNK)
                grads = nn(side, stack[:, part])
                dsT[odd, :, part] = (pT[seq, place, :, part].astype(f32) * grads).astype(bf16)
                yield
            value_grad = nt(grown, pT[seq, place]).astype(bf16)
            yield
            key_grad = nt(qkT[seq, own, cols], dsT[odd]).astype(bf16)
            yield
            query_grad = (nn(qkT[seq, key_rows, cols], dsT[odd]) * scale).astype(bf16)
            yield
            doT[seq, own, cols] = value_grad
            qkT[seq, key_rows, cols] = key_grad
            qkT[seq, own, cols] = query_grad

    def joint_sums(seq):
        turned = xT[seq]
        gj[:, 0 : 2 * width] += nt(turned, qkT[seq])
        gj[:, 2 * width : 3 * width] += nt(turned, doT[seq])

    def together(*parts):
        parts = list(parts)
        while parts:
            for part in list(parts):
                if next(part, parts) is parts:
                    parts.remove(part)

    attend(0)
    gather_b.finish()
    unpack(
        held_b, 0, ((wo, wot, shards[1]), (we, wet, shards[2]), (wr, wrt, shards[3]))
    )
    chunks(lambda index, at: together(dense(0, at)))
    weight_sums(0)
    out_copy(0).start()

    def middle(seq, carry):
        attend(seq)

        @pl.when(seq >= 2)
        def _():
            out_copy(seq - 2).wait()

        chunks(lambda index, at: together(dense(seq, at), attend_back(seq - 1, index)))
        weight_sums(seq)
        joint_sums(seq - 1)
        out_copy(seq).start()
        return carry

    lax.fori_loop(1, count, middle, 0)

    def pack(reduce, sources):
        for device in range(devices):
            outer = device // inners
            pieces = []
            for ref in sources:
                depth = ref.shape[0] // devices
                pieces += column_blocks(ref[device * depth : (device + 1) * depth, :])
            packed = reduce.packed
            packed[outer % 2, outer // 2, device % inners] = padded_rows(pieces, packed.shape[3])

    sum_a, sum_b = Reduce(peers, *reduce_a), Reduce(peers, *reduce_b)
    pack(sum_a, (go.at[0:width], ge.at[0:width], gr.at[0:inner_width]))
    sum_a.first()

    def last(index, carry):
        together(attend_back(count - 1, index))

        @pl.when(index == 0)
        def _():
            sum_a.second()

        @pl.when(index == HEADS // 2 * blocks - 1)
        def _():
            sum_a.third()

        return carry

    lax.fori_loop(0, HEADS // 2 * blocks, last, 0)
    joint_sums(count - 1)
    rows = [
        gj[width : width + 1, 0:width],
        gj[width : width + 1, 2 * width : 3 * width],
        go[width : width + 1, :],
        jnp.zeros((2, width), f32),
        gr[inner_width : inner_width + 1, :],
        jnp.zeros((1, width), f32),
        accc[0:1, :],
    ]
    missing = 128 - sum(row.shape[0] for row in rows)
    columns = jnp.concatenate(rows + [jnp.zeros((missing, width), f32)], axis=0).T
    lanes = lax.broadcasted_iota(jnp.int32, (width, 128), 1)
    for at, place in ((6, 0), (3, width), (4, 2 * width)):
        total = jnp.sum(accb[place : place + width, :], axis=1, keepdims=True)
        columns = jnp.where(lanes == at, total, columns)
    wide = jnp.broadcast_to(ge[width : width + 1, :], (128, inner_width)).T
    for first in range(2):
        item = [wide[k * share : (k + 1) * share] for k in range(first, 2 * devices, 2)]
        columns = jnp.where(lanes == VECTORS + first, jnp.concatenate(item, axis=0), columns)
    bcol[0] = columns
    pack(sum_b, (bcol.at[0], gj.at[0:width]))
    sum_b.first()

    def tg_copies(seq):
        slot = lax.rem(seq, 2)
        return [
            pltpu.make_async_copy(
                turn.at[slot * 2 + tile, pl.ds(0, length)],
                tg_hbm.at[seq, tile],
                tg_sem.at[slot, tile],
            )
            for tile in range(tiles)
        ]

    def inputs_back(seq, carry):
        @pl.when(seq >= 2)
        def _():
            for copy in tg_copies(seq - 2):
                copy.wait()

        slot = lax.rem(seq, 2)

        def one(index, at):
            rows = tokens_at(at)
            result = (
                nn(wj[:, 0 : 2 * width], qkT[seq, :, rows])
                + nn(wj[:, 2 * width : 3 * width], doT[seq, :, rows])
                + blow[seq, :, rows].astype(f32)
            ).T
            for tile in range(tiles):
                turn[slot * 2 + tile, rows, :] = result[:, tile * 128 : (tile + 1) * 128]

        chunks(one)
        for copy in tg_copies(seq):
            copy.start()

        @pl.when(seq == 0)
        def _():
            sum_b.second()

        if count > 2:

            @pl.when(seq == 2)
            def _():
                sum_b.third()

        return carry

    lax.fori_loop(0, count, inputs_back, 0)
    if count <= 2:
        sum_b.third()
    fin_a[...] = sum_a.finish()
    fin_b[...] = sum_b.finish()
    for seq in range(max(count - 2, 0), count):
        out_copy(seq).wait()
        for copy in tg_copies(seq):
            copy.wait()


def run_layer(outers, inners, tokens, segment_ids, padding_mask, cotangent, shards):
    count, length, width = tokens.shape
    devices = outers * inners
    share = width // devices
    inner_width = shards[2].shape[1]
    tiles = width // 128
    chips = outers // 2
    blocks = length // HALF

    def rows_of(items):
        return sum(item.size // 128 for item in items)

    held_a = rounded_up(share + rows_of(shards[:1]), 16)
    held_b = rounded_up(rows_of(shards[1:4]), 16)
    dma = pltpu.SemaphoreType.DMA
    vmem = pltpu.VMEM
    shape = jax.ShapeDtypeStruct
    scratch = [vmem(item.shape, bf16) for item in shards]
    scratch += [
        vmem((2, length, width), bf16),
        vmem((2, length, width), bf16),
        vmem((count, length), jnp.int32),
        vmem((count, length), jnp.int32),
        vmem((width, 3 * width), bf16),
        vmem((width, width), bf16),
        vmem((width, inner_width), bf16),
        vmem((inner_width, width), bf16),
        vmem((3 * width, width), bf16),
        vmem((width, width), bf16),
        vmem((inner_width, width), bf16),
        vmem((width, inner_width), bf16),
        vmem((3 * width, 128), f32),
        vmem((inner_width, 128), f32),
        vmem((6, width, 128), f32),
        vmem((8, width), f32),
        vmem((2 * tiles, length + HALF, 128), f32),
        vmem((count, length, width), bf16),
        vmem((count, width + 16, length), bf16),
        vmem((count, width, length), bf16),
        vmem((count, length, 128), bf16),
        vmem((count, HEAD_DIM, length), bf16),
        vmem((count, 2 * width, length), bf16),
        vmem((width, length), bf16),
        vmem((HEADS, length, 128), bf16),
        vmem((count, length, width), bf16),
        vmem((count, HEADS * blocks, HALF, HALF), bf16),
        vmem((HEADS, 8, length), f32),
        vmem((width + 16, length), bf16),
        vmem((width, CHUNK), f32),
        vmem((8, CHUNK), f32),
        vmem((inner_width + 16, length), bf16),
        vmem((width, length), bf16),
        vmem((inner_width, length), bf16),
        vmem((width + 16, length), bf16),
        vmem((count, width, length), bf16),
        vmem((inner_width, CHUNK), f32),
        vmem((2, HALF, HALF), bf16),
        vmem((count, HEADS, 8, length), f32),
        vmem((width + 16, 3 * width), f32),
        vmem((width + 16, width), f32),
        vmem((width + 16, inner_width), f32),
        vmem((inner_width + 16, width), f32),
        vmem((3 * width, 128), f32),
        vmem((16, width), f32),
        vmem((2, chips, inners, held_a, 128), bf16),
        dma((inners + 2 * chips,)),
        dma((inners + 2 * chips,)),
        vmem((2, chips, inners, held_b, 128), bf16),
        dma((inners + 2 * chips,)),
        dma((inners + 2 * chips,)),
    ]
    scratch += reduce_scratch(outers, inners, held_b)
    scratch += reduce_scratch(outers, inners, held_a)
    scratch += [dma((len(shards) + 2,)), dma((2, 2)), dma((2,)), dma((2, tiles))]
    hbm = pl.BlockSpec(memory_space=pl.ANY)
    return pl.pallas_call(
        functools.partial(layer_kernel, outers, inners),
        in_specs=[pl.BlockSpec(memory_space=pltpu.SMEM)] + [hbm] * (4 + len(shards)),
        out_specs=[hbm, hbm] + [pl.BlockSpec(memory_space=pltpu.VMEM)] * 2,
        out_shape=[
            shape(tokens.shape, bf16),
            shape((count, tiles, length, 128), f32),
            shape((held_b, 128), f32),
            shape((held_a, 128), f32),
        ],
        scratch_shapes=scratch,
        compiler_params=pltpu.CompilerParams(
            collective_id=0, has_side_effects=True, vmem_limit_bytes=64 * 1024 * 1024 - 65536
        ),
        name="layer",
    )(segment_ids, tokens, cotangent, segment_ids, padding_mask, *shards)


def finish_kernel(seg_smem, out_turned, tg_turned, fin_a, fin_b, *refs):
    layer_out, tokens_grad, matrices, vectors = refs[0], refs[1], refs[2:6], refs[6:-2]
    plain, bent = refs[-2:]
    seq = pl.program_id(0)
    length, width = layer_out.shape[1], layer_out.shape[2]
    start = big_cell_start(seg_smem, seq, length)
    tiles = width // 128
    for tile in range(tiles):
        lanes = slice(tile * 128, (tile + 1) * 128)
        plain[tile] = out_turned[0, :, lanes].astype(f32)
        for k, source in enumerate((plain.at[tile], tg_turned.at[0, tile])):
            bent[k, tile, 0:CHUNK] = source[length - CHUNK : length]
            bent[k, tile, CHUNK : 2 * CHUNK] = source[0:CHUNK]
    for at in range(0, length, CHUNK):
        begin = lax.rem(length + at - start, length)

        def give(pieces):
            for tile in range(tiles):
                lanes = slice(tile * 128, (tile + 1) * 128)
                for k, target in enumerate((layer_out, tokens_grad)):
                    piece = pieces(k, tile)
                    target[0, at : at + CHUNK, lanes] = piece.astype(target.dtype)

        @pl.when(begin <= length - CHUNK)
        def _():
            whole = [lambda tile: plain.at[tile], lambda tile: tg_turned.at[0, tile]]
            give(lambda k, tile: whole[k](tile)[pl.ds(begin, CHUNK), :])

        @pl.when(begin > length - CHUNK)
        def _():
            give(lambda k, tile: bent[k, tile, pl.ds(begin - (length - CHUNK), CHUNK), :])

    @pl.when(seq == 0)
    def _():
        rows = vectors[0].shape[0]
        lines = fin_b[0:rows, :].T
        for at, ref in enumerate(vectors[:-1]):
            ref[...] = lines[at, :]
        vectors[-1][...] = jnp.concatenate([lines[VECTORS, :], lines[VECTORS + 1, :]])
        for source, at, targets in ((fin_b, rows, matrices[:1]), (fin_a, 0, matrices[1:])):
            for ref in targets:
                depth = ref.shape[0]
                for column in range(0, ref.shape[1], 128):
                    ref[:, column : column + 128] = source[at : at + depth, :]
                    at += depth


def finish(segment_ids, out_turned, tg_turned, fin_a, fin_b, shards):
    count, length, width = out_turned.shape
    tiles = width // 128

    def whole(shape):
        return pl.BlockSpec(shape, lambda i: (0,) * len(shape))

    per_seq = pl.BlockSpec((1, length, width), lambda i: (i, 0, 0))
    shape = jax.ShapeDtypeStruct
    return pl.pallas_call(
        finish_kernel,
        grid=(count,),
        in_specs=[
            pl.BlockSpec(memory_space=pltpu.SMEM),
            per_seq,
            pl.BlockSpec((1, tiles, length, 128), lambda i: (i, 0, 0, 0)),
            whole(fin_a.shape),
            whole(fin_b.shape),
        ],
        out_specs=[per_seq, per_seq] + [whole(item.shape) for item in shards],
        out_shape=[shape(out_turned.shape, bf16), shape(out_turned.shape, f32)]
        + [shape(item.shape, f32) for item in shards],
        scratch_shapes=[
            pltpu.VMEM((tiles, length, 128), f32),
            pltpu.VMEM((2, tiles, 2 * CHUNK, 128), f32),
        ],
        compiler_params=pltpu.CompilerParams(
            dimension_semantics=("arbitrary",), vmem_limit_bytes=60 * 1024 * 1024
        ),
        name="finish",
    )(segment_ids, out_turned, tg_turned, fin_a, fin_b)


def on_device(
    outers,
    inners,
    tokens,
    segment_ids,
    padding_mask,
    joint_weight,
    query_bias,
    value_bias,
    output_weight,
    output_bias,
    first_gain,
    first_shift,
    expand_weight,
    expand_bias,
    reduce_weight,
    reduce_bias,
    second_gain,
    second_shift,
    cotangent,
):
    shards = (
        joint_weight,
        output_weight,
        expand_weight,
        reduce_weight,
        query_bias,
        value_bias,
        output_bias,
        first_gain,
        first_shift,
        reduce_bias,
        second_gain,
        second_shift,
        expand_bias,
    )
    turned = run_layer(outers, inners, tokens, segment_ids, padding_mask, cotangent, shards)
    layer_out, tokens_grad, *owned = finish(segment_ids, *turned, shards)
    gj, go, ge, gr, query, value, out, gain1, shift1, reduce, gain2, shift2, expand = owned
    return (
        layer_out,
        tokens_grad,
        gj,
        query,
        value,
        go,
        out,
        gain1,
        shift1,
        ge,
        expand,
        gr,
        reduce,
        gain2,
        shift2,
    )


def solution(mesh):
    rows = P(("outer", "inner"))
    rows2 = P(("outer", "inner"), None)
    rows3 = P(("outer", "inner"), None, None)
    weights = (rows2, rows, rows, rows2, rows, rows, rows, rows2, rows, rows2, rows, rows, rows)
    return jax.shard_map(
        functools.partial(on_device, mesh.shape["outer"], mesh.shape["inner"]),
        mesh=mesh,
        in_specs=(rows3, rows2, rows2) + weights + (rows3,),
        out_specs=(rows3, rows3) + weights,
        check_vma=False,
    )
```

```python
import functools
import math

import jax
import jax.numpy as jnp
from jax import lax
from jax.experimental import pallas as pl
from jax.experimental.pallas import tpu as pltpu
from jax.sharding import PartitionSpec as P

HEADS = 4
HEAD_DIM = 64
HALF = 512
CHUNK = 256
VECTORS = 8
MESH = pl.DeviceIdType.MESH

norm_epsilon = 1e-06
mask_step = -(2.0**100)
log2_e = math.log2(math.e)
gelu_a = math.sqrt(2.0 / math.pi)
gelu_b = 0.044715

f32 = jnp.float32
bf16 = jnp.bfloat16


def nn(left, right):
    return lax.dot_general(left, right, (((1,), (0,)), ((), ())), preferred_element_type=f32)


def nt(left, right):
    return lax.dot_general(left, right, (((1,), (1,)), ((), ())), preferred_element_type=f32)


def over_features(values):
    return jnp.sum(values, axis=0, keepdims=True)


def column_blocks(values):
    return [values[:, at : at + 128] for at in range(0, values.shape[1], 128)]


def padded_rows(pieces, rows):
    have = sum(piece.shape[0] for piece in pieces)
    if rows > have:
        pieces = pieces + [jnp.zeros((rows - have, 128), f32)]
    return jnp.concatenate(pieces, axis=0)


def rounded_up(amount, to):
    return (amount + to - 1) // to * to


def big_cell_start(seg_ref, seq, length):
    wanted = seg_ref[seq, HALF - 1]
    low = jnp.int32(0)
    step = HALF
    while step > 1:
        step //= 2
        probe = low + step
        low = jnp.where(seg_ref[seq, probe - 1] < wanted, probe, low)
    last = jnp.minimum(low + HALF - 1, length - 1)
    return jnp.where(seg_ref[seq, last] == wanted, low, HALF)


def copy_to(source, target, send, receive, outer, inner):
    return pltpu.make_async_remote_copy(
        src_ref=source,
        dst_ref=target,
        send_sem=send,
        recv_sem=receive,
        device_id=(outer, inner),
        device_id_type=MESH,
    )


class Peers:
    def __init__(self, outers, inners):
        self.outers, self.inners = outers, inners
        self.outer = lax.axis_index("outer")
        self.inner = lax.axis_index("inner")
        self.core = lax.rem(self.outer, 2)
        self.chip = lax.div(self.outer, 2)
        self.chips = outers // 2
        self.mate = self.chip * 2 + 1 - self.core

    def along_inner(self):
        return [lax.rem(self.inner + step, self.inners) for step in range(1, self.inners)]

    def along_chips(self):
        return [lax.rem(self.chip + step, self.chips) for step in range(1, self.chips)]

    def greet(self):
        barrier = pltpu.get_barrier_semaphore()
        others = [(self.outer, at) for at in self.along_inner()]
        others += [(at * 2 + self.core, self.inner) for at in self.along_chips()]
        others += [(self.mate, self.inner)]
        for other in others:
            pl.semaphore_signal(barrier, inc=1, device_id=other, device_id_type=MESH)
        pl.semaphore_wait(barrier, len(others))


class Gather:
    def __init__(self, peers, held, send, receive):
        self.peers, self.held, self.send, self.receive = peers, held, send, receive

    def one(self, at, spot, outer, inner):
        peers = self.peers
        block = self.held.at[peers.core, peers.chip, at]
        return copy_to(block, block, self.send.at[spot], self.receive.at[at], outer, inner)

    def block(self, core, chip, spot, signal, outer):
        peers = self.peers
        block = self.held.at[core, chip]
        signal = self.receive.at[peers.inners + signal]
        return copy_to(block, block, self.send.at[spot], signal, outer, peers.inner)

    def to_inner(self):
        peers = self.peers
        return [
            self.one(peers.inner, k, peers.outer, at) for k, at in enumerate(peers.along_inner())
        ]

    def to_chips(self):
        peers = self.peers
        return [
            self.block(peers.core, peers.chip, peers.inners + k, peers.chip, other * 2 + peers.core)
            for k, other in enumerate(peers.along_chips())
        ]

    def to_mate(self, k):
        peers = self.peers
        chip = ([peers.chip] + peers.along_chips())[k]
        spot = peers.inners + peers.chips + k
        return self.block(peers.core, chip, spot, peers.chips + chip, peers.mate)

    def first(self):
        for copy in self.to_inner():
            copy.start()

    def second(self):
        peers = self.peers
        for at in peers.along_inner():
            self.one(at, 0, peers.outer, peers.inner).wait_recv()
        for copy in self.to_chips() + [self.to_mate(0)]:
            copy.start()

    def third(self):
        peers = self.peers
        for k, other in enumerate(peers.along_chips()):
            self.block(peers.core, other, 0, other, peers.outer).wait_recv()
            self.to_mate(k + 1).start()

    def finish(self):
        peers = self.peers
        for chip in [peers.chip] + peers.along_chips():
            self.block(1 - peers.core, chip, 0, peers.chips + chip, peers.outer).wait_recv()
        for copy in (
            self.to_inner() + self.to_chips() + [self.to_mate(k) for k in range(peers.chips)]
        ):
            copy.wait_send()


class Reduce:
    def __init__(self, peers, packed, from_mate, mid, from_chips, last, from_inner, send, receive):
        self.peers, self.packed, self.from_mate = peers, packed, from_mate
        self.mid, self.from_chips, self.last = mid, from_chips, last
        self.from_inner, self.send, self.receive = from_inner, send, receive

    def to_mate(self):
        peers = self.peers
        return copy_to(
            self.packed.at[1 - peers.core],
            self.from_mate,
            self.send.at[0],
            self.receive.at[0],
            peers.mate,
            peers.inner,
        )

    def to_chips(self):
        peers = self.peers
        return [
            copy_to(
                self.mid.at[k],
                self.from_chips.at[k],
                self.send.at[1 + k],
                self.receive.at[1 + k],
                other * 2 + peers.core,
                peers.inner,
            )
            for k, other in enumerate(peers.along_chips())
        ]

    def to_inner(self):
        peers = self.peers
        return [
            copy_to(
                self.last.at[k],
                self.from_inner.at[k],
                self.send.at[peers.chips + k],
                self.receive.at[peers.chips + k],
                peers.outer,
                at,
            )
            for k, at in enumerate(peers.along_inner())
        ]

    def first(self):
        self.to_mate().start()

    def second(self):
        peers = self.peers
        self.to_mate().wait()
        for k, (other, copy) in enumerate(zip(peers.along_chips(), self.to_chips())):
            for at in range(peers.inners):
                total = self.packed[peers.core, other, at] + self.from_mate[other, at]
                self.mid[k, at] = total.astype(bf16)
            copy.start()

    def own(self, at):
        peers = self.peers
        total = self.packed[peers.core, peers.chip, at] + self.from_mate[peers.chip, at]
        for k in range(peers.chips - 1):
            total += self.from_chips[k, at].astype(f32)
        return total

    def third(self):
        for copy in self.to_chips():
            copy.wait()
        for k, (at, copy) in enumerate(zip(self.peers.along_inner(), self.to_inner())):
            self.last[k] = self.own(at).astype(bf16)
            copy.start()

    def finish(self):
        total = self.own(self.peers.inner)
        for k, copy in enumerate(self.to_inner()):
            copy.wait()
            total += self.from_inner[k].astype(f32)
        return total


def reduce_scratch(outers, inners, rows):
    chips = outers // 2
    return [
        pltpu.VMEM((2, chips, inners, rows, 128), f32),
        pltpu.VMEM((chips, inners, rows, 128), f32),
        pltpu.VMEM((max(chips - 1, 1), inners, rows, 128), bf16),
        pltpu.VMEM((max(chips - 1, 1), inners, rows, 128), bf16),
        pltpu.VMEM((inners - 1, rows, 128), bf16),
        pltpu.VMEM((inners - 1, rows, 128), bf16),
        pltpu.SemaphoreType.DMA((chips + inners,)),
        pltpu.SemaphoreType.DMA((chips + inners,)),
    ]


REDUCE_SCRATCH = 8


def unit(hidden, width):
    centred = hidden - over_features(hidden) * (1.0 / width)
    inverse = lax.rsqrt(over_features(centred * centred) * (1.0 / width) + norm_epsilon)
    return centred * inverse, inverse


def unit_back(inside, hat, inverse, width):
    return inverse * (
        inside
        - over_features(inside) * (1.0 / width)
        - hat * (over_features(inside * hat) * (1.0 / width))
    )


def layer_kernel(outers, inners, *refs):
    refs = list(refs)

    def grab(amount):
        taken = refs[:amount]
        del refs[:amount]
        return taken

    seg_smem, tokens_hbm, cot_hbm, seg_hbm, pad_hbm = grab(5)
    shard_hbm = grab(4 + VECTORS + 1)
    out_hbm, tg_hbm, fin_a, fin_b = grab(4)
    shards = grab(4 + VECTORS + 1)
    land_x, land_c, segv, padv = grab(4)
    wj, wo, we, wr, wjt, wot, wet, wrt, bj, be, bcol, vrow = grab(12)
    turn, xtok, xT, cT, codek, codeq = grab(6)
    qkT, vT, kaug, vtok, pT, inv, mixT = grab(7)
    hat1, rinv1, act, slow, igr, flow, blow, dgelu, dsT = grab(9)
    (dots,) = grab(1)
    doT = cT
    gj, go, ge, gr, accb, accc = grab(6)
    held_a, send_a, receive_a, held_b, send_b, receive_b = grab(6)
    reduce_a, reduce_b = grab(REDUCE_SCRATCH), grab(REDUCE_SCRATCH)
    shard_sem, land_sem, out_sem, tg_sem = grab(4)

    count, length, width = tokens_hbm.shape
    inner_width = we.shape[1]
    devices = outers * inners
    share = width // devices
    scale = HEAD_DIM**-0.5
    tiles = width // 128
    blocks = length // HALF
    peers = Peers(outers, inners)

    def land(seq):
        slot = lax.rem(seq, 2)
        return [
            pltpu.make_async_copy(tokens_hbm.at[seq], land_x.at[slot], land_sem.at[0, slot]),
            pltpu.make_async_copy(cot_hbm.at[seq], land_c.at[slot], land_sem.at[1, slot]),
        ]

    small = [
        pltpu.make_async_copy(source, target, shard_sem.at[k])
        for k, (source, target) in enumerate(
            zip(shard_hbm + [seg_hbm, pad_hbm], shards + [segv, padv])
        )
    ]
    for copy in small:
        copy.start()
    for seq in range(min(2, count)):
        for copy in land(jnp.int32(seq)):
            copy.start()
    for copy in small:
        copy.wait()

    lines = [ref[...].astype(f32).reshape(1, ref.shape[0]) for ref in shards[4:]]
    lines = lines[:-1] + [lines[-1][:, :share], lines[-1][:, share:]]
    lines.append(jnp.zeros((128 - len(lines), share), f32))
    pieces = [jnp.concatenate(lines, axis=0).T] + column_blocks(shards[0][...].astype(f32))
    here = (peers.core, peers.chip, peers.inner)
    held_a[here] = padded_rows(pieces, held_a.shape[3]).astype(bf16)
    pieces = []
    for ref in shards[1:4]:
        pieces += column_blocks(ref[...].astype(f32))
    held_b[here] = padded_rows(pieces, held_b.shape[3]).astype(bf16)
    peers.greet()
    gather_a = Gather(peers, held_a, send_a, receive_a)
    gather_b = Gather(peers, held_b, send_b, receive_b)
    gather_a.first()

    identity = (
        lax.broadcasted_iota(jnp.int32, (CHUNK, CHUNK), 0)
        == lax.broadcasted_iota(jnp.int32, (CHUNK, CHUNK), 1)
    )
    identity = identity.astype(f32).astype(bf16)

    for ref in [mixT, act, flow] + [xT.at[seq] for seq in range(count)]:
        ref[ref.shape[0] - 16 : ref.shape[0], :] = jnp.ones((16, length), bf16)
    for ref in (gj, go, ge, gr, accb, accc):
        ref[...] = jnp.zeros_like(ref)
    some_ones = jnp.ones((16, CHUNK), bf16)

    def chunks(body):
        for index in range(length // CHUNK):
            body(index, index * CHUNK)

    def tokens_at(at, offset=0, size=CHUNK):
        return slice(at + offset, at + offset + size)

    def prepare(seq):
        for copy in land(seq):
            copy.wait()
        start = big_cell_start(seg_smem, seq, length)
        slot = lax.rem(seq, 2)

        def take(tile, at):
            return turn[tile, pl.ds(start + at, CHUNK), :]

        for k, source in enumerate((land_x, land_c)):

            def lay(index, at):
                for tile in range(tiles):
                    lanes = slice(tile * 128, (tile + 1) * 128)
                    piece = source[slot, tokens_at(at), lanes].astype(f32)
                    turn[2 * k + tile, tokens_at(at), :] = piece
                    if index < HALF // CHUNK:
                        turn[2 * k + tile, tokens_at(at, length), :] = piece

            chunks(lay)

        def bring(index, at):
            for k, target in enumerate((xT, cT)):
                piece = jnp.concatenate([take(2 * k + tile, at) for tile in range(tiles)], axis=1)
                piece = piece.astype(bf16)
                if k == 0:
                    xtok[seq, tokens_at(at), :] = piece
                else:
                    accc[...] += nn(some_ones, piece)
                target[seq, 0:width, tokens_at(at)] = nt(identity, piece).astype(bf16)

        chunks(bring)

        @pl.when(seq + 2 < count)
        def _():
            for copy in land(seq + 2):
                copy.start()

        def mark(index, at):
            position = at + lax.broadcasted_iota(jnp.int32, (1, CHUNK), 1)
            code = lax.broadcasted_iota(jnp.int32, (8, CHUNK), 0)
            hidden = (padv[pl.ds(seq, 1), tokens_at(at)] != 1).astype(f32)
            same = (segv[pl.ds(seq, 1), tokens_at(at)] == code).astype(f32)
            parts_q = [1.0 - same]
            parts_k = [same * mask_step]
            for digit in ((position // 64) % 8, (position // 8) % 8, position % 8):
                equal = (digit == code).astype(f32)
                parts_q.append(1.0 - equal)
                parts_k.append(equal * hidden * mask_step)
            both = jnp.concatenate(parts_k + parts_q + parts_k + parts_q, axis=0).astype(bf16)
            flat = nt(identity, both)
            turn[0, tokens_at(at), :] = flat
            if index < HALF // CHUNK:
                turn[0, tokens_at(at, length), :] = flat

        chunks(mark)
        nothing = jnp.zeros((32, CHUNK), f32)

        def bring_marks(index, at):
            piece = take(0, at).astype(bf16)
            codek[seq, tokens_at(at), :] = piece
            across = nt(identity[0:128, 0:128], piece)
            codeq[seq, :, tokens_at(at)] = jnp.concatenate([across[32:64], nothing], axis=0).astype(
                bf16
            )

        chunks(bring_marks)

    def prepare_step(seq, carry):
        prepare(seq)

        @pl.when(seq == 0)
        def _():
            gather_a.second()
            gather_b.first()

        if count > 1:

            @pl.when(seq == 1)
            def _():
                gather_a.third()

        if count > 2:

            @pl.when(seq == 2)
            def _():
                gather_b.second()

        return carry

    lax.fori_loop(0, count, prepare_step, 0)
    if count <= 1:
        gather_a.third()
    if count <= 2:
        gather_b.second()
    gather_a.finish()
    gather_b.third()

    def stacked(held, at, depth):
        stack = []
        for device in range(devices):
            outer, inner = device // inners, device % inners
            stack.append(held[outer % 2, outer // 2, inner].astype(f32)[at : at + depth])
        return jnp.concatenate(stack, axis=0)

    columns = stacked(held_a, 0, share)
    def unpack(held, at, matrices):
        for straight, across, source in matrices:
            depth = source.shape[0]
            for column in range(0, straight.shape[1], 128):
                whole = stacked(held, at, depth)
                straight[:, column : column + 128] = whole.astype(bf16)
                if across is wjt and column < width:
                    whole = whole * scale
                across[column : column + 128, :] = whole.T.astype(bf16)
                at += depth

    unpack(held_a, share, ((wj, wjt, shards[0]),))

    def spread(at):
        return jnp.broadcast_to(columns[:, at : at + 1], (width, 128))

    bj[0:width, :] = spread(0) * scale
    bj[width : 2 * width, :] = jnp.zeros((width, 128), f32)
    bj[2 * width : 3 * width, :] = spread(1)
    for at in range(6):
        bcol[at, :, :] = spread(2 + at)
    halves = [spread(8), spread(9)]
    be[...] = jnp.concatenate(
        [halves[k % 2][k // 2 * share : (k // 2 + 1) * share] for k in range(2 * devices)], axis=0
    )
    vrow[...] = columns.T[0:8, :]

    lane = lax.broadcasted_iota(jnp.int32, (CHUNK, 128), 1)
    low_lanes = lane < HEAD_DIM
    halves = [slice(t, t + 128) for t in range(0, CHUNK, 128)]
    ones = jnp.ones((16, HALF), bf16)

    def add_sums(row, values):
        accb[row : row + values.shape[0], :] += values

    def out_copy(seq):
        slot = lax.rem(seq, 2)
        return pltpu.make_async_copy(land_x.at[slot], out_hbm.at[seq], out_sem.at[slot])

    def attend(seq):
        def project(index, at):
            made = nn(wjt[...], xT[seq, 0:width, tokens_at(at)])
            flat = nn(xtok[seq, tokens_at(at), :], wj[:, width : 3 * width])
            for half in halves:
                there = tokens_at(at, half.start, 128)
                low = (made[:, half] + bj[...]).astype(bf16)
                qkT[seq, :, there] = low[0 : 2 * width]
                vT[:, there] = low[2 * width : 3 * width]
            vtok[seq, tokens_at(at), :] = (flat[:, width : 2 * width] + vrow[1:2, :]).astype(bf16)
            codes = codek[seq, tokens_at(at), :].astype(f32)
            for head in range(HEADS):
                lanes = slice((head // 2) * 128, (head // 2 + 1) * 128)
                mine = low_lanes if head % 2 == 0 else ~low_lanes
                kaug[head, tokens_at(at), :] = jnp.where(mine, flat[:, lanes], codes).astype(bf16)

        chunks(project)

        units = [
            (head, block, at)
            for head in range(HEADS)
            for block in range(blocks)
            for at in range(0, HALF, CHUNK)
        ]

        def scores_of(head, block, at):
            there = tokens_at(block * HALF, at)
            own = slice(head * HEAD_DIM, (head + 1) * HEAD_DIM)
            parts = [qkT[seq, own, there], codeq[seq, :, there]]
            if head % 2:
                parts = parts[::-1]
            keys = kaug[head, tokens_at(block * HALF, 0, HALF), :]
            return nn(keys, jnp.concatenate(parts, axis=0))

        def mix(head, block, at):
            own = slice(head * HEAD_DIM, (head + 1) * HEAD_DIM)
            there = tokens_at(block * HALF, at)
            values = vT[own, tokens_at(block * HALF, 0, HALF)]
            mixed = nn(
                jnp.concatenate([values, ones], axis=0),
                pT[seq, head * blocks + block, :, at : at + CHUNK],
            )
            inverse = 1.0 / mixed[HEAD_DIM : HEAD_DIM + 1, :]
            inv[head, 0:1, there] = inverse
            mixT[own, there] = (mixed[0:HEAD_DIM, :] * inverse).astype(bf16)

        coming = scores_of(*units[0])
        for k, (head, block, at) in enumerate(units):
            scores = coming
            if k + 1 < len(units):
                coming = scores_of(*units[k + 1])
            place = head * blocks + block
            for tile in range(0, CHUNK, 128):
                mine = scores[:, tile : tile + 128]
                highest = jnp.max(mine, axis=0, keepdims=True)
                pT[seq, place, :, at + tile : at + tile + 128] = jnp.exp2(
                    (mine - highest) * log2_e
                ).astype(bf16)
            if k:
                mix(*units[k - 1])
        mix(*units[-1])

    def dense(seq, side, at):
        slot = lax.rem(seq, 2)
        rows = tokens_at(at)
        branch = nn(wot[...], mixT[0:width, rows])
        firsts = []
        for half in halves:
            there = tokens_at(at, half.start, 128)
            hat, inverse = unit(
                xT[seq, 0:width, there].astype(f32) + branch[:, half] + bcol[0], width
            )
            hat1[side, :, half] = hat
            rinv1[side, 0:1, half] = inverse
            first = hat * bcol[1] + bcol[2]
            flow[0:width, there] = first.astype(bf16)
            firsts.append(first)
            yield
        inner = nn(wet[...], flow[0:width, rows])
        for half in halves:
            there = tokens_at(at, half.start, 128)
            for r in range(0, inner_width, 32):
                u = inner[r : r + 32, half] + be[r : r + 32, :]
                square = u * u
                t = jnp.tanh(u * (gelu_a + (gelu_a * gelu_b) * square))
                h = 0.5 + 0.5 * t
                value = u * h
                act[r : r + 32, there] = value.astype(bf16)
                dgelu[side, r : r + 32, half] = h + value * (1.0 - h) * (
                    2.0 * gelu_a + (6.0 * gelu_a * gelu_b) * square
                )
                if r % 256 == 224:
                    yield
        second = nn(wrt[...], act[0:inner_width, rows])
        grads, results, gains = [], [], []
        for k, half in enumerate(halves):
            there = tokens_at(at, half.start, 128)
            hat, inverse = unit(firsts[k] + second[:, half] + bcol[3], width)
            results.append((hat * bcol[4] + bcol[5]).astype(bf16))
            upstream = cT[seq, :, there].astype(f32)
            gains.append(upstream * hat)
            back = unit_back(upstream * bcol[4], hat, inverse, width)
            slow[:, there] = back.astype(bf16)
            grads.append(back)
            yield
        add_sums(0, gains[0] + gains[1])
        active_grad = nn(wr[...], slow[:, rows])
        land_x[slot, rows, :] = nt(identity, jnp.concatenate(results, axis=1)).astype(bf16)
        for half in halves:
            there = tokens_at(at, half.start, 128)
            for r in range(0, inner_width, 32):
                igr[r : r + 32, there] = (
                    active_grad[r : r + 32, half] * dgelu[side, r : r + 32, half]
                ).astype(bf16)
            yield
        deeper = nn(we[...], igr[:, rows])
        gains, shifts = [], []
        for k, half in enumerate(halves):
            there = tokens_at(at, half.start, 128)
            first_grad = grads[k] + deeper[:, half]
            hat = hat1[side, :, half]
            gains.append(first_grad * hat)
            shifts.append(first_grad)
            back = unit_back(first_grad * bcol[1], hat, rinv1[side, 0:1, half], width)
            blow[seq, :, there] = back.astype(bf16)
            yield
        add_sums(width, gains[0] + gains[1])
        add_sums(2 * width, shifts[0] + shifts[1])
        grown = nn(wo[...], blow[seq, :, rows]).astype(bf16).astype(f32)
        for head in range(HEADS):
            own = slice(head * HEAD_DIM, (head + 1) * HEAD_DIM)
            piece = grown[own, :] * inv[head, 0:1, rows]
            total = over_features(piece * mixT[own, rows].astype(f32))
            high = total.astype(bf16).astype(f32)
            dots[seq, head, 0:1, rows] = high
            dots[seq, head, 1:2, rows] = total - high
            doT[seq, own, rows] = piece.astype(bf16)
        yield

    def weight_sums(seq):
        gr[...] += nt(act[...], slow[...])
        ge[...] += nt(flow[...], igr[...])
        go[...] += nt(mixT[...], blow[seq])

    low_half = lax.broadcasted_iota(jnp.int32, (HALF, 128), 1) < HEAD_DIM
    keep = [low_half.astype(f32).astype(bf16), (~low_half).astype(f32).astype(bf16)]
    fill = [-keep[1], -keep[0]]
    extra_row = lax.broadcasted_iota(jnp.int32, (16, HALF), 0)

    def attend_back(seq, index):
        pair, block = index // blocks, index % blocks
        first = block * HALF
        lanes = slice(pair * 128, pair * 128 + 128)
        cols = tokens_at(first, 0, HALF)
        for odd in range(2):
            head = pair * 2 + odd
            own = slice(head * HEAD_DIM, (head + 1) * HEAD_DIM)
            key_rows = slice(width + own.start, width + own.stop)
            place = head * blocks + block
            high, rest = dots[seq, head, 0:1, cols], dots[seq, head, 1:2, cols]
            extra = jnp.where(extra_row == 0, high, jnp.where(extra_row == 1, rest, 0.0))
            extra = jnp.concatenate([extra, jnp.zeros((HEAD_DIM - 16, HALF), f32)], axis=0)
            grown = doT[seq, own, cols]
            stack = [grown, extra.astype(bf16)]
            if odd:
                stack = stack[::-1]
            stack = jnp.concatenate(stack, axis=0)
            side = vtok[seq, cols, lanes] * keep[odd] + fill[odd]
            for at in range(0, HALF, CHUNK):
                part = slice(at, at + CHUNK)
                grads = nn(side, stack[:, part])
                dsT[odd, :, part] = (pT[seq, place, :, part].astype(f32) * grads).astype(bf16)
                yield
            value_grad = nt(grown, pT[seq, place]).astype(bf16)
            yield
            key_grad = nt(qkT[seq, own, cols], dsT[odd]).astype(bf16)
            yield
            query_grad = (nn(qkT[seq, key_rows, cols], dsT[odd]) * scale).astype(bf16)
            yield
            doT[seq, own, cols] = value_grad
            qkT[seq, key_rows, cols] = key_grad
            qkT[seq, own, cols] = query_grad

    def joint_sums(seq):
        turned = xT[seq]
        gj[:, 0 : 2 * width] += nt(turned, qkT[seq])
        gj[:, 2 * width : 3 * width] += nt(turned, doT[seq])

    def together(*parts):
        parts = list(parts)
        while parts:
            for part in list(parts):
                if next(part, parts) is parts:
                    parts.remove(part)

    def chains(seq):
        def chain(side):
            chunk_count = length // CHUNK
            for index in range(side * chunk_count // 2, (side + 1) * chunk_count // 2):
                yield from dense(seq, side, index * CHUNK)

        return [chain(0), chain(1)]

    def backs(seq):
        for index in range(HEADS // 2 * blocks):
            yield from attend_back(seq, index)

    attend(0)
    gather_b.finish()
    unpack(
        held_b, 0, ((wo, wot, shards[1]), (we, wet, shards[2]), (wr, wrt, shards[3]))
    )
    together(*chains(0))
    weight_sums(0)
    out_copy(0).start()

    def middle(seq, carry):
        attend(seq)

        @pl.when(seq >= 2)
        def _():
            out_copy(seq - 2).wait()

        together(*chains(seq), backs(seq - 1))
        weight_sums(seq)
        joint_sums(seq - 1)
        out_copy(seq).start()
        return carry

    lax.fori_loop(1, count, middle, 0)

    def pack(reduce, sources):
        for device in range(devices):
            outer = device // inners
            pieces = []
            for ref in sources:
                depth = ref.shape[0] // devices
                pieces += column_blocks(ref[device * depth : (device + 1) * depth, :])
            packed = reduce.packed
            packed[outer % 2, outer // 2, device % inners] = padded_rows(pieces, packed.shape[3])

    sum_a, sum_b = Reduce(peers, *reduce_a), Reduce(peers, *reduce_b)
    pack(sum_a, (go.at[0:width], ge.at[0:width], gr.at[0:inner_width]))
    sum_a.first()

    for k, step in enumerate(backs(count - 1)):
        if k == 12:
            sum_a.second()
        if k == 30:
            sum_a.third()
    joint_sums(count - 1)
    rows = [
        gj[width : width + 1, 0:width],
        gj[width : width + 1, 2 * width : 3 * width],
        go[width : width + 1, :],
        jnp.zeros((2, width), f32),
        gr[inner_width : inner_width + 1, :],
        jnp.zeros((1, width), f32),
        accc[0:1, :],
    ]
    missing = 128 - sum(row.shape[0] for row in rows)
    columns = jnp.concatenate(rows + [jnp.zeros((missing, width), f32)], axis=0).T
    lanes = lax.broadcasted_iota(jnp.int32, (width, 128), 1)
    for at, place in ((6, 0), (3, width), (4, 2 * width)):
        total = jnp.sum(accb[place : place + width, :], axis=1, keepdims=True)
        columns = jnp.where(lanes == at, total, columns)
    wide = jnp.broadcast_to(ge[width : width + 1, :], (128, inner_width)).T
    for first in range(2):
        item = [wide[k * share : (k + 1) * share] for k in range(first, 2 * devices, 2)]
        columns = jnp.where(lanes == VECTORS + first, jnp.concatenate(item, axis=0), columns)
    bcol[0] = columns
    pack(sum_b, (bcol.at[0], gj.at[0:width]))
    sum_b.first()

    def tg_copies(seq):
        slot = lax.rem(seq, 2)
        return [
            pltpu.make_async_copy(
                turn.at[slot * 2 + tile, pl.ds(0, length)],
                tg_hbm.at[seq, tile],
                tg_sem.at[slot, tile],
            )
            for tile in range(tiles)
        ]

    def inputs_back(seq, carry):
        @pl.when(seq >= 2)
        def _():
            for copy in tg_copies(seq - 2):
                copy.wait()

        slot = lax.rem(seq, 2)

        def one(index, at):
            rows = tokens_at(at)
            result = (
                nn(wj[:, 0 : 2 * width], qkT[seq, :, rows])
                + nn(wj[:, 2 * width : 3 * width], doT[seq, :, rows])
                + blow[seq, :, rows].astype(f32)
            ).T
            for tile in range(tiles):
                turn[slot * 2 + tile, rows, :] = result[:, tile * 128 : (tile + 1) * 128]

        chunks(one)
        for copy in tg_copies(seq):
            copy.start()

        @pl.when(seq == 0)
        def _():
            sum_b.second()

        if count > 2:

            @pl.when(seq == 2)
            def _():
                sum_b.third()

        return carry

    lax.fori_loop(0, count, inputs_back, 0)
    if count <= 2:
        sum_b.third()
    fin_a[...] = sum_a.finish()
    fin_b[...] = sum_b.finish()
    for seq in range(max(count - 2, 0), count):
        out_copy(seq).wait()
        for copy in tg_copies(seq):
            copy.wait()


def run_layer(outers, inners, tokens, segment_ids, padding_mask, cotangent, shards):
    count, length, width = tokens.shape
    devices = outers * inners
    share = width // devices
    inner_width = shards[2].shape[1]
    tiles = width // 128
    chips = outers // 2
    blocks = length // HALF

    def rows_of(items):
        return sum(item.size // 128 for item in items)

    held_a = rounded_up(share + rows_of(shards[:1]), 16)
    held_b = rounded_up(rows_of(shards[1:4]), 16)
    dma = pltpu.SemaphoreType.DMA
    vmem = pltpu.VMEM
    shape = jax.ShapeDtypeStruct
    scratch = [vmem(item.shape, bf16) for item in shards]
    scratch += [
        vmem((2, length, width), bf16),
        vmem((2, length, width), bf16),
        vmem((count, length), jnp.int32),
        vmem((count, length), jnp.int32),
        vmem((width, 3 * width), bf16),
        vmem((width, width), bf16),
        vmem((width, inner_width), bf16),
        vmem((inner_width, width), bf16),
        vmem((3 * width, width), bf16),
        vmem((width, width), bf16),
        vmem((inner_width, width), bf16),
        vmem((width, inner_width), bf16),
        vmem((3 * width, 128), f32),
        vmem((inner_width, 128), f32),
        vmem((6, width, 128), f32),
        vmem((8, width), f32),
        vmem((2 * tiles, length + HALF, 128), f32),
        vmem((count, length, width), bf16),
        vmem((count, width + 16, length), bf16),
        vmem((count, width, length), bf16),
        vmem((count, length, 128), bf16),
        vmem((count, HEAD_DIM, length), bf16),
        vmem((count, 2 * width, length), bf16),
        vmem((width, length), bf16),
        vmem((HEADS, length, 128), bf16),
        vmem((count, length, width), bf16),
        vmem((count, HEADS * blocks, HALF, HALF), bf16),
        vmem((HEADS, 8, length), f32),
        vmem((width + 16, length), bf16),
        vmem((2, width, CHUNK), f32),
        vmem((2, 8, CHUNK), f32),
        vmem((inner_width + 16, length), bf16),
        vmem((width, length), bf16),
        vmem((inner_width, length), bf16),
        vmem((width + 16, length), bf16),
        vmem((count, width, length), bf16),
        vmem((2, inner_width, CHUNK), f32),
        vmem((2, HALF, HALF), bf16),
        vmem((count, HEADS, 8, length), f32),
        vmem((width + 16, 3 * width), f32),
        vmem((width + 16, width), f32),
        vmem((width + 16, inner_width), f32),
        vmem((inner_width + 16, width), f32),
        vmem((3 * width, 128), f32),
        vmem((16, width), f32),
        vmem((2, chips, inners, held_a, 128), bf16),
        dma((inners + 2 * chips,)),
        dma((inners + 2 * chips,)),
        vmem((2, chips, inners, held_b, 128), bf16),
        dma((inners + 2 * chips,)),
        dma((inners + 2 * chips,)),
    ]
    scratch += reduce_scratch(outers, inners, held_b)
    scratch += reduce_scratch(outers, inners, held_a)
    scratch += [dma((len(shards) + 2,)), dma((2, 2)), dma((2,)), dma((2, tiles))]
    hbm = pl.BlockSpec(memory_space=pl.ANY)
    return pl.pallas_call(
        functools.partial(layer_kernel, outers, inners),
        in_specs=[pl.BlockSpec(memory_space=pltpu.SMEM)] + [hbm] * (4 + len(shards)),
        out_specs=[hbm, hbm] + [pl.BlockSpec(memory_space=pltpu.VMEM)] * 2,
        out_shape=[
            shape(tokens.shape, bf16),
            shape((count, tiles, length, 128), f32),
            shape((held_b, 128), f32),
            shape((held_a, 128), f32),
        ],
        scratch_shapes=scratch,
        compiler_params=pltpu.CompilerParams(
            collective_id=0, has_side_effects=True, vmem_limit_bytes=64 * 1024 * 1024 - 65536
        ),
        name="layer",
    )(segment_ids, tokens, cotangent, segment_ids, padding_mask, *shards)


def finish_kernel(seg_smem, out_turned, tg_turned, fin_a, fin_b, *refs):
    layer_out, tokens_grad, matrices, vectors = refs[0], refs[1], refs[2:6], refs[6:-2]
    plain, bent = refs[-2:]
    seq = pl.program_id(0)
    length, width = layer_out.shape[1], layer_out.shape[2]
    start = big_cell_start(seg_smem, seq, length)
    tiles = width // 128
    for tile in range(tiles):
        lanes = slice(tile * 128, (tile + 1) * 128)
        plain[tile] = out_turned[0, :, lanes].astype(f32)
        for k, source in enumerate((plain.at[tile], tg_turned.at[0, tile])):
            bent[k, tile, 0:CHUNK] = source[length - CHUNK : length]
            bent[k, tile, CHUNK : 2 * CHUNK] = source[0:CHUNK]
    for at in range(0, length, CHUNK):
        begin = lax.rem(length + at - start, length)

        def give(pieces):
            for tile in range(tiles):
                lanes = slice(tile * 128, (tile + 1) * 128)
                for k, target in enumerate((layer_out, tokens_grad)):
                    piece = pieces(k, tile)
                    target[0, at : at + CHUNK, lanes] = piece.astype(target.dtype)

        @pl.when(begin <= length - CHUNK)
        def _():
            whole = [lambda tile: plain.at[tile], lambda tile: tg_turned.at[0, tile]]
            give(lambda k, tile: whole[k](tile)[pl.ds(begin, CHUNK), :])

        @pl.when(begin > length - CHUNK)
        def _():
            give(lambda k, tile: bent[k, tile, pl.ds(begin - (length - CHUNK), CHUNK), :])

    @pl.when(seq == 0)
    def _():
        rows = vectors[0].shape[0]
        lines = fin_b[0:rows, :].T
        for at, ref in enumerate(vectors[:-1]):
            ref[...] = lines[at, :]
        vectors[-1][...] = jnp.concatenate([lines[VECTORS, :], lines[VECTORS + 1, :]])
        for source, at, targets in ((fin_b, rows, matrices[:1]), (fin_a, 0, matrices[1:])):
            for ref in targets:
                depth = ref.shape[0]
                for column in range(0, ref.shape[1], 128):
                    ref[:, column : column + 128] = source[at : at + depth, :]
                    at += depth


def finish(segment_ids, out_turned, tg_turned, fin_a, fin_b, shards):
    count, length, width = out_turned.shape
    tiles = width // 128

    def whole(shape):
        return pl.BlockSpec(shape, lambda i: (0,) * len(shape))

    per_seq = pl.BlockSpec((1, length, width), lambda i: (i, 0, 0))
    shape = jax.ShapeDtypeStruct
    return pl.pallas_call(
        finish_kernel,
        grid=(count,),
        in_specs=[
            pl.BlockSpec(memory_space=pltpu.SMEM),
            per_seq,
            pl.BlockSpec((1, tiles, length, 128), lambda i: (i, 0, 0, 0)),
            whole(fin_a.shape),
            whole(fin_b.shape),
        ],
        out_specs=[per_seq, per_seq] + [whole(item.shape) for item in shards],
        out_shape=[shape(out_turned.shape, bf16), shape(out_turned.shape, f32)]
        + [shape(item.shape, f32) for item in shards],
        scratch_shapes=[
            pltpu.VMEM((tiles, length, 128), f32),
            pltpu.VMEM((2, tiles, 2 * CHUNK, 128), f32),
        ],
        compiler_params=pltpu.CompilerParams(
            dimension_semantics=("arbitrary",), vmem_limit_bytes=60 * 1024 * 1024
        ),
        name="finish",
    )(segment_ids, out_turned, tg_turned, fin_a, fin_b)


def on_device(
    outers,
    inners,
    tokens,
    segment_ids,
    padding_mask,
    joint_weight,
    query_bias,
    value_bias,
    output_weight,
    output_bias,
    first_gain,
    first_shift,
    expand_weight,
    expand_bias,
    reduce_weight,
    reduce_bias,
    second_gain,
    second_shift,
    cotangent,
):
    shards = (
        joint_weight,
        output_weight,
        expand_weight,
        reduce_weight,
        query_bias,
        value_bias,
        output_bias,
        first_gain,
        first_shift,
        reduce_bias,
        second_gain,
        second_shift,
        expand_bias,
    )
    turned = run_layer(outers, inners, tokens, segment_ids, padding_mask, cotangent, shards)
    layer_out, tokens_grad, *owned = finish(segment_ids, *turned, shards)
    gj, go, ge, gr, query, value, out, gain1, shift1, reduce, gain2, shift2, expand = owned
    return (
        layer_out,
        tokens_grad,
        gj,
        query,
        value,
        go,
        out,
        gain1,
        shift1,
        ge,
        expand,
        gr,
        reduce,
        gain2,
        shift2,
    )


def solution(mesh):
    rows = P(("outer", "inner"))
    rows2 = P(("outer", "inner"), None)
    rows3 = P(("outer", "inner"), None, None)
    weights = (rows2, rows, rows, rows2, rows, rows, rows, rows2, rows, rows2, rows, rows, rows)
    return jax.shard_map(
        functools.partial(on_device, mesh.shape["outer"], mesh.shape["inner"]),
        mesh=mesh,
        in_specs=(rows3, rows2, rows2) + weights + (rows3,),
        out_specs=(rows3, rows3) + weights,
        check_vma=False,
    )
```

```python
import functools
import math

import jax
import jax.numpy as jnp
from jax import lax
from jax.experimental import pallas as pl
from jax.experimental.pallas import tpu as pltpu
from jax.sharding import PartitionSpec as P

HEADS = 4
HEAD_DIM = 64
HALF = 512
CHUNK = 256
VECTORS = 8
MESH = pl.DeviceIdType.MESH

norm_epsilon = 1e-06
mask_step = -(2.0**100)
log2_e = math.log2(math.e)
gelu_a = math.sqrt(2.0 / math.pi)
gelu_b = 0.044715

f32 = jnp.float32
bf16 = jnp.bfloat16


def nn(left, right):
    return lax.dot_general(left, right, (((1,), (0,)), ((), ())), preferred_element_type=f32)


def nt(left, right):
    return lax.dot_general(left, right, (((1,), (1,)), ((), ())), preferred_element_type=f32)


def over_features(values):
    return jnp.sum(values, axis=0, keepdims=True)


def column_blocks(values):
    return [values[:, at : at + 128] for at in range(0, values.shape[1], 128)]


def padded_rows(pieces, rows):
    have = sum(piece.shape[0] for piece in pieces)
    if rows > have:
        pieces = pieces + [jnp.zeros((rows - have, 128), f32)]
    return jnp.concatenate(pieces, axis=0)


def rounded_up(amount, to):
    return (amount + to - 1) // to * to


def big_cell_start(seg_ref, seq, length):
    wanted = seg_ref[seq, HALF - 1]
    low = jnp.int32(0)
    step = HALF
    while step > 1:
        step //= 2
        probe = low + step
        low = jnp.where(seg_ref[seq, probe - 1] < wanted, probe, low)
    last = jnp.minimum(low + HALF - 1, length - 1)
    return jnp.where(seg_ref[seq, last] == wanted, low, HALF)


def copy_to(source, target, send, receive, outer, inner):
    return pltpu.make_async_remote_copy(
        src_ref=source,
        dst_ref=target,
        send_sem=send,
        recv_sem=receive,
        device_id=(outer, inner),
        device_id_type=MESH,
    )


class Peers:
    def __init__(self, outers, inners):
        self.outers, self.inners = outers, inners
        self.outer = lax.axis_index("outer")
        self.inner = lax.axis_index("inner")
        self.core = lax.rem(self.outer, 2)
        self.chip = lax.div(self.outer, 2)
        self.chips = outers // 2
        self.mate = self.chip * 2 + 1 - self.core

    def along_inner(self):
        return [lax.rem(self.inner + step, self.inners) for step in range(1, self.inners)]

    def along_chips(self):
        return [lax.rem(self.chip + step, self.chips) for step in range(1, self.chips)]

    def greet(self):
        barrier = pltpu.get_barrier_semaphore()
        others = [(self.outer, at) for at in self.along_inner()]
        others += [(at * 2 + self.core, self.inner) for at in self.along_chips()]
        others += [(self.mate, self.inner)]
        for other in others:
            pl.semaphore_signal(barrier, inc=1, device_id=other, device_id_type=MESH)

    def meet(self):
        pl.semaphore_wait(pltpu.get_barrier_semaphore(), self.inners - 1 + self.chips - 1 + 1)


class Gather:
    def __init__(self, peers, held, send, receive):
        self.peers, self.held, self.send, self.receive = peers, held, send, receive

    def one(self, at, spot, outer, inner):
        peers = self.peers
        block = self.held.at[peers.core, peers.chip, at]
        return copy_to(block, block, self.send.at[spot], self.receive.at[at], outer, inner)

    def block(self, core, chip, spot, signal, outer):
        peers = self.peers
        block = self.held.at[core, chip]
        signal = self.receive.at[peers.inners + signal]
        return copy_to(block, block, self.send.at[spot], signal, outer, peers.inner)

    def to_inner(self):
        peers = self.peers
        return [
            self.one(peers.inner, k, peers.outer, at) for k, at in enumerate(peers.along_inner())
        ]

    def to_chips(self):
        peers = self.peers
        return [
            self.block(peers.core, peers.chip, peers.inners + k, peers.chip, other * 2 + peers.core)
            for k, other in enumerate(peers.along_chips())
        ]

    def to_mate(self, k):
        peers = self.peers
        chip = ([peers.chip] + peers.along_chips())[k]
        spot = peers.inners + peers.chips + k
        return self.block(peers.core, chip, spot, peers.chips + chip, peers.mate)

    def first(self):
        for copy in self.to_inner():
            copy.start()

    def second(self):
        peers = self.peers
        for at in peers.along_inner():
            self.one(at, 0, peers.outer, peers.inner).wait_recv()
        for copy in self.to_chips() + [self.to_mate(0)]:
            copy.start()

    def third(self):
        peers = self.peers
        for k, other in enumerate(peers.along_chips()):
            self.block(peers.core, other, 0, other, peers.outer).wait_recv()
            self.to_mate(k + 1).start()

    def finish(self):
        peers = self.peers
        for chip in [peers.chip] + peers.along_chips():
            self.block(1 - peers.core, chip, 0, peers.chips + chip, peers.outer).wait_recv()
        for copy in (
            self.to_inner() + self.to_chips() + [self.to_mate(k) for k in range(peers.chips)]
        ):
            copy.wait_send()


class Reduce:
    def __init__(self, peers, packed, from_mate, mid, from_chips, last, from_inner, send, receive):
        self.peers, self.packed, self.from_mate = peers, packed, from_mate
        self.mid, self.from_chips, self.last = mid, from_chips, last
        self.from_inner, self.send, self.receive = from_inner, send, receive

    def to_mate(self):
        peers = self.peers
        return copy_to(
            self.packed.at[1 - peers.core],
            self.from_mate,
            self.send.at[0],
            self.receive.at[0],
            peers.mate,
            peers.inner,
        )

    def to_chips(self):
        peers = self.peers
        return [
            copy_to(
                self.mid.at[k],
                self.from_chips.at[k],
                self.send.at[1 + k],
                self.receive.at[1 + k],
                other * 2 + peers.core,
                peers.inner,
            )
            for k, other in enumerate(peers.along_chips())
        ]

    def to_inner(self):
        peers = self.peers
        return [
            copy_to(
                self.last.at[k],
                self.from_inner.at[k],
                self.send.at[peers.chips + k],
                self.receive.at[peers.chips + k],
                peers.outer,
                at,
            )
            for k, at in enumerate(peers.along_inner())
        ]

    def first(self):
        self.to_mate().start()

    def second(self):
        peers = self.peers
        self.to_mate().wait()
        for k, (other, copy) in enumerate(zip(peers.along_chips(), self.to_chips())):
            for at in range(peers.inners):
                total = self.packed[peers.core, other, at] + self.from_mate[other, at]
                self.mid[k, at] = total.astype(bf16)
            copy.start()

    def own(self, at):
        peers = self.peers
        total = self.packed[peers.core, peers.chip, at] + self.from_mate[peers.chip, at]
        for k in range(peers.chips - 1):
            total += self.from_chips[k, at].astype(f32)
        return total

    def third(self):
        for copy in self.to_chips():
            copy.wait()
        for k, (at, copy) in enumerate(zip(self.peers.along_inner(), self.to_inner())):
            self.last[k] = self.own(at).astype(bf16)
            copy.start()

    def finish(self):
        total = self.own(self.peers.inner)
        for k, copy in enumerate(self.to_inner()):
            copy.wait()
            total += self.from_inner[k].astype(f32)
        return total


def reduce_scratch(outers, inners, rows):
    chips = outers // 2
    return [
        pltpu.VMEM((2, chips, inners, rows, 128), f32),
        pltpu.VMEM((chips, inners, rows, 128), f32),
        pltpu.VMEM((max(chips - 1, 1), inners, rows, 128), bf16),
        pltpu.VMEM((max(chips - 1, 1), inners, rows, 128), bf16),
        pltpu.VMEM((inners - 1, rows, 128), bf16),
        pltpu.VMEM((inners - 1, rows, 128), bf16),
        pltpu.SemaphoreType.DMA((chips + inners,)),
        pltpu.SemaphoreType.DMA((chips + inners,)),
    ]


REDUCE_SCRATCH = 8


def unit(hidden, width):
    centred = hidden - over_features(hidden) * (1.0 / width)
    inverse = lax.rsqrt(over_features(centred * centred) * (1.0 / width) + norm_epsilon)
    return centred * inverse, inverse


def unit_back(inside, hat, inverse, width):
    return inverse * (
        inside
        - over_features(inside) * (1.0 / width)
        - hat * (over_features(inside * hat) * (1.0 / width))
    )


def layer_kernel(outers, inners, *refs):
    refs = list(refs)

    def grab(amount):
        taken = refs[:amount]
        del refs[:amount]
        return taken

    seg_smem, tokens_hbm, cot_hbm, seg_hbm, pad_hbm = grab(5)
    shard_hbm = grab(4 + VECTORS + 1)
    out_hbm, tg_hbm, fin_a, fin_b, fin_c = grab(5)
    shards = grab(4 + VECTORS + 1)
    land_x, land_c, segv, padv = grab(4)
    wj, wo, we, wr, wjt, wot, wet, wrt, bj, be, bcol, vrow = grab(12)
    turn, xtok, xT, cT, codek, codeq = grab(6)
    qkT, vT, kaug, vtok, pT, inv, mixT = grab(7)
    hat1, rinv1, act, slow, igr, flow, blow, dgelu, dsT = grab(9)
    (dots,) = grab(1)
    doT = cT
    gj, go, ge, gr, accb, accc = grab(6)
    held_a, send_a, receive_a, held_b, send_b, receive_b = grab(6)
    reduce_a, reduce_b, reduce_c = [grab(REDUCE_SCRATCH) for k in range(3)]
    shard_sem, land_sem, out_sem, tg_sem = grab(4)

    count, length, width = tokens_hbm.shape
    inner_width = we.shape[1]
    devices = outers * inners
    share = width // devices
    scale = HEAD_DIM**-0.5
    tiles = width // 128
    blocks = length // HALF
    peers = Peers(outers, inners)

    def land(seq):
        slot = lax.rem(seq, 2)
        return [
            pltpu.make_async_copy(tokens_hbm.at[seq], land_x.at[slot], land_sem.at[0, slot]),
            pltpu.make_async_copy(cot_hbm.at[seq], land_c.at[slot], land_sem.at[1, slot]),
        ]

    small = [
        pltpu.make_async_copy(source, target, shard_sem.at[k])
        for k, (source, target) in enumerate(
            zip(shard_hbm + [seg_hbm, pad_hbm], shards + [segv, padv])
        )
    ]
    for copy in small:
        copy.start()
    peers.greet()
    for seq in range(min(2, count)):
        for copy in land(jnp.int32(seq)):
            copy.start()
    for copy in small:
        copy.wait()

    lines = [ref[...].astype(f32).reshape(1, ref.shape[0]) for ref in shards[4:]]
    lines = lines[:-1] + [lines[-1][:, :share], lines[-1][:, share:]]
    lines.append(jnp.zeros((128 - len(lines), share), f32))
    pieces = [jnp.concatenate(lines, axis=0).T] + column_blocks(shards[0][...].astype(f32))
    here = (peers.core, peers.chip, peers.inner)
    held_a[here] = padded_rows(pieces, held_a.shape[3]).astype(bf16)
    pieces = []
    for ref in shards[1:4]:
        pieces += column_blocks(ref[...].astype(f32))
    held_b[here] = padded_rows(pieces, held_b.shape[3]).astype(bf16)
    peers.meet()
    gather_a = Gather(peers, held_a, send_a, receive_a)
    gather_b = Gather(peers, held_b, send_b, receive_b)
    gather_a.first()

    identity = (
        lax.broadcasted_iota(jnp.int32, (CHUNK, CHUNK), 0)
        == lax.broadcasted_iota(jnp.int32, (CHUNK, CHUNK), 1)
    )
    identity = identity.astype(f32).astype(bf16)

    for ref in [mixT, act, flow] + [xT.at[seq] for seq in range(count)]:
        ref[ref.shape[0] - 16 : ref.shape[0], :] = jnp.ones((16, length), bf16)
    for ref in (gj, go, ge, gr, accb, accc):
        ref[...] = jnp.zeros_like(ref)
    some_ones = jnp.ones((16, CHUNK), bf16)

    def chunks(body):
        for index in range(length // CHUNK):
            body(index, index * CHUNK)

    def tokens_at(at, offset=0, size=CHUNK):
        return slice(at + offset, at + offset + size)

    def prepare(seq):
        for copy in land(seq):
            copy.wait()
        start = big_cell_start(seg_smem, seq, length)
        slot = lax.rem(seq, 2)

        def take(tile, at):
            return turn[tile, pl.ds(start + at, CHUNK), :]

        for k, source in enumerate((land_x, land_c)):

            def lay(index, at):
                for tile in range(tiles):
                    lanes = slice(tile * 128, (tile + 1) * 128)
                    piece = source[slot, tokens_at(at), lanes].astype(f32)
                    turn[2 * k + tile, tokens_at(at), :] = piece
                    if index < HALF // CHUNK:
                        turn[2 * k + tile, tokens_at(at, length), :] = piece

            chunks(lay)

        def bring(index, at):
            for k, target in enumerate((xT, cT)):
                piece = jnp.concatenate([take(2 * k + tile, at) for tile in range(tiles)], axis=1)
                piece = piece.astype(bf16)
                if k == 0:
                    xtok[seq, tokens_at(at), :] = piece
                else:
                    accc[...] += nn(some_ones, piece)
                target[seq, 0:width, tokens_at(at)] = nt(identity, piece).astype(bf16)

        chunks(bring)

        @pl.when(seq + 2 < count)
        def _():
            for copy in land(seq + 2):
                copy.start()

        def mark(index, at):
            position = at + lax.broadcasted_iota(jnp.int32, (1, CHUNK), 1)
            code = lax.broadcasted_iota(jnp.int32, (8, CHUNK), 0)
            hidden = (padv[pl.ds(seq, 1), tokens_at(at)] != 1).astype(f32)
            same = (segv[pl.ds(seq, 1), tokens_at(at)] == code).astype(f32)
            parts_q = [1.0 - same]
            parts_k = [same * mask_step]
            for digit in ((position // 64) % 8, (position // 8) % 8, position % 8):
                equal = (digit == code).astype(f32)
                parts_q.append(1.0 - equal)
                parts_k.append(equal * hidden * mask_step)
            both = jnp.concatenate(parts_k + parts_q + parts_k + parts_q, axis=0).astype(bf16)
            flat = nt(identity, both)
            turn[0, tokens_at(at), :] = flat
            if index < HALF // CHUNK:
                turn[0, tokens_at(at, length), :] = flat

        chunks(mark)
        nothing = jnp.zeros((32, CHUNK), f32)

        def bring_marks(index, at):
            piece = take(0, at).astype(bf16)
            codek[seq, tokens_at(at), :] = piece
            across = nt(identity[0:128, 0:128], piece)
            codeq[seq, :, tokens_at(at)] = jnp.concatenate([across[32:64], nothing], axis=0).astype(
                bf16
            )

        chunks(bring_marks)

    def prepare_step(seq, carry):
        prepare(seq)

        @pl.when(seq == 0)
        def _():
            gather_a.second()
            gather_b.first()

        if count > 1:

            @pl.when(seq == 1)
            def _():
                gather_a.third()

        if count > 2:

            @pl.when(seq == 2)
            def _():
                gather_b.second()

        return carry

    lax.fori_loop(0, count, prepare_step, 0)
    if count <= 1:
        gather_a.third()
    if count <= 2:
        gather_b.second()
    gather_a.finish()

    def stacked(held, at, depth):
        stack = []
        for device in range(devices):
            outer, inner = device // inners, device % inners
            stack.append(held[outer % 2, outer // 2, inner].astype(f32)[at : at + depth])
        return jnp.concatenate(stack, axis=0)

    columns = stacked(held_a, 0, share)
    def unpack(held, at, matrices):
        for straight, across, source in matrices:
            depth = source.shape[0]
            for column in range(0, straight.shape[1], 128):
                whole = stacked(held, at, depth)
                straight[:, column : column + 128] = whole.astype(bf16)
                if across is wjt and column < width:
                    whole = whole * scale
                across[column : column + 128, :] = whole.T.astype(bf16)
                at += depth

    unpack(held_a, share, ((wj, wjt, shards[0]),))

    def spread(at):
        return jnp.broadcast_to(columns[:, at : at + 1], (width, 128))

    bj[0:width, :] = spread(0) * scale
    bj[width : 2 * width, :] = jnp.zeros((width, 128), f32)
    bj[2 * width : 3 * width, :] = spread(1)
    for at in range(6):
        bcol[at, :, :] = spread(2 + at)
    halves = [spread(8), spread(9)]
    be[...] = jnp.concatenate(
        [halves[k % 2][k // 2 * share : (k // 2 + 1) * share] for k in range(2 * devices)], axis=0
    )
    vrow[...] = columns.T[0:8, :]

    lane = lax.broadcasted_iota(jnp.int32, (CHUNK, 128), 1)
    low_lanes = lane < HEAD_DIM
    halves = [slice(t, t + 128) for t in range(0, CHUNK, 128)]
    ones = jnp.ones((16, HALF), bf16)

    def add_sums(row, values):
        accb[row : row + values.shape[0], :] += values

    def out_copy(seq):
        slot = lax.rem(seq, 2)
        return pltpu.make_async_copy(land_x.at[slot], out_hbm.at[seq], out_sem.at[slot])

    def attend(seq, between=()):
        between = dict(between)

        def project(index, at):
            made = nn(wjt[...], xT[seq, 0:width, tokens_at(at)])
            flat = nn(xtok[seq, tokens_at(at), :], wj[:, width : 3 * width])
            for half in halves:
                there = tokens_at(at, half.start, 128)
                low = (made[:, half] + bj[...]).astype(bf16)
                qkT[seq, :, there] = low[0 : 2 * width]
                vT[:, there] = low[2 * width : 3 * width]
            vtok[seq, tokens_at(at), :] = (flat[:, width : 2 * width] + vrow[1:2, :]).astype(bf16)
            codes = codek[seq, tokens_at(at), :].astype(f32)
            for head in range(HEADS):
                lanes = slice((head // 2) * 128, (head // 2 + 1) * 128)
                mine = low_lanes if head % 2 == 0 else ~low_lanes
                kaug[head, tokens_at(at), :] = jnp.where(mine, flat[:, lanes], codes).astype(bf16)

        chunks(project)

        units = [
            (head, block, at)
            for head in range(HEADS)
            for block in range(blocks)
            for at in range(0, HALF, CHUNK)
        ]

        def scores_of(head, block, at):
            there = tokens_at(block * HALF, at)
            own = slice(head * HEAD_DIM, (head + 1) * HEAD_DIM)
            parts = [qkT[seq, own, there], codeq[seq, :, there]]
            if head % 2:
                parts = parts[::-1]
            keys = kaug[head, tokens_at(block * HALF, 0, HALF), :]
            return nn(keys, jnp.concatenate(parts, axis=0))

        def mix(head, block, at):
            own = slice(head * HEAD_DIM, (head + 1) * HEAD_DIM)
            there = tokens_at(block * HALF, at)
            values = vT[own, tokens_at(block * HALF, 0, HALF)]
            mixed = nn(
                jnp.concatenate([values, ones], axis=0),
                pT[seq, head * blocks + block, :, at : at + CHUNK],
            )
            inverse = 1.0 / mixed[HEAD_DIM : HEAD_DIM + 1, :]
            inv[head : head + 1, there] = inverse
            mixT[own, there] = (mixed[0:HEAD_DIM, :] * inverse).astype(bf16)

        coming = scores_of(*units[0])
        for k, (head, block, at) in enumerate(units):
            scores = coming
            if k + 1 < len(units):
                coming = scores_of(*units[k + 1])
            place = head * blocks + block
            for tile in range(0, CHUNK, 128):
                mine = scores[:, tile : tile + 128]
                highest = jnp.max(mine, axis=0, keepdims=True)
                pT[seq, place, :, at + tile : at + tile + 128] = jnp.exp2(
                    (mine - highest) * log2_e
                ).astype(bf16)
            if k:
                mix(*units[k - 1])
            if k in between:
                between[k]()
        mix(*units[-1])

    def dense(seq, side, at):
        slot = lax.rem(seq, 2)
        rows = tokens_at(at)
        branch = nn(wot[...], mixT[0:width, rows])
        firsts = []
        for half in halves:
            there = tokens_at(at, half.start, 128)
            hat, inverse = unit(
                xT[seq, 0:width, there].astype(f32) + branch[:, half] + bcol[0], width
            )
            hat1[side, :, half] = hat
            rinv1[side, 0:1, half] = inverse
            first = hat * bcol[1] + bcol[2]
            flow[0:width, there] = first.astype(bf16)
            firsts.append(first)
            yield
        inner = nn(wet[...], flow[0:width, rows])
        for half in halves:
            there = tokens_at(at, half.start, 128)
            for r in range(0, inner_width, 32):
                u = inner[r : r + 32, half] + be[r : r + 32, :]
                square = u * u
                t = jnp.tanh(u * (gelu_a + (gelu_a * gelu_b) * square))
                h = 0.5 + 0.5 * t
                value = u * h
                act[r : r + 32, there] = value.astype(bf16)
                dgelu[side, r : r + 32, half] = h + value * (1.0 - h) * (
                    2.0 * gelu_a + (6.0 * gelu_a * gelu_b) * square
                )
                if r % 256 == 224:
                    yield
        second = nn(wrt[...], act[0:inner_width, rows])
        grads, results, gains = [], [], []
        for k, half in enumerate(halves):
            there = tokens_at(at, half.start, 128)
            hat, inverse = unit(firsts[k] + second[:, half] + bcol[3], width)
            results.append((hat * bcol[4] + bcol[5]).astype(bf16))
            upstream = cT[seq, :, there].astype(f32)
            gains.append(upstream * hat)
            back = unit_back(upstream * bcol[4], hat, inverse, width)
            slow[:, there] = back.astype(bf16)
            grads.append(back)
            yield
        add_sums(0, gains[0] + gains[1])
        active_grad = nn(wr[...], slow[:, rows])
        land_x[slot, rows, :] = nt(identity, jnp.concatenate(results, axis=1)).astype(bf16)
        for half in halves:
            there = tokens_at(at, half.start, 128)
            for r in range(0, inner_width, 32):
                igr[r : r + 32, there] = (
                    active_grad[r : r + 32, half] * dgelu[side, r : r + 32, half]
                ).astype(bf16)
            yield
        deeper = nn(we[...], igr[:, rows])
        gains, shifts = [], []
        for k, half in enumerate(halves):
            there = tokens_at(at, half.start, 128)
            first_grad = grads[k] + deeper[:, half]
            hat = hat1[side, :, half]
            gains.append(first_grad * hat)
            shifts.append(first_grad)
            back = unit_back(first_grad * bcol[1], hat, rinv1[side, 0:1, half], width)
            blow[seq, :, there] = back.astype(bf16)
            yield
        add_sums(width, gains[0] + gains[1])
        add_sums(2 * width, shifts[0] + shifts[1])
        grown = nn(wo[...], blow[seq, :, rows]).astype(bf16).astype(f32)
        for head in range(HEADS):
            own = slice(head * HEAD_DIM, (head + 1) * HEAD_DIM)
            piece = grown[own, :] * inv[head : head + 1, rows]
            total = over_features(piece * mixT[own, rows].astype(f32))
            high = total.astype(bf16).astype(f32)
            dots[seq, 2 * head : 2 * head + 1, rows] = high
            dots[seq, 2 * head + 1 : 2 * head + 2, rows] = total - high
            doT[seq, own, rows] = piece.astype(bf16)
        yield

    def weight_sums(seq):
        gr[...] += nt(act[...], slow[...])
        ge[...] += nt(flow[...], igr[...])
        go[...] += nt(mixT[...], blow[seq])

    low_half = lax.broadcasted_iota(jnp.int32, (HALF, 128), 1) < HEAD_DIM
    keep = [low_half.astype(f32).astype(bf16), (~low_half).astype(f32).astype(bf16)]
    fill = [-keep[1], -keep[0]]
    extra_row = lax.broadcasted_iota(jnp.int32, (16, HALF), 0)

    def attend_back(seq, index):
        pair, block = index // blocks, index % blocks
        first = block * HALF
        lanes = slice(pair * 128, pair * 128 + 128)
        cols = tokens_at(first, 0, HALF)
        for odd in range(2):
            head = pair * 2 + odd
            own = slice(head * HEAD_DIM, (head + 1) * HEAD_DIM)
            key_rows = slice(width + own.start, width + own.stop)
            place = head * blocks + block
            high = dots[seq, 2 * head : 2 * head + 1, cols]
            rest = dots[seq, 2 * head + 1 : 2 * head + 2, cols]
            extra = jnp.where(extra_row == 0, high, jnp.where(extra_row == 1, rest, 0.0))
            extra = jnp.concatenate([extra, jnp.zeros((HEAD_DIM - 16, HALF), f32)], axis=0)
            grown = doT[seq, own, cols]
            stack = [grown, extra.astype(bf16)]
            if odd:
                stack = stack[::-1]
            stack = jnp.concatenate(stack, axis=0)
            side = vtok[seq, cols, lanes] * keep[odd] + fill[odd]
            for at in range(0, HALF, CHUNK):
                part = slice(at, at + CHUNK)
                grads = nn(side, stack[:, part])
                dsT[odd, :, part] = (pT[seq, place, :, part].astype(f32) * grads).astype(bf16)
                yield
            value_grad = nt(grown, pT[seq, place]).astype(bf16)
            yield
            key_grad = nt(qkT[seq, own, cols], dsT[odd]).astype(bf16)
            yield
            query_grad = (nn(qkT[seq, key_rows, cols], dsT[odd]) * scale).astype(bf16)
            yield
            doT[seq, own, cols] = value_grad
            qkT[seq, key_rows, cols] = key_grad
            qkT[seq, own, cols] = query_grad

    def joint_sums(seq, pair):
        for third in range(3):
            source = doT if third == 2 else qkT
            at = pair * 128 + (width if third == 1 else 0)
            lanes = slice(third * width + pair * 128, third * width + (pair + 1) * 128)
            gj[:, lanes] += nt(xT[seq], source[seq, at : at + 128, :])

    def together(*parts):
        parts = list(parts)
        while parts:
            for part in list(parts):
                if next(part, parts) is parts:
                    parts.remove(part)

    def chains(seq):
        def chain(side):
            chunk_count = length // CHUNK
            for index in range(side * chunk_count // 2, (side + 1) * chunk_count // 2):
                yield from dense(seq, side, index * CHUNK)

        return [chain(0), chain(1)]

    attend(0, {4: gather_b.third})
    gather_b.finish()
    unpack(
        held_b, 0, ((wo, wot, shards[1]), (we, wet, shards[2]), (wr, wrt, shards[3]))
    )
    together(*chains(0))
    weight_sums(0)
    out_copy(0).start()

    def middle(seq, carry):
        attend(seq)

        @pl.when(seq >= 2)
        def _():
            out_copy(seq - 2).wait()

        together(*chains(seq))
        weight_sums(seq)
        out_copy(seq).start()
        return carry

    lax.fori_loop(1, count, middle, 0)

    def pack(reduce, sources):
        for device in range(devices):
            outer = device // inners
            pieces = []
            for ref in sources:
                depth = ref.shape[0] // devices
                pieces += column_blocks(ref[device * depth : (device + 1) * depth, :])
            packed = reduce.packed
            packed[outer % 2, outer // 2, device % inners] = padded_rows(pieces, packed.shape[3])

    sum_a, sum_b, sum_c = Reduce(peers, *reduce_a), Reduce(peers, *reduce_b), Reduce(peers, *reduce_c)
    pack(sum_a, (go.at[0:width], ge.at[0:width], gr.at[0:inner_width]))
    sum_a.first()

    def joint_columns(pair):
        return [
            gj.at[0:width, third * width + pair * 128 : third * width + (pair + 1) * 128]
            for third in range(3)
        ]

    def back_of(pair, steps):
        def back(seq, carry):
            for block in range(blocks):
                together(attend_back(seq, pair * blocks + block))
            joint_sums(seq, pair)
            for at, step in steps.items():

                @pl.when(seq == min(at, count - 1))
                def _():
                    step()

            return carry

        lax.fori_loop(0, count, back, 0)

    back_of(0, {1: sum_a.second})
    pack(sum_b, joint_columns(0))
    sum_b.first()
    back_of(1, {0: sum_a.third, 1: sum_b.second})
    rows = [
        gj[width : width + 1, 0:width],
        gj[width : width + 1, 2 * width : 3 * width],
        go[width : width + 1, :],
        jnp.zeros((2, width), f32),
        gr[inner_width : inner_width + 1, :],
        jnp.zeros((1, width), f32),
        accc[0:1, :],
    ]
    missing = 128 - sum(row.shape[0] for row in rows)
    columns = jnp.concatenate(rows + [jnp.zeros((missing, width), f32)], axis=0).T
    lanes = lax.broadcasted_iota(jnp.int32, (width, 128), 1)
    for at, place in ((6, 0), (3, width), (4, 2 * width)):
        total = jnp.sum(accb[place : place + width, :], axis=1, keepdims=True)
        columns = jnp.where(lanes == at, total, columns)
    wide = jnp.broadcast_to(ge[width : width + 1, :], (128, inner_width)).T
    for first in range(2):
        item = [wide[k * share : (k + 1) * share] for k in range(first, 2 * devices, 2)]
        columns = jnp.where(lanes == VECTORS + first, jnp.concatenate(item, axis=0), columns)
    bcol[0] = columns
    pack(sum_c, [bcol.at[0]] + joint_columns(1))
    sum_c.first()

    def tg_copies(seq):
        slot = lax.rem(seq, 2)
        return [
            pltpu.make_async_copy(
                turn.at[slot * 2 + tile, pl.ds(0, length)],
                tg_hbm.at[seq, tile],
                tg_sem.at[slot, tile],
            )
            for tile in range(tiles)
        ]

    def inputs_back(seq, carry):
        @pl.when(seq >= 2)
        def _():
            for copy in tg_copies(seq - 2):
                copy.wait()

        slot = lax.rem(seq, 2)

        def one(index, at):
            rows = tokens_at(at)
            result = (
                nn(wj[:, 0 : 2 * width], qkT[seq, :, rows])
                + nn(wj[:, 2 * width : 3 * width], doT[seq, :, rows])
                + blow[seq, :, rows].astype(f32)
            ).T
            for tile in range(tiles):
                turn[slot * 2 + tile, rows, :] = result[:, tile * 128 : (tile + 1) * 128]

        chunks(one)
        for copy in tg_copies(seq):
            copy.start()

        @pl.when(seq == min(1, count - 1))
        def _():
            sum_b.third()

        @pl.when(seq == min(2, count - 1))
        def _():
            sum_c.second()

        return carry

    lax.fori_loop(0, count, inputs_back, 0)
    fin_a[...] = sum_a.finish()
    fin_b[...] = sum_b.finish()
    sum_c.third()
    fin_c[...] = sum_c.finish()
    for seq in range(max(count - 2, 0), count):
        out_copy(seq).wait()
        for copy in tg_copies(seq):
            copy.wait()


def run_layer(outers, inners, tokens, segment_ids, padding_mask, cotangent, shards):
    count, length, width = tokens.shape
    devices = outers * inners
    share = width // devices
    inner_width = shards[2].shape[1]
    tiles = width // 128
    chips = outers // 2
    blocks = length // HALF

    def rows_of(items):
        return sum(item.size // 128 for item in items)

    held_a = rounded_up(share + rows_of(shards[:1]), 16)
    held_b = rounded_up(rows_of(shards[1:4]), 16)
    dma = pltpu.SemaphoreType.DMA
    vmem = pltpu.VMEM
    shape = jax.ShapeDtypeStruct
    scratch = [vmem(item.shape, bf16) for item in shards]
    scratch += [
        vmem((2, length, width), bf16),
        vmem((2, length, width), bf16),
        vmem((count, length), jnp.int32),
        vmem((count, length), jnp.int32),
        vmem((width, 3 * width), bf16),
        vmem((width, width), bf16),
        vmem((width, inner_width), bf16),
        vmem((inner_width, width), bf16),
        vmem((3 * width, width), bf16),
        vmem((width, width), bf16),
        vmem((inner_width, width), bf16),
        vmem((width, inner_width), bf16),
        vmem((3 * width, 128), f32),
        vmem((inner_width, 128), f32),
        vmem((6, width, 128), f32),
        vmem((8, width), f32),
        vmem((2 * tiles, length + HALF, 128), f32),
        vmem((count, length, width), bf16),
        vmem((count, width + 16, length), bf16),
        vmem((count, width, length), bf16),
        vmem((count, length, 128), bf16),
        vmem((count, HEAD_DIM, length), bf16),
        vmem((count, 2 * width, length), bf16),
        vmem((width, length), bf16),
        vmem((HEADS, length, 128), bf16),
        vmem((count, length, width), bf16),
        vmem((count, HEADS * blocks, HALF, HALF), bf16),
        vmem((8, length), f32),
        vmem((width + 16, length), bf16),
        vmem((2, width, CHUNK), f32),
        vmem((2, 8, CHUNK), f32),
        vmem((inner_width + 16, length), bf16),
        vmem((width, length), bf16),
        vmem((inner_width, length), bf16),
        vmem((width + 16, length), bf16),
        vmem((count, width, length), bf16),
        vmem((2, inner_width, CHUNK), f32),
        vmem((2, HALF, HALF), bf16),
        vmem((count, 2 * HEADS, length), f32),
        vmem((width + 16, 3 * width), f32),
        vmem((width + 16, width), f32),
        vmem((width + 16, inner_width), f32),
        vmem((inner_width + 16, width), f32),
        vmem((3 * width, 128), f32),
        vmem((16, width), f32),
        vmem((2, chips, inners, held_a, 128), bf16),
        dma((inners + 2 * chips,)),
        dma((inners + 2 * chips,)),
        vmem((2, chips, inners, held_b, 128), bf16),
        dma((inners + 2 * chips,)),
        dma((inners + 2 * chips,)),
    ]
    sums_b = rounded_up(3 * share, 16)
    sums_c = rounded_up(4 * share, 16)
    for rows in (held_b, sums_b, sums_c):
        scratch += reduce_scratch(outers, inners, rows)
    scratch += [dma((len(shards) + 2,)), dma((2, 2)), dma((2,)), dma((2, tiles))]
    hbm = pl.BlockSpec(memory_space=pl.ANY)
    return pl.pallas_call(
        functools.partial(layer_kernel, outers, inners),
        in_specs=[pl.BlockSpec(memory_space=pltpu.SMEM)] + [hbm] * (4 + len(shards)),
        out_specs=[hbm, hbm] + [pl.BlockSpec(memory_space=pltpu.VMEM)] * 3,
        out_shape=[
            shape(tokens.shape, bf16),
            shape((count, tiles, length, 128), f32),
            shape((held_b, 128), f32),
            shape((sums_b, 128), f32),
            shape((sums_c, 128), f32),
        ],
        scratch_shapes=scratch,
        compiler_params=pltpu.CompilerParams(
            collective_id=0, has_side_effects=True, vmem_limit_bytes=64 * 1024 * 1024 - 65536
        ),
        name="layer",
    )(segment_ids, tokens, cotangent, segment_ids, padding_mask, *shards)


def finish_kernel(seg_smem, out_turned, tg_turned, fin_a, fin_b, fin_c, *refs):
    layer_out, tokens_grad, matrices, vectors = refs[0], refs[1], refs[2:6], refs[6:-2]
    plain, bent = refs[-2:]
    seq = pl.program_id(0)
    length, width = layer_out.shape[1], layer_out.shape[2]
    start = big_cell_start(seg_smem, seq, length)
    tiles = width // 128
    for tile in range(tiles):
        lanes = slice(tile * 128, (tile + 1) * 128)
        plain[tile] = out_turned[0, :, lanes].astype(f32)
        for k, source in enumerate((plain.at[tile], tg_turned.at[0, tile])):
            bent[k, tile, 0:CHUNK] = source[length - CHUNK : length]
            bent[k, tile, CHUNK : 2 * CHUNK] = source[0:CHUNK]
    for at in range(0, length, CHUNK):
        begin = lax.rem(length + at - start, length)

        def give(pieces):
            for tile in range(tiles):
                lanes = slice(tile * 128, (tile + 1) * 128)
                for k, target in enumerate((layer_out, tokens_grad)):
                    piece = pieces(k, tile)
                    target[0, at : at + CHUNK, lanes] = piece.astype(target.dtype)

        @pl.when(begin <= length - CHUNK)
        def _():
            whole = [lambda tile: plain.at[tile], lambda tile: tg_turned.at[0, tile]]
            give(lambda k, tile: whole[k](tile)[pl.ds(begin, CHUNK), :])

        @pl.when(begin > length - CHUNK)
        def _():
            give(lambda k, tile: bent[k, tile, pl.ds(begin - (length - CHUNK), CHUNK), :])

    @pl.when(seq == 0)
    def _():
        rows = vectors[0].shape[0]
        lines = fin_c[0:rows, :].T
        for at, ref in enumerate(vectors[:-1]):
            ref[...] = lines[at, :]
        vectors[-1][...] = jnp.concatenate([lines[VECTORS, :], lines[VECTORS + 1, :]])
        for third in range(3):
            for pair, (source, at) in enumerate(((fin_b, 0), (fin_c, rows))):
                column = (third * (HEADS // 2) + pair) * 128
                at += third * rows
                matrices[0][:, column : column + 128] = source[at : at + rows, :]
        at = 0
        for ref in matrices[1:]:
            depth = ref.shape[0]
            for column in range(0, ref.shape[1], 128):
                ref[:, column : column + 128] = fin_a[at : at + depth, :]
                at += depth


def finish(segment_ids, out_turned, tg_turned, fin_a, fin_b, fin_c, shards):
    count, length, width = out_turned.shape
    tiles = width // 128

    def whole(shape):
        return pl.BlockSpec(shape, lambda i: (0,) * len(shape))

    per_seq = pl.BlockSpec((1, length, width), lambda i: (i, 0, 0))
    shape = jax.ShapeDtypeStruct
    return pl.pallas_call(
        finish_kernel,
        grid=(count,),
        in_specs=[
            pl.BlockSpec(memory_space=pltpu.SMEM),
            per_seq,
            pl.BlockSpec((1, tiles, length, 128), lambda i: (i, 0, 0, 0)),
            whole(fin_a.shape),
            whole(fin_b.shape),
            whole(fin_c.shape),
        ],
        out_specs=[per_seq, per_seq] + [whole(item.shape) for item in shards],
        out_shape=[shape(out_turned.shape, bf16), shape(out_turned.shape, f32)]
        + [shape(item.shape, f32) for item in shards],
        scratch_shapes=[
            pltpu.VMEM((tiles, length, 128), f32),
            pltpu.VMEM((2, tiles, 2 * CHUNK, 128), f32),
        ],
        compiler_params=pltpu.CompilerParams(
            dimension_semantics=("arbitrary",), vmem_limit_bytes=60 * 1024 * 1024
        ),
        name="finish",
    )(segment_ids, out_turned, tg_turned, fin_a, fin_b, fin_c)


def on_device(
    outers,
    inners,
    tokens,
    segment_ids,
    padding_mask,
    joint_weight,
    query_bias,
    value_bias,
    output_weight,
    output_bias,
    first_gain,
    first_shift,
    expand_weight,
    expand_bias,
    reduce_weight,
    reduce_bias,
    second_gain,
    second_shift,
    cotangent,
):
    shards = (
        joint_weight,
        output_weight,
        expand_weight,
        reduce_weight,
        query_bias,
        value_bias,
        output_bias,
        first_gain,
        first_shift,
        reduce_bias,
        second_gain,
        second_shift,
        expand_bias,
    )
    turned = run_layer(outers, inners, tokens, segment_ids, padding_mask, cotangent, shards)
    layer_out, tokens_grad, *owned = finish(segment_ids, *turned, shards)
    gj, go, ge, gr, query, value, out, gain1, shift1, reduce, gain2, shift2, expand = owned
    return (
        layer_out,
        tokens_grad,
        gj,
        query,
        value,
        go,
        out,
        gain1,
        shift1,
        ge,
        expand,
        gr,
        reduce,
        gain2,
        shift2,
    )


def solution(mesh):
    rows = P(("outer", "inner"))
    rows2 = P(("outer", "inner"), None)
    rows3 = P(("outer", "inner"), None, None)
    weights = (rows2, rows, rows, rows2, rows, rows, rows, rows2, rows, rows2, rows, rows, rows)
    return jax.shard_map(
        functools.partial(on_device, mesh.shape["outer"], mesh.shape["inner"]),
        mesh=mesh,
        in_specs=(rows3, rows2, rows2) + weights + (rows3,),
        out_specs=(rows3, rows3) + weights,
        check_vma=False,
    )
```

```python
import functools
import math

import jax
import jax.numpy as jnp
from jax import lax
from jax.experimental import pallas as pl
from jax.experimental.pallas import tpu as pltpu
from jax.sharding import PartitionSpec as P

HEADS = 4
HEAD_DIM = 64
HALF = 512
CHUNK = 256
VECTORS = 8
MESH = pl.DeviceIdType.MESH

norm_epsilon = 1e-06
mask_step = -(2.0**100)
log2_e = math.log2(math.e)
gelu_a = math.sqrt(2.0 / math.pi)
gelu_b = 0.044715

f32 = jnp.float32
bf16 = jnp.bfloat16


def nn(left, right):
    return lax.dot_general(left, right, (((1,), (0,)), ((), ())), preferred_element_type=f32)


def nt(left, right):
    return lax.dot_general(left, right, (((1,), (1,)), ((), ())), preferred_element_type=f32)


def over_features(values):
    return jnp.sum(values, axis=0, keepdims=True)


def column_blocks(values):
    return [values[:, at : at + 128] for at in range(0, values.shape[1], 128)]


def padded_rows(pieces, rows):
    have = sum(piece.shape[0] for piece in pieces)
    if rows > have:
        pieces = pieces + [jnp.zeros((rows - have, 128), f32)]
    return jnp.concatenate(pieces, axis=0)


def rounded_up(amount, to):
    return (amount + to - 1) // to * to


def big_cell_start(seg_ref, seq, length):
    wanted = seg_ref[seq, HALF - 1]
    low = jnp.int32(0)
    step = HALF
    while step > 1:
        step //= 2
        probe = low + step
        low = jnp.where(seg_ref[seq, probe - 1] < wanted, probe, low)
    last = jnp.minimum(low + HALF - 1, length - 1)
    return jnp.where(seg_ref[seq, last] == wanted, low, HALF)


def copy_to(source, target, send, receive, outer, inner):
    return pltpu.make_async_remote_copy(
        src_ref=source,
        dst_ref=target,
        send_sem=send,
        recv_sem=receive,
        device_id=(outer, inner),
        device_id_type=MESH,
    )


class Peers:
    def __init__(self, outers, inners):
        self.outers, self.inners = outers, inners
        self.outer = lax.axis_index("outer")
        self.inner = lax.axis_index("inner")
        self.core = lax.rem(self.outer, 2)
        self.chip = lax.div(self.outer, 2)
        self.chips = outers // 2
        self.mate = self.chip * 2 + 1 - self.core

    def along_inner(self):
        return [lax.rem(self.inner + step, self.inners) for step in range(1, self.inners)]

    def along_chips(self):
        return [lax.rem(self.chip + step, self.chips) for step in range(1, self.chips)]

    def greet(self):
        barrier = pltpu.get_barrier_semaphore()
        others = [(self.outer, at) for at in self.along_inner()]
        others += [(at * 2 + self.core, self.inner) for at in self.along_chips()]
        others += [(self.mate, self.inner)]
        for other in others:
            pl.semaphore_signal(barrier, inc=1, device_id=other, device_id_type=MESH)

    def meet(self):
        pl.semaphore_wait(pltpu.get_barrier_semaphore(), self.inners - 1 + self.chips - 1 + 1)


class Gather:
    def __init__(self, peers, held, send, receive):
        self.peers, self.held, self.send, self.receive = peers, held, send, receive

    def one(self, at, spot, outer, inner):
        peers = self.peers
        block = self.held.at[peers.core, peers.chip, at]
        return copy_to(block, block, self.send.at[spot], self.receive.at[at], outer, inner)

    def block(self, core, chip, spot, signal, outer):
        peers = self.peers
        block = self.held.at[core, chip]
        signal = self.receive.at[peers.inners + signal]
        return copy_to(block, block, self.send.at[spot], signal, outer, peers.inner)

    def to_inner(self):
        peers = self.peers
        return [
            self.one(peers.inner, k, peers.outer, at) for k, at in enumerate(peers.along_inner())
        ]

    def to_chips(self):
        peers = self.peers
        return [
            self.block(peers.core, peers.chip, peers.inners + k, peers.chip, other * 2 + peers.core)
            for k, other in enumerate(peers.along_chips())
        ]

    def to_mate(self, k):
        peers = self.peers
        chip = ([peers.chip] + peers.along_chips())[k]
        spot = peers.inners + peers.chips + k
        return self.block(peers.core, chip, spot, peers.chips + chip, peers.mate)

    def first(self):
        for copy in self.to_inner():
            copy.start()

    def second(self):
        peers = self.peers
        for at in peers.along_inner():
            self.one(at, 0, peers.outer, peers.inner).wait_recv()
        for copy in self.to_chips() + [self.to_mate(0)]:
            copy.start()

    def third(self):
        peers = self.peers
        for k, other in enumerate(peers.along_chips()):
            self.block(peers.core, other, 0, other, peers.outer).wait_recv()
            self.to_mate(k + 1).start()

    def finish(self):
        peers = self.peers
        for chip in [peers.chip] + peers.along_chips():
            self.block(1 - peers.core, chip, 0, peers.chips + chip, peers.outer).wait_recv()
        for copy in (
            self.to_inner() + self.to_chips() + [self.to_mate(k) for k in range(peers.chips)]
        ):
            copy.wait_send()


class Reduce:
    def __init__(self, peers, packed, from_mate, mid, from_chips, last, from_inner, send, receive):
        self.peers, self.packed, self.from_mate = peers, packed, from_mate
        self.mid, self.from_chips, self.last = mid, from_chips, last
        self.from_inner, self.send, self.receive = from_inner, send, receive

    def to_mate(self):
        peers = self.peers
        return copy_to(
            self.packed.at[1 - peers.core],
            self.from_mate,
            self.send.at[0],
            self.receive.at[0],
            peers.mate,
            peers.inner,
        )

    def to_chips(self):
        peers = self.peers
        return [
            copy_to(
                self.mid.at[k],
                self.from_chips.at[k],
                self.send.at[1 + k],
                self.receive.at[1 + k],
                other * 2 + peers.core,
                peers.inner,
            )
            for k, other in enumerate(peers.along_chips())
        ]

    def to_inner(self):
        peers = self.peers
        return [
            copy_to(
                self.last.at[k],
                self.from_inner.at[k],
                self.send.at[peers.chips + k],
                self.receive.at[peers.chips + k],
                peers.outer,
                at,
            )
            for k, at in enumerate(peers.along_inner())
        ]

    def first(self):
        self.to_mate().start()

    def second(self):
        peers = self.peers
        self.to_mate().wait()
        for k, (other, copy) in enumerate(zip(peers.along_chips(), self.to_chips())):
            for at in range(peers.inners):
                total = self.packed[peers.core, other, at] + self.from_mate[other, at]
                self.mid[k, at] = total.astype(bf16)
            copy.start()

    def own(self, at):
        peers = self.peers
        total = self.packed[peers.core, peers.chip, at] + self.from_mate[peers.chip, at]
        for k in range(peers.chips - 1):
            total += self.from_chips[k, at].astype(f32)
        return total

    def third(self):
        for copy in self.to_chips():
            copy.wait()
        for k, (at, copy) in enumerate(zip(self.peers.along_inner(), self.to_inner())):
            self.last[k] = self.own(at).astype(bf16)
            copy.start()

    def finish(self):
        total = self.own(self.peers.inner)
        for k, copy in enumerate(self.to_inner()):
            copy.wait()
            total += self.from_inner[k].astype(f32)
        return total


def reduce_scratch(outers, inners, rows):
    chips = outers // 2
    return [
        pltpu.VMEM((2, chips, inners, rows, 128), f32),
        pltpu.VMEM((chips, inners, rows, 128), f32),
        pltpu.VMEM((max(chips - 1, 1), inners, rows, 128), bf16),
        pltpu.VMEM((max(chips - 1, 1), inners, rows, 128), bf16),
        pltpu.VMEM((inners - 1, rows, 128), bf16),
        pltpu.VMEM((inners - 1, rows, 128), bf16),
        pltpu.SemaphoreType.DMA((chips + inners,)),
        pltpu.SemaphoreType.DMA((chips + inners,)),
    ]


REDUCE_SCRATCH = 8


def unit(hidden, width):
    centred = hidden - over_features(hidden) * (1.0 / width)
    inverse = lax.rsqrt(over_features(centred * centred) * (1.0 / width) + norm_epsilon)
    return centred * inverse, inverse


def unit_back(inside, hat, inverse, width):
    return inverse * (
        inside
        - over_features(inside) * (1.0 / width)
        - hat * (over_features(inside * hat) * (1.0 / width))
    )


def layer_kernel(outers, inners, *refs):
    refs = list(refs)

    def grab(amount):
        taken = refs[:amount]
        del refs[:amount]
        return taken

    tokens_hbm, cot_hbm, seg_hbm, pad_hbm = grab(4)
    shard_hbm = grab(4 + VECTORS + 1)
    out_hbm, tg_hbm, fin_a, fin_b, fin_c = grab(5)
    shards = grab(4 + VECTORS + 1)
    land_x, land_c, segv, padv, seg_smem = grab(5)
    wj, wo, we, wr, wjt, wot, wet, wrt, bj, be, bcol, vrow = grab(12)
    turn, xtok, xT, cT, codek, codeq = grab(6)
    qkT, vT, kaug, vtok, pT, inv, mixT = grab(7)
    hat1, rinv1, act, slow, igr, flow, blow, dgelu, dsT = grab(9)
    (dots,) = grab(1)
    doT = cT
    gj, go, ge, gr, accb, accc = grab(6)
    held_a, send_a, receive_a, held_b, send_b, receive_b = grab(6)
    reduce_a, reduce_b, reduce_c = [grab(REDUCE_SCRATCH) for k in range(3)]
    shard_sem, land_sem, out_sem, tg_sem = grab(4)

    count, length, width = tokens_hbm.shape
    inner_width = we.shape[1]
    devices = outers * inners
    share = width // devices
    scale = HEAD_DIM**-0.5
    tiles = width // 128
    blocks = length // HALF
    peers = Peers(outers, inners)

    def land(seq):
        slot = lax.rem(seq, 2)
        return [
            pltpu.make_async_copy(tokens_hbm.at[seq], land_x.at[slot], land_sem.at[0, slot]),
            pltpu.make_async_copy(cot_hbm.at[seq], land_c.at[slot], land_sem.at[1, slot]),
        ]

    small = [
        pltpu.make_async_copy(source, target, shard_sem.at[k])
        for k, (source, target) in enumerate(
            zip(shard_hbm + [seg_hbm, pad_hbm, seg_hbm], shards + [segv, padv, seg_smem])
        )
    ]
    for copy in small:
        copy.start()
    peers.greet()
    for seq in range(min(2, count)):
        for copy in land(jnp.int32(seq)):
            copy.start()
    for copy in small:
        copy.wait()

    lines = [ref[...].astype(f32).reshape(1, ref.shape[0]) for ref in shards[4:]]
    lines = lines[:-1] + [lines[-1][:, :share], lines[-1][:, share:]]
    lines.append(jnp.zeros((128 - len(lines), share), f32))
    pieces = [jnp.concatenate(lines, axis=0).T] + column_blocks(shards[0][...].astype(f32))
    here = (peers.core, peers.chip, peers.inner)
    held_a[here] = padded_rows(pieces, held_a.shape[3]).astype(bf16)
    pieces = []
    for ref in shards[1:4]:
        pieces += column_blocks(ref[...].astype(f32))
    held_b[here] = padded_rows(pieces, held_b.shape[3]).astype(bf16)
    peers.meet()
    gather_a = Gather(peers, held_a, send_a, receive_a)
    gather_b = Gather(peers, held_b, send_b, receive_b)
    gather_a.first()

    identity = (
        lax.broadcasted_iota(jnp.int32, (CHUNK, CHUNK), 0)
        == lax.broadcasted_iota(jnp.int32, (CHUNK, CHUNK), 1)
    )
    identity = identity.astype(f32).astype(bf16)

    for ref in [mixT, act, flow] + [xT.at[seq] for seq in range(count)]:
        ref[ref.shape[0] - 16 : ref.shape[0], :] = jnp.ones((16, length), bf16)
    for ref in (gj, go, ge, gr, accb, accc):
        ref[...] = jnp.zeros_like(ref)
    some_ones = jnp.ones((16, CHUNK), bf16)

    def chunks(body):
        for index in range(length // CHUNK):
            body(index, index * CHUNK)

    def tokens_at(at, offset=0, size=CHUNK):
        return slice(at + offset, at + offset + size)

    def prepare(seq):
        for copy in land(seq):
            copy.wait()
        start = big_cell_start(seg_smem, seq, length)
        slot = lax.rem(seq, 2)

        def take(tile, at):
            return turn[tile, pl.ds(start + at, CHUNK), :]

        for k, source in enumerate((land_x, land_c)):

            def lay(index, at):
                for tile in range(tiles):
                    lanes = slice(tile * 128, (tile + 1) * 128)
                    piece = source[slot, tokens_at(at), lanes].astype(f32)
                    turn[2 * k + tile, tokens_at(at), :] = piece
                    if index < HALF // CHUNK:
                        turn[2 * k + tile, tokens_at(at, length), :] = piece

            chunks(lay)

        def bring(index, at):
            for k, target in enumerate((xT, cT)):
                piece = jnp.concatenate([take(2 * k + tile, at) for tile in range(tiles)], axis=1)
                piece = piece.astype(bf16)
                if k == 0:
                    xtok[seq, tokens_at(at), :] = piece
                else:
                    accc[...] += nn(some_ones, piece)
                target[seq, 0:width, tokens_at(at)] = nt(identity, piece).astype(bf16)

        chunks(bring)

        @pl.when(seq + 2 < count)
        def _():
            for copy in land(seq + 2):
                copy.start()

        def mark(index, at):
            position = at + lax.broadcasted_iota(jnp.int32, (1, CHUNK), 1)
            code = lax.broadcasted_iota(jnp.int32, (8, CHUNK), 0)
            hidden = (padv[pl.ds(seq, 1), tokens_at(at)] != 1).astype(f32)
            same = (segv[pl.ds(seq, 1), tokens_at(at)] == code).astype(f32)
            parts_q = [1.0 - same]
            parts_k = [same * mask_step]
            for digit in ((position // 64) % 8, (position // 8) % 8, position % 8):
                equal = (digit == code).astype(f32)
                parts_q.append(1.0 - equal)
                parts_k.append(equal * hidden * mask_step)
            both = jnp.concatenate(parts_k + parts_q + parts_k + parts_q, axis=0).astype(bf16)
            flat = nt(identity, both)
            turn[0, tokens_at(at), :] = flat
            if index < HALF // CHUNK:
                turn[0, tokens_at(at, length), :] = flat

        chunks(mark)
        nothing = jnp.zeros((32, CHUNK), f32)

        def bring_marks(index, at):
            piece = take(0, at).astype(bf16)
            codek[seq, tokens_at(at), :] = piece
            across = nt(identity[0:128, 0:128], piece)
            codeq[seq, :, tokens_at(at)] = jnp.concatenate([across[32:64], nothing], axis=0).astype(
                bf16
            )

        chunks(bring_marks)

    def prepare_step(seq, carry):
        prepare(seq)

        @pl.when(seq == 0)
        def _():
            gather_a.second()
            gather_b.first()

        if count > 1:

            @pl.when(seq == 1)
            def _():
                gather_a.third()

        if count > 2:

            @pl.when(seq == 2)
            def _():
                gather_b.second()

        return carry

    lax.fori_loop(0, count, prepare_step, 0)
    if count <= 1:
        gather_a.third()
    if count <= 2:
        gather_b.second()
    gather_a.finish()

    def stacked(held, at, depth):
        stack = []
        for device in range(devices):
            outer, inner = device // inners, device % inners
            stack.append(held[outer % 2, outer // 2, inner].astype(f32)[at : at + depth])
        return jnp.concatenate(stack, axis=0)

    columns = stacked(held_a, 0, share)
    def unpack(held, at, matrices):
        for straight, across, source in matrices:
            depth = source.shape[0]
            for column in range(0, straight.shape[1], 128):
                whole = stacked(held, at, depth)
                straight[:, column : column + 128] = whole.astype(bf16)
                if across is wjt and column < width:
                    whole = whole * scale
                across[column : column + 128, :] = whole.T.astype(bf16)
                at += depth

    unpack(held_a, share, ((wj, wjt, shards[0]),))

    def spread(at):
        return jnp.broadcast_to(columns[:, at : at + 1], (width, 128))

    bj[0:width, :] = spread(0) * scale
    bj[width : 2 * width, :] = jnp.zeros((width, 128), f32)
    bj[2 * width : 3 * width, :] = spread(1)
    for at in range(6):
        bcol[at, :, :] = spread(2 + at)
    halves = [spread(8), spread(9)]
    be[...] = jnp.concatenate(
        [halves[k % 2][k // 2 * share : (k // 2 + 1) * share] for k in range(2 * devices)], axis=0
    )
    vrow[...] = columns.T[0:8, :]

    lane = lax.broadcasted_iota(jnp.int32, (CHUNK, 128), 1)
    low_lanes = lane < HEAD_DIM
    halves = [slice(t, t + 128) for t in range(0, CHUNK, 128)]
    ones = jnp.ones((16, HALF), bf16)

    def add_sums(row, values):
        accb[row : row + values.shape[0], :] += values

    def out_copy(seq):
        return pltpu.make_async_copy(xtok.at[seq], out_hbm.at[seq], out_sem.at[seq])

    def attend(seq, between=()):
        between = dict(between)

        def project(index, at):
            made = nn(wjt[...], xT[seq, 0:width, tokens_at(at)])
            flat = nn(xtok[seq, tokens_at(at), :], wj[:, width : 3 * width])
            for half in halves:
                there = tokens_at(at, half.start, 128)
                low = (made[:, half] + bj[...]).astype(bf16)
                qkT[seq, :, there] = low[0 : 2 * width]
                vT[:, there] = low[2 * width : 3 * width]
            vtok[seq, tokens_at(at), :] = (flat[:, width : 2 * width] + vrow[1:2, :]).astype(bf16)
            codes = codek[seq, tokens_at(at), :].astype(f32)
            for head in range(HEADS):
                lanes = slice((head // 2) * 128, (head // 2 + 1) * 128)
                mine = low_lanes if head % 2 == 0 else ~low_lanes
                kaug[head, tokens_at(at), :] = jnp.where(mine, flat[:, lanes], codes).astype(bf16)

        chunks(project)

        units = [
            (head, block, at)
            for head in range(HEADS)
            for block in range(blocks)
            for at in range(0, HALF, CHUNK)
        ]

        def scores_of(head, block, at):
            there = tokens_at(block * HALF, at)
            own = slice(head * HEAD_DIM, (head + 1) * HEAD_DIM)
            parts = [qkT[seq, own, there], codeq[seq, :, there]]
            if head % 2:
                parts = parts[::-1]
            keys = kaug[head, tokens_at(block * HALF, 0, HALF), :]
            return nn(keys, jnp.concatenate(parts, axis=0))

        def mix(head, block, at):
            own = slice(head * HEAD_DIM, (head + 1) * HEAD_DIM)
            there = tokens_at(block * HALF, at)
            values = vT[own, tokens_at(block * HALF, 0, HALF)]
            mixed = nn(
                jnp.concatenate([values, ones], axis=0),
                pT[seq, head * blocks + block, :, at : at + CHUNK],
            )
            inverse = 1.0 / mixed[HEAD_DIM : HEAD_DIM + 1, :]
            inv[head : head + 1, there] = inverse
            mixT[own, there] = (mixed[0:HEAD_DIM, :] * inverse).astype(bf16)

        coming = scores_of(*units[0])
        for k, (head, block, at) in enumerate(units):
            scores = coming
            if k + 1 < len(units):
                coming = scores_of(*units[k + 1])
            place = head * blocks + block
            for tile in range(0, CHUNK, 128):
                mine = scores[:, tile : tile + 128]
                highest = jnp.max(mine, axis=0, keepdims=True)
                pT[seq, place, :, at + tile : at + tile + 128] = jnp.exp2(
                    (mine - highest) * log2_e
                ).astype(bf16)
            if k:
                mix(*units[k - 1])
            if k in between:
                between[k]()
        mix(*units[-1])

    def dense(seq, side, at):
        rows = tokens_at(at)
        branch = nn(wot[...], mixT[0:width, rows])
        firsts = []
        for half in halves:
            there = tokens_at(at, half.start, 128)
            hat, inverse = unit(
                xT[seq, 0:width, there].astype(f32) + branch[:, half] + bcol[0], width
            )
            hat1[side, :, half] = hat
            rinv1[side, 0:1, half] = inverse
            first = hat * bcol[1] + bcol[2]
            flow[0:width, there] = first.astype(bf16)
            firsts.append(first)
            yield
        inner = nn(wet[...], flow[0:width, rows])
        for half in halves:
            there = tokens_at(at, half.start, 128)
            for r in range(0, inner_width, 32):
                u = inner[r : r + 32, half] + be[r : r + 32, :]
                square = u * u
                t = jnp.tanh(u * (gelu_a + (gelu_a * gelu_b) * square))
                h = 0.5 + 0.5 * t
                value = u * h
                act[r : r + 32, there] = value.astype(bf16)
                dgelu[side, r : r + 32, half] = h + value * (1.0 - h) * (
                    2.0 * gelu_a + (6.0 * gelu_a * gelu_b) * square
                )
                if r % 256 == 224:
                    yield
        second = nn(wrt[...], act[0:inner_width, rows])
        grads, results, gains = [], [], []
        for k, half in enumerate(halves):
            there = tokens_at(at, half.start, 128)
            hat, inverse = unit(firsts[k] + second[:, half] + bcol[3], width)
            results.append((hat * bcol[4] + bcol[5]).astype(bf16))
            upstream = cT[seq, :, there].astype(f32)
            gains.append(upstream * hat)
            back = unit_back(upstream * bcol[4], hat, inverse, width)
            slow[:, there] = back.astype(bf16)
            grads.append(back)
            yield
        add_sums(0, gains[0] + gains[1])
        active_grad = nn(wr[...], slow[:, rows])
        xtok[seq, rows, :] = nt(identity, jnp.concatenate(results, axis=1)).astype(bf16)
        for half in halves:
            there = tokens_at(at, half.start, 128)
            for r in range(0, inner_width, 32):
                igr[r : r + 32, there] = (
                    active_grad[r : r + 32, half] * dgelu[side, r : r + 32, half]
                ).astype(bf16)
            yield
        deeper = nn(we[...], igr[:, rows])
        gains, shifts = [], []
        for k, half in enumerate(halves):
            there = tokens_at(at, half.start, 128)
            first_grad = grads[k] + deeper[:, half]
            hat = hat1[side, :, half]
            gains.append(first_grad * hat)
            shifts.append(first_grad)
            back = unit_back(first_grad * bcol[1], hat, rinv1[side, 0:1, half], width)
            blow[seq, :, there] = back.astype(bf16)
            yield
        add_sums(width, gains[0] + gains[1])
        add_sums(2 * width, shifts[0] + shifts[1])
        grown = nn(wo[...], blow[seq, :, rows]).astype(bf16).astype(f32)
        for head in range(HEADS):
            own = slice(head * HEAD_DIM, (head + 1) * HEAD_DIM)
            piece = grown[own, :] * inv[head : head + 1, rows]
            total = over_features(piece * mixT[own, rows].astype(f32))
            high = total.astype(bf16).astype(f32)
            dots[seq, 2 * head : 2 * head + 1, rows] = high
            dots[seq, 2 * head + 1 : 2 * head + 2, rows] = total - high
            doT[seq, own, rows] = piece.astype(bf16)
        yield

    def weight_sums(seq):
        gr[...] += nt(act[...], slow[...])
        ge[...] += nt(flow[...], igr[...])
        go[...] += nt(mixT[...], blow[seq])

    low_half = lax.broadcasted_iota(jnp.int32, (HALF, 128), 1) < HEAD_DIM
    keep = [low_half.astype(f32).astype(bf16), (~low_half).astype(f32).astype(bf16)]
    fill = [-keep[1], -keep[0]]
    extra_row = lax.broadcasted_iota(jnp.int32, (16, HALF), 0)

    def attend_back(seq, index):
        pair, block = index // blocks, index % blocks
        first = block * HALF
        lanes = slice(pair * 128, pair * 128 + 128)
        cols = tokens_at(first, 0, HALF)
        for odd in range(2):
            head = pair * 2 + odd
            own = slice(head * HEAD_DIM, (head + 1) * HEAD_DIM)
            key_rows = slice(width + own.start, width + own.stop)
            place = head * blocks + block
            high = dots[seq, 2 * head : 2 * head + 1, cols]
            rest = dots[seq, 2 * head + 1 : 2 * head + 2, cols]
            extra = jnp.where(extra_row == 0, high, jnp.where(extra_row == 1, rest, 0.0))
            extra = jnp.concatenate([extra, jnp.zeros((HEAD_DIM - 16, HALF), f32)], axis=0)
            grown = doT[seq, own, cols]
            stack = [grown, extra.astype(bf16)]
            if odd:
                stack = stack[::-1]
            stack = jnp.concatenate(stack, axis=0)
            side = vtok[seq, cols, lanes] * keep[odd] + fill[odd]
            for at in range(0, HALF, CHUNK):
                part = slice(at, at + CHUNK)
                grads = nn(side, stack[:, part])
                dsT[odd, :, part] = (pT[seq, place, :, part].astype(f32) * grads).astype(bf16)
                yield
            value_grad = nt(grown, pT[seq, place]).astype(bf16)
            yield
            key_grad = nt(qkT[seq, own, cols], dsT[odd]).astype(bf16)
            yield
            query_grad = (nn(qkT[seq, key_rows, cols], dsT[odd]) * scale).astype(bf16)
            yield
            doT[seq, own, cols] = value_grad
            qkT[seq, key_rows, cols] = key_grad
            qkT[seq, own, cols] = query_grad

    def joint_sums(seq, pair):
        for third in range(3):
            source = doT if third == 2 else qkT
            at = pair * 128 + (width if third == 1 else 0)
            lanes = slice(third * width + pair * 128, third * width + (pair + 1) * 128)
            gj[:, lanes] += nt(xT[seq], source[seq, at : at + 128, :])

    def together(*parts):
        parts = list(parts)
        while parts:
            for part in list(parts):
                if next(part, parts) is parts:
                    parts.remove(part)

    def chains(seq):
        def chain(side):
            chunk_count = length // CHUNK
            for index in range(side * chunk_count // 2, (side + 1) * chunk_count // 2):
                yield from dense(seq, side, index * CHUNK)

        return [chain(0), chain(1)]

    attend(0, {4: gather_b.third})
    gather_b.finish()
    unpack(
        held_b, 0, ((wo, wot, shards[1]), (we, wet, shards[2]), (wr, wrt, shards[3]))
    )
    together(*chains(0))
    weight_sums(0)

    def middle(seq, carry):
        attend(seq)
        together(*chains(seq))
        weight_sums(seq)
        return carry

    lax.fori_loop(1, count, middle, 0)

    def pack(reduce, sources):
        for device in range(devices):
            outer = device // inners
            pieces = []
            for ref in sources:
                depth = ref.shape[0] // devices
                pieces += column_blocks(ref[device * depth : (device + 1) * depth, :])
            packed = reduce.packed
            packed[outer % 2, outer // 2, device % inners] = padded_rows(pieces, packed.shape[3])

    sum_a, sum_b, sum_c = Reduce(peers, *reduce_a), Reduce(peers, *reduce_b), Reduce(peers, *reduce_c)
    pack(sum_a, (go.at[0:width], ge.at[0:width], gr.at[0:inner_width]))
    sum_a.first()

    def joint_columns(pair):
        return [
            gj.at[0:width, third * width + pair * 128 : third * width + (pair + 1) * 128]
            for third in range(3)
        ]

    def back_of(pair, steps):
        def back(seq, carry):
            for block in range(blocks):
                together(attend_back(seq, pair * blocks + block))
            joint_sums(seq, pair)
            for at, step in steps.items():

                @pl.when(seq == min(at, count - 1))
                def _():
                    step()

            return carry

        lax.fori_loop(0, count, back, 0)

    back_of(0, {1: sum_a.second})
    pack(sum_b, joint_columns(0))
    sum_b.first()
    back_of(1, {0: sum_a.third, 1: sum_b.second})
    rows = [
        gj[width : width + 1, 0:width],
        gj[width : width + 1, 2 * width : 3 * width],
        go[width : width + 1, :],
        jnp.zeros((2, width), f32),
        gr[inner_width : inner_width + 1, :],
        jnp.zeros((1, width), f32),
        accc[0:1, :],
    ]
    missing = 128 - sum(row.shape[0] for row in rows)
    columns = jnp.concatenate(rows + [jnp.zeros((missing, width), f32)], axis=0).T
    lanes = lax.broadcasted_iota(jnp.int32, (width, 128), 1)
    for at, place in ((6, 0), (3, width), (4, 2 * width)):
        total = jnp.sum(accb[place : place + width, :], axis=1, keepdims=True)
        columns = jnp.where(lanes == at, total, columns)
    wide = jnp.broadcast_to(ge[width : width + 1, :], (128, inner_width)).T
    for first in range(2):
        item = [wide[k * share : (k + 1) * share] for k in range(first, 2 * devices, 2)]
        columns = jnp.where(lanes == VECTORS + first, jnp.concatenate(item, axis=0), columns)
    bcol[0] = columns
    pack(sum_c, [bcol.at[0]] + joint_columns(1))
    sum_c.first()

    def tg_copies(seq):
        return [
            pltpu.make_async_copy(
                turn.at[tiles + tile, pl.ds(0, length)],
                tg_hbm.at[seq, :, pl.ds(tile * 128, 128)],
                tg_sem.at[tile],
            )
            for tile in range(tiles)
        ]

    def turn_back(tile, at, piece):
        turn[tile, HALF + at : HALF + at + CHUNK, :] = piece
        if at >= HALF:
            turn[tile, at - HALF : at - HALF + CHUNK, :] = piece

    def inputs_back(seq, carry):
        start = big_cell_start(seg_smem, seq, length)

        def give_back(tile, at):
            return turn[tile, pl.ds(HALF - start + at, CHUNK), :]

        def lay(index, at):
            for tile in range(tiles):
                lanes = slice(tile * 128, (tile + 1) * 128)
                turn_back(tile, at, xtok[seq, tokens_at(at), lanes].astype(f32))

        def give_out(index, at):
            for tile in range(tiles):
                lanes = slice(tile * 128, (tile + 1) * 128)
                xtok[seq, tokens_at(at), lanes] = give_back(tile, at).astype(bf16)

        chunks(lay)
        chunks(give_out)
        out_copy(seq).start()

        @pl.when(seq >= 1)
        def _():
            for copy in tg_copies(seq - 1):
                copy.wait()

        def one(index, at):
            rows = tokens_at(at)
            result = (
                nn(wj[:, 0 : 2 * width], qkT[seq, :, rows])
                + nn(wj[:, 2 * width : 3 * width], doT[seq, :, rows])
                + blow[seq, :, rows].astype(f32)
            ).T
            for tile in range(tiles):
                turn_back(tile, at, result[:, tile * 128 : (tile + 1) * 128])

        def give_grad(index, at):
            for tile in range(tiles):
                turn[tiles + tile, tokens_at(at), :] = give_back(tile, at)

        chunks(one)
        chunks(give_grad)
        for copy in tg_copies(seq):
            copy.start()

        @pl.when(seq == 0)
        def _():
            sum_b.third()
            sum_c.second()

        if count > 2:

            @pl.when(seq == 2)
            def _():
                sum_c.third()

        return carry

    lax.fori_loop(0, count, inputs_back, 0)
    if count <= 2:
        sum_c.third()
    fin_a[...] = sum_a.finish()
    fin_b[...] = sum_b.finish()
    fin_c[...] = sum_c.finish()
    for seq in range(count):
        out_copy(seq).wait()
    for copy in tg_copies(count - 1):
        copy.wait()


def run_layer(outers, inners, tokens, segment_ids, padding_mask, cotangent, shards):
    count, length, width = tokens.shape
    devices = outers * inners
    share = width // devices
    inner_width = shards[2].shape[1]
    tiles = width // 128
    chips = outers // 2
    blocks = length // HALF

    def rows_of(items):
        return sum(item.size // 128 for item in items)

    held_a = rounded_up(share + rows_of(shards[:1]), 16)
    held_b = rounded_up(rows_of(shards[1:4]), 16)
    dma = pltpu.SemaphoreType.DMA
    vmem = pltpu.VMEM
    shape = jax.ShapeDtypeStruct
    scratch = [vmem(item.shape, bf16) for item in shards]
    scratch += [
        vmem((2, length, width), bf16),
        vmem((2, length, width), bf16),
        vmem((count, length), jnp.int32),
        vmem((count, length), jnp.int32),
        pltpu.SMEM((count, length), jnp.int32),
        vmem((width, 3 * width), bf16),
        vmem((width, width), bf16),
        vmem((width, inner_width), bf16),
        vmem((inner_width, width), bf16),
        vmem((3 * width, width), bf16),
        vmem((width, width), bf16),
        vmem((inner_width, width), bf16),
        vmem((width, inner_width), bf16),
        vmem((3 * width, 128), f32),
        vmem((inner_width, 128), f32),
        vmem((6, width, 128), f32),
        vmem((8, width), f32),
        vmem((2 * tiles, length + HALF, 128), f32),
        vmem((count, length, width), bf16),
        vmem((count, width + 16, length), bf16),
        vmem((count, width, length), bf16),
        vmem((count, length, 128), bf16),
        vmem((count, HEAD_DIM, length), bf16),
        vmem((count, 2 * width, length), bf16),
        vmem((width, length), bf16),
        vmem((HEADS, length, 128), bf16),
        vmem((count, length, width), bf16),
        vmem((count, HEADS * blocks, HALF, HALF), bf16),
        vmem((8, length), f32),
        vmem((width + 16, length), bf16),
        vmem((2, width, CHUNK), f32),
        vmem((2, 8, CHUNK), f32),
        vmem((inner_width + 16, length), bf16),
        vmem((width, length), bf16),
        vmem((inner_width, length), bf16),
        vmem((width + 16, length), bf16),
        vmem((count, width, length), bf16),
        vmem((2, inner_width, CHUNK), f32),
        vmem((2, HALF, HALF), bf16),
        vmem((count, 2 * HEADS, length), f32),
        vmem((width + 16, 3 * width), f32),
        vmem((width + 16, width), f32),
        vmem((width + 16, inner_width), f32),
        vmem((inner_width + 16, width), f32),
        vmem((3 * width, 128), f32),
        vmem((16, width), f32),
        vmem((2, chips, inners, held_a, 128), bf16),
        dma((inners + 2 * chips,)),
        dma((inners + 2 * chips,)),
        vmem((2, chips, inners, held_b, 128), bf16),
        dma((inners + 2 * chips,)),
        dma((inners + 2 * chips,)),
    ]
    sums_b = rounded_up(3 * share, 16)
    sums_c = rounded_up(4 * share, 16)
    for rows in (held_b, sums_b, sums_c):
        scratch += reduce_scratch(outers, inners, rows)
    scratch += [dma((len(shards) + 3,)), dma((2, 2)), dma((count,)), dma((tiles,))]
    hbm = pl.BlockSpec(memory_space=pl.ANY)
    return pl.pallas_call(
        functools.partial(layer_kernel, outers, inners),
        in_specs=[hbm] * (4 + len(shards)),
        out_specs=[hbm, hbm] + [pl.BlockSpec(memory_space=pltpu.VMEM)] * 3,
        out_shape=[
            shape(tokens.shape, bf16),
            shape(tokens.shape, f32),
            shape((held_b, 128), f32),
            shape((sums_b, 128), f32),
            shape((sums_c, 128), f32),
        ],
        scratch_shapes=scratch,
        compiler_params=pltpu.CompilerParams(
            collective_id=0, has_side_effects=True, vmem_limit_bytes=64 * 1024 * 1024 - 65536
        ),
        name="layer",
    )(tokens, cotangent, segment_ids, padding_mask, *shards)


def finish_kernel(out_made, tg_made, fin_a, fin_b, fin_c, *refs):
    layer_out, tokens_grad, matrices, vectors, sems = *refs[:2], refs[2:6], refs[6:-1], refs[-1]
    count = layer_out.shape[0]
    copies = [
        pltpu.make_async_copy(source.at[seq], target.at[seq], sems.at[k, seq])
        for seq in range(count)
        for k, (source, target) in enumerate(((tg_made, tokens_grad), (out_made, layer_out)))
    ]
    for copy in copies:
        copy.start()
    rows = vectors[0].shape[0]
    lines = fin_c[0:rows, :].T
    for at, ref in enumerate(vectors[:-1]):
        ref[...] = lines[at, :]
    vectors[-1][...] = jnp.concatenate([lines[VECTORS, :], lines[VECTORS + 1, :]])
    for third in range(3):
        for pair, (source, at) in enumerate(((fin_b, 0), (fin_c, rows))):
            column = (third * (HEADS // 2) + pair) * 128
            at += third * rows
            matrices[0][:, column : column + 128] = source[at : at + rows, :]
    at = 0
    for ref in matrices[1:]:
        depth = ref.shape[0]
        for column in range(0, ref.shape[1], 128):
            ref[:, column : column + 128] = fin_a[at : at + depth, :]
            at += depth
    for copy in copies:
        copy.wait()


def finish(out_made, tg_made, fin_a, fin_b, fin_c, shards):
    hbm = pl.BlockSpec(memory_space=pl.ANY)
    vmem = pl.BlockSpec(memory_space=pltpu.VMEM)
    shape = jax.ShapeDtypeStruct
    return pl.pallas_call(
        finish_kernel,
        in_specs=[hbm, hbm] + [vmem] * 3,
        out_specs=[hbm, hbm] + [vmem] * len(shards),
        out_shape=[shape(out_made.shape, bf16), shape(tg_made.shape, f32)]
        + [shape(item.shape, f32) for item in shards],
        scratch_shapes=[pltpu.SemaphoreType.DMA((2, out_made.shape[0]))],
        compiler_params=pltpu.CompilerParams(vmem_limit_bytes=60 * 1024 * 1024),
        name="finish",
    )(out_made, tg_made, fin_a, fin_b, fin_c)


def on_device(
    outers,
    inners,
    tokens,
    segment_ids,
    padding_mask,
    joint_weight,
    query_bias,
    value_bias,
    output_weight,
    output_bias,
    first_gain,
    first_shift,
    expand_weight,
    expand_bias,
    reduce_weight,
    reduce_bias,
    second_gain,
    second_shift,
    cotangent,
):
    shards = (
        joint_weight,
        output_weight,
        expand_weight,
        reduce_weight,
        query_bias,
        value_bias,
        output_bias,
        first_gain,
        first_shift,
        reduce_bias,
        second_gain,
        second_shift,
        expand_bias,
    )
    turned = run_layer(outers, inners, tokens, segment_ids, padding_mask, cotangent, shards)
    layer_out, tokens_grad, *owned = finish(*turned, shards)
    gj, go, ge, gr, query, value, out, gain1, shift1, reduce, gain2, shift2, expand = owned
    return (
        layer_out,
        tokens_grad,
        gj,
        query,
        value,
        go,
        out,
        gain1,
        shift1,
        ge,
        expand,
        gr,
        reduce,
        gain2,
        shift2,
    )


def solution(mesh):
    rows = P(("outer", "inner"))
    rows2 = P(("outer", "inner"), None)
    rows3 = P(("outer", "inner"), None, None)
    weights = (rows2, rows, rows, rows2, rows, rows, rows, rows2, rows, rows2, rows, rows, rows)
    return jax.shard_map(
        functools.partial(on_device, mesh.shape["outer"], mesh.shape["inner"]),
        mesh=mesh,
        in_specs=(rows3, rows2, rows2) + weights + (rows3,),
        out_specs=(rows3, rows3) + weights,
        check_vma=False,
    )
```

```python
import functools
import math

import jax
import jax.numpy as jnp
from jax import lax
from jax.experimental import pallas as pl
from jax.experimental.pallas import tpu as pltpu
from jax.sharding import PartitionSpec as P

HEADS = 4
HEAD_DIM = 64
HALF = 512
CHUNK = 256
VECTORS = 8
MESH = pl.DeviceIdType.MESH

norm_epsilon = 1e-06
mask_step = -(2.0**100)
log2_e = math.log2(math.e)
gelu_a = math.sqrt(2.0 / math.pi)
gelu_b = 0.044715

f32 = jnp.float32
bf16 = jnp.bfloat16


def nn(left, right):
    return lax.dot_general(left, right, (((1,), (0,)), ((), ())), preferred_element_type=f32)


def nt(left, right):
    return lax.dot_general(left, right, (((1,), (1,)), ((), ())), preferred_element_type=f32)


def over_features(values):
    return jnp.sum(values, axis=0, keepdims=True)


def column_blocks(values):
    return [values[:, at : at + 128] for at in range(0, values.shape[1], 128)]


def padded_rows(pieces, rows):
    have = sum(piece.shape[0] for piece in pieces)
    if rows > have:
        pieces = pieces + [jnp.zeros((rows - have, 128), f32)]
    return jnp.concatenate(pieces, axis=0)


def rounded_up(amount, to):
    return (amount + to - 1) // to * to


def big_cell_start(seg_ref, seq, length):
    wanted = seg_ref[seq, HALF - 1]
    low = jnp.int32(0)
    step = HALF
    while step > 1:
        step //= 2
        probe = low + step
        low = jnp.where(seg_ref[seq, probe - 1] < wanted, probe, low)
    last = jnp.minimum(low + HALF - 1, length - 1)
    return jnp.where(seg_ref[seq, last] == wanted, low, HALF)


def copy_to(source, target, send, receive, outer, inner):
    return pltpu.make_async_remote_copy(
        src_ref=source,
        dst_ref=target,
        send_sem=send,
        recv_sem=receive,
        device_id=(outer, inner),
        device_id_type=MESH,
    )


class Peers:
    def __init__(self, outers, inners):
        self.outers, self.inners = outers, inners
        self.outer = lax.axis_index("outer")
        self.inner = lax.axis_index("inner")
        self.core = lax.rem(self.outer, 2)
        self.chip = lax.div(self.outer, 2)
        self.chips = outers // 2
        self.mate = self.chip * 2 + 1 - self.core

    def along_inner(self):
        return [lax.rem(self.inner + step, self.inners) for step in range(1, self.inners)]

    def along_chips(self):
        return [lax.rem(self.chip + step, self.chips) for step in range(1, self.chips)]

    def greet(self):
        barrier = pltpu.get_barrier_semaphore()
        others = [(self.outer, at) for at in self.along_inner()]
        others += [(at * 2 + self.core, self.inner) for at in self.along_chips()]
        others += [(self.mate, self.inner)]
        for other in others:
            pl.semaphore_signal(barrier, inc=1, device_id=other, device_id_type=MESH)

    def meet(self):
        pl.semaphore_wait(pltpu.get_barrier_semaphore(), self.inners - 1 + self.chips - 1 + 1)


class Gather:
    def __init__(self, peers, held, send, receive):
        self.peers, self.held, self.send, self.receive = peers, held, send, receive

    def one(self, at, spot, outer, inner):
        peers = self.peers
        block = self.held.at[peers.core, peers.chip, at]
        return copy_to(block, block, self.send.at[spot], self.receive.at[at], outer, inner)

    def block(self, core, chip, spot, signal, outer):
        peers = self.peers
        block = self.held.at[core, chip]
        signal = self.receive.at[peers.inners + signal]
        return copy_to(block, block, self.send.at[spot], signal, outer, peers.inner)

    def to_inner(self):
        peers = self.peers
        return [
            self.one(peers.inner, k, peers.outer, at) for k, at in enumerate(peers.along_inner())
        ]

    def to_chips(self):
        peers = self.peers
        return [
            self.block(peers.core, peers.chip, peers.inners + k, peers.chip, other * 2 + peers.core)
            for k, other in enumerate(peers.along_chips())
        ]

    def to_mate(self, k):
        peers = self.peers
        chip = ([peers.chip] + peers.along_chips())[k]
        spot = peers.inners + peers.chips + k
        return self.block(peers.core, chip, spot, peers.chips + chip, peers.mate)

    def first(self):
        for copy in self.to_inner():
            copy.start()

    def second(self):
        peers = self.peers
        for at in peers.along_inner():
            self.one(at, 0, peers.outer, peers.inner).wait_recv()
        for copy in self.to_chips() + [self.to_mate(0)]:
            copy.start()

    def third(self):
        peers = self.peers
        for k, other in enumerate(peers.along_chips()):
            self.block(peers.core, other, 0, other, peers.outer).wait_recv()
            self.to_mate(k + 1).start()

    def finish(self):
        peers = self.peers
        for chip in [peers.chip] + peers.along_chips():
            self.block(1 - peers.core, chip, 0, peers.chips + chip, peers.outer).wait_recv()
        for copy in (
            self.to_inner() + self.to_chips() + [self.to_mate(k) for k in range(peers.chips)]
        ):
            copy.wait_send()


class Reduce:
    def __init__(self, peers, packed, from_mate, mid, from_chips, last, from_inner, send, receive):
        self.peers, self.packed, self.from_mate = peers, packed, from_mate
        self.mid, self.from_chips, self.last = mid, from_chips, last
        self.from_inner, self.send, self.receive = from_inner, send, receive

    def to_mate(self):
        peers = self.peers
        return copy_to(
            self.packed.at[1 - peers.core],
            self.from_mate,
            self.send.at[0],
            self.receive.at[0],
            peers.mate,
            peers.inner,
        )

    def to_chips(self):
        peers = self.peers
        return [
            copy_to(
                self.mid.at[k],
                self.from_chips.at[k],
                self.send.at[1 + k],
                self.receive.at[1 + k],
                other * 2 + peers.core,
                peers.inner,
            )
            for k, other in enumerate(peers.along_chips())
        ]

    def to_inner(self):
        peers = self.peers
        return [
            copy_to(
                self.last.at[k],
                self.from_inner.at[k],
                self.send.at[peers.chips + k],
                self.receive.at[peers.chips + k],
                peers.outer,
                at,
            )
            for k, at in enumerate(peers.along_inner())
        ]

    def first(self):
        self.to_mate().start()

    def second(self):
        peers = self.peers
        self.to_mate().wait()
        for k, (other, copy) in enumerate(zip(peers.along_chips(), self.to_chips())):
            for at in range(peers.inners):
                total = self.packed[peers.core, other, at] + self.from_mate[other, at]
                self.mid[k, at] = total.astype(bf16)
            copy.start()

    def own(self, at):
        peers = self.peers
        total = self.packed[peers.core, peers.chip, at] + self.from_mate[peers.chip, at]
        for k in range(peers.chips - 1):
            total += self.from_chips[k, at].astype(f32)
        return total

    def third(self):
        for copy in self.to_chips():
            copy.wait()
        for k, (at, copy) in enumerate(zip(self.peers.along_inner(), self.to_inner())):
            self.last[k] = self.own(at).astype(bf16)
            copy.start()

    def finish(self):
        total = self.own(self.peers.inner)
        for k, copy in enumerate(self.to_inner()):
            copy.wait()
            total += self.from_inner[k].astype(f32)
        return total


def reduce_scratch(outers, inners, rows):
    chips = outers // 2
    return [
        pltpu.VMEM((2, chips, inners, rows, 128), f32),
        pltpu.VMEM((chips, inners, rows, 128), f32),
        pltpu.VMEM((max(chips - 1, 1), inners, rows, 128), bf16),
        pltpu.VMEM((max(chips - 1, 1), inners, rows, 128), bf16),
        pltpu.VMEM((inners - 1, rows, 128), bf16),
        pltpu.VMEM((inners - 1, rows, 128), bf16),
        pltpu.SemaphoreType.DMA((chips + inners,)),
        pltpu.SemaphoreType.DMA((chips + inners,)),
    ]


REDUCE_SCRATCH = 8


def unit(hidden, width):
    centred = hidden - over_features(hidden) * (1.0 / width)
    inverse = lax.rsqrt(over_features(centred * centred) * (1.0 / width) + norm_epsilon)
    return centred * inverse, inverse


def unit_back(inside, hat, inverse, width):
    return inverse * (
        inside
        - over_features(inside) * (1.0 / width)
        - hat * (over_features(inside * hat) * (1.0 / width))
    )


def layer_kernel(outers, inners, *refs):
    refs = list(refs)

    def grab(amount):
        taken = refs[:amount]
        del refs[:amount]
        return taken

    tokens_hbm, cot_hbm, seg_hbm, pad_hbm = grab(4)
    shard_hbm = grab(4 + VECTORS + 1)
    out_hbm, tg_hbm, fin_a, fin_b, fin_c = grab(5)
    shards = grab(4 + VECTORS + 1)
    land_x, land_c, segv, padv, seg_smem = grab(5)
    wj, wo, we, wr, wjt, wot, wet, wrt, bj, be, bcol, vrow = grab(12)
    turn, xtok, xT, cT, codek, codeq = grab(6)
    qkT, vT, kaug, vtok, pT, inv, mixT = grab(7)
    hat1, rinv1, act, slow, igr, flow, blow, dgelu, dsT = grab(9)
    (dots,) = grab(1)
    doT = cT
    gj, go, ge, gr, accb, accc = grab(6)
    held_a, send_a, receive_a, held_b, send_b, receive_b = grab(6)
    reduce_a, reduce_b, reduce_c = [grab(REDUCE_SCRATCH) for k in range(3)]
    shard_sem, land_sem, out_sem, tg_sem = grab(4)

    count, length, width = tokens_hbm.shape
    inner_width = we.shape[1]
    devices = outers * inners
    share = width // devices
    scale = HEAD_DIM**-0.5
    tiles = width // 128
    blocks = length // HALF
    peers = Peers(outers, inners)

    def land(seq):
        slot = lax.rem(seq, 2)
        return [
            pltpu.make_async_copy(tokens_hbm.at[seq], land_x.at[slot], land_sem.at[0, slot]),
            pltpu.make_async_copy(cot_hbm.at[seq], land_c.at[slot], land_sem.at[1, slot]),
        ]

    small = [
        pltpu.make_async_copy(source, target, shard_sem.at[k])
        for k, (source, target) in enumerate(
            zip(shard_hbm + [seg_hbm, pad_hbm, seg_hbm], shards + [segv, padv, seg_smem])
        )
    ]
    for copy in small:
        copy.start()
    peers.greet()
    for seq in range(min(2, count)):
        for copy in land(jnp.int32(seq)):
            copy.start()
    for copy in small:
        copy.wait()

    lines = [ref[...].astype(f32).reshape(1, ref.shape[0]) for ref in shards[4:]]
    lines = lines[:-1] + [lines[-1][:, :share], lines[-1][:, share:]]
    lines.append(jnp.zeros((128 - len(lines), share), f32))
    pieces = [jnp.concatenate(lines, axis=0).T] + column_blocks(shards[0][...].astype(f32))
    here = (peers.core, peers.chip, peers.inner)
    held_a[here] = padded_rows(pieces, held_a.shape[3]).astype(bf16)
    pieces = []
    for ref in shards[1:4]:
        pieces += column_blocks(ref[...].astype(f32))
    held_b[here] = padded_rows(pieces, held_b.shape[3]).astype(bf16)
    peers.meet()
    gather_a = Gather(peers, held_a, send_a, receive_a)
    gather_b = Gather(peers, held_b, send_b, receive_b)
    gather_a.first()

    identity = (
        lax.broadcasted_iota(jnp.int32, (CHUNK, CHUNK), 0)
        == lax.broadcasted_iota(jnp.int32, (CHUNK, CHUNK), 1)
    )
    identity = identity.astype(f32).astype(bf16)

    for ref in [mixT, act, flow] + [xT.at[seq] for seq in range(count)]:
        ref[ref.shape[0] - 16 : ref.shape[0], :] = jnp.ones((16, length), bf16)
    for ref in (gj, go, ge, gr, accb, accc):
        ref[...] = jnp.zeros_like(ref)
    some_ones = jnp.ones((16, CHUNK), bf16)

    def chunks(body):
        for index in range(length // CHUNK):
            body(index, index * CHUNK)

    def tokens_at(at, offset=0, size=CHUNK):
        return slice(at + offset, at + offset + size)

    def prepare(seq):
        for copy in land(seq):
            copy.wait()
        start = big_cell_start(seg_smem, seq, length)
        slot = lax.rem(seq, 2)

        def take(tile, at):
            return turn[tile, pl.ds(start + at, CHUNK), :]

        for k, source in enumerate((land_x, land_c)):

            def lay(index, at):
                for tile in range(tiles):
                    lanes = slice(tile * 128, (tile + 1) * 128)
                    piece = source[slot, tokens_at(at), lanes].astype(f32)
                    turn[2 * k + tile, tokens_at(at), :] = piece
                    if index < HALF // CHUNK:
                        turn[2 * k + tile, tokens_at(at, length), :] = piece

            chunks(lay)

        def bring(index, at):
            for k, target in enumerate((xT, cT)):
                piece = jnp.concatenate([take(2 * k + tile, at) for tile in range(tiles)], axis=1)
                piece = piece.astype(bf16)
                if k == 0:
                    xtok[seq, tokens_at(at), :] = piece
                else:
                    accc[...] += nn(some_ones, piece)
                target[seq, 0:width, tokens_at(at)] = nt(identity, piece).astype(bf16)

        chunks(bring)

        @pl.when(seq + 2 < count)
        def _():
            for copy in land(seq + 2):
                copy.start()

        def mark(index, at):
            position = at + lax.broadcasted_iota(jnp.int32, (1, CHUNK), 1)
            code = lax.broadcasted_iota(jnp.int32, (8, CHUNK), 0)
            hidden = (padv[pl.ds(seq, 1), tokens_at(at)] != 1).astype(f32)
            same = (segv[pl.ds(seq, 1), tokens_at(at)] == code).astype(f32)
            parts_q = [1.0 - same]
            parts_k = [same * mask_step]
            for digit in ((position // 64) % 8, (position // 8) % 8, position % 8):
                equal = (digit == code).astype(f32)
                parts_q.append(1.0 - equal)
                parts_k.append(equal * hidden * mask_step)
            both = jnp.concatenate(parts_k + parts_q + parts_k + parts_q, axis=0).astype(bf16)
            flat = nt(identity, both)
            turn[0, tokens_at(at), :] = flat
            if index < HALF // CHUNK:
                turn[0, tokens_at(at, length), :] = flat

        chunks(mark)
        nothing = jnp.zeros((32, CHUNK), f32)

        def bring_marks(index, at):
            piece = take(0, at).astype(bf16)
            codek[seq, tokens_at(at), :] = piece
            across = nt(identity[0:128, 0:128], piece)
            codeq[seq, :, tokens_at(at)] = jnp.concatenate([across[32:64], nothing], axis=0).astype(
                bf16
            )

        chunks(bring_marks)

    def prepare_step(seq, carry):
        prepare(seq)

        @pl.when(seq == 0)
        def _():
            gather_a.second()
            gather_b.first()

        if count > 1:

            @pl.when(seq == 1)
            def _():
                gather_a.third()

        if count > 2:

            @pl.when(seq == 2)
            def _():
                gather_b.second()

        return carry

    lax.fori_loop(0, count, prepare_step, 0)
    if count <= 1:
        gather_a.third()
    if count <= 2:
        gather_b.second()
    gather_a.finish()

    def stacked(held, at, depth):
        stack = []
        for device in range(devices):
            outer, inner = device // inners, device % inners
            stack.append(held[outer % 2, outer // 2, inner].astype(f32)[at : at + depth])
        return jnp.concatenate(stack, axis=0)

    columns = stacked(held_a, 0, share)
    def unpack(held, at, matrices):
        for straight, across, source in matrices:
            depth = source.shape[0]
            for column in range(0, straight.shape[1], 128):
                whole = stacked(held, at, depth)
                straight[:, column : column + 128] = whole.astype(bf16)
                if across is wjt and column < width:
                    whole = whole * scale
                across[column : column + 128, :] = whole.T.astype(bf16)
                at += depth

    unpack(held_a, share, ((wj, wjt, shards[0]),))

    def spread(at):
        return jnp.broadcast_to(columns[:, at : at + 1], (width, 128))

    bj[0:width, :] = spread(0) * scale
    bj[width : 2 * width, :] = jnp.zeros((width, 128), f32)
    bj[2 * width : 3 * width, :] = spread(1)
    for at in range(6):
        bcol[at, :, :] = spread(2 + at)
    halves = [spread(8), spread(9)]
    be[...] = jnp.concatenate(
        [halves[k % 2][k // 2 * share : (k // 2 + 1) * share] for k in range(2 * devices)], axis=0
    )
    vrow[...] = columns.T[0:8, :]

    lane = lax.broadcasted_iota(jnp.int32, (CHUNK, 128), 1)
    low_lanes = lane < HEAD_DIM
    halves = [slice(t, t + 128) for t in range(0, CHUNK, 128)]
    ones = jnp.ones((16, HALF), bf16)

    def add_sums(row, values):
        accb[row : row + values.shape[0], :] += values

    def out_copy(seq):
        return pltpu.make_async_copy(xtok.at[seq], out_hbm.at[seq], out_sem.at[seq])

    def attend(seq, between=()):
        between = dict(between)

        def project(index, at):
            made = nn(wjt[...], xT[seq, 0:width, tokens_at(at)])
            flat = nn(xtok[seq, tokens_at(at), :], wj[:, width : 3 * width])
            for half in halves:
                there = tokens_at(at, half.start, 128)
                low = (made[:, half] + bj[...]).astype(bf16)
                qkT[seq, :, there] = low[0 : 2 * width]
                vT[:, there] = low[2 * width : 3 * width]
            vtok[seq, tokens_at(at), :] = (flat[:, width : 2 * width] + vrow[1:2, :]).astype(bf16)
            codes = codek[seq, tokens_at(at), :].astype(f32)
            for head in range(HEADS):
                lanes = slice((head // 2) * 128, (head // 2 + 1) * 128)
                mine = low_lanes if head % 2 == 0 else ~low_lanes
                kaug[head, tokens_at(at), :] = jnp.where(mine, flat[:, lanes], codes).astype(bf16)

        chunks(project)

        units = [
            (head, block, at)
            for head in range(HEADS)
            for block in range(blocks)
            for at in range(0, HALF, CHUNK)
        ]

        def scores_of(head, block, at):
            there = tokens_at(block * HALF, at)
            own = slice(head * HEAD_DIM, (head + 1) * HEAD_DIM)
            parts = [qkT[seq, own, there], codeq[seq, :, there]]
            if head % 2:
                parts = parts[::-1]
            keys = kaug[head, tokens_at(block * HALF, 0, HALF), :]
            return nn(keys, jnp.concatenate(parts, axis=0))

        def mix(head, block, at):
            own = slice(head * HEAD_DIM, (head + 1) * HEAD_DIM)
            there = tokens_at(block * HALF, at)
            values = vT[own, tokens_at(block * HALF, 0, HALF)]
            mixed = nn(
                jnp.concatenate([values, ones], axis=0),
                pT[seq, head * blocks + block, :, at : at + CHUNK],
            )
            inverse = 1.0 / mixed[HEAD_DIM : HEAD_DIM + 1, :]
            inv[head : head + 1, there] = inverse
            mixT[own, there] = (mixed[0:HEAD_DIM, :] * inverse).astype(bf16)

        coming = scores_of(*units[0])
        for k, (head, block, at) in enumerate(units):
            scores = coming
            if k + 1 < len(units):
                coming = scores_of(*units[k + 1])
            place = head * blocks + block
            for tile in range(0, CHUNK, 128):
                mine = scores[:, tile : tile + 128]
                highest = jnp.max(mine, axis=0, keepdims=True)
                pT[seq, place, :, at + tile : at + tile + 128] = jnp.exp2(
                    (mine - highest) * log2_e
                ).astype(bf16)
            if k:
                mix(*units[k - 1])
            if k in between:
                between[k]()
        mix(*units[-1])

    def dense(seq, side, at):
        rows = tokens_at(at)
        branch = nn(wot[...], mixT[0:width, rows])
        firsts = []
        for half in halves:
            there = tokens_at(at, half.start, 128)
            hat, inverse = unit(
                xT[seq, 0:width, there].astype(f32) + branch[:, half] + bcol[0], width
            )
            hat1[side, :, half] = hat
            rinv1[side, 0:1, half] = inverse
            first = hat * bcol[1] + bcol[2]
            flow[0:width, there] = first.astype(bf16)
            firsts.append(first)
            yield
        inner = nn(wet[...], flow[0:width, rows])
        for half in halves:
            there = tokens_at(at, half.start, 128)
            for r in range(0, inner_width, 32):
                u = inner[r : r + 32, half] + be[r : r + 32, :]
                square = u * u
                t = jnp.tanh(u * (gelu_a + (gelu_a * gelu_b) * square))
                h = 0.5 + 0.5 * t
                value = u * h
                act[r : r + 32, there] = value.astype(bf16)
                dgelu[side, r : r + 32, half] = h + value * (1.0 - h) * (
                    2.0 * gelu_a + (6.0 * gelu_a * gelu_b) * square
                )
                if r % 256 == 224:
                    yield
        second = nn(wrt[...], act[0:inner_width, rows])
        grads, results, gains = [], [], []
        for k, half in enumerate(halves):
            there = tokens_at(at, half.start, 128)
            hat, inverse = unit(firsts[k] + second[:, half] + bcol[3], width)
            results.append((hat * bcol[4] + bcol[5]).astype(bf16))
            upstream = cT[seq, :, there].astype(f32)
            gains.append(upstream * hat)
            back = unit_back(upstream * bcol[4], hat, inverse, width)
            slow[:, there] = back.astype(bf16)
            grads.append(back)
            yield
        add_sums(0, gains[0] + gains[1])
        active_grad = nn(wr[...], slow[:, rows])
        xtok[seq, rows, :] = nt(identity, jnp.concatenate(results, axis=1)).astype(bf16)
        for half in halves:
            there = tokens_at(at, half.start, 128)
            for r in range(0, inner_width, 32):
                igr[r : r + 32, there] = (
                    active_grad[r : r + 32, half] * dgelu[side, r : r + 32, half]
                ).astype(bf16)
            yield
        deeper = nn(we[...], igr[:, rows])
        gains, shifts = [], []
        for k, half in enumerate(halves):
            there = tokens_at(at, half.start, 128)
            first_grad = grads[k] + deeper[:, half]
            hat = hat1[side, :, half]
            gains.append(first_grad * hat)
            shifts.append(first_grad)
            back = unit_back(first_grad * bcol[1], hat, rinv1[side, 0:1, half], width)
            blow[seq, :, there] = back.astype(bf16)
            yield
        add_sums(width, gains[0] + gains[1])
        add_sums(2 * width, shifts[0] + shifts[1])
        grown = nn(wo[...], blow[seq, :, rows]).astype(bf16).astype(f32)
        for head in range(HEADS):
            own = slice(head * HEAD_DIM, (head + 1) * HEAD_DIM)
            piece = grown[own, :] * inv[head : head + 1, rows]
            total = over_features(piece * mixT[own, rows].astype(f32))
            high = total.astype(bf16).astype(f32)
            dots[seq, 2 * head : 2 * head + 1, rows] = high
            dots[seq, 2 * head + 1 : 2 * head + 2, rows] = total - high
            doT[seq, own, rows] = piece.astype(bf16)
        yield

    def weight_sums(seq):
        gr[...] += nt(act[...], slow[...])
        ge[...] += nt(flow[...], igr[...])
        go[...] += nt(mixT[...], blow[seq])

    low_half = lax.broadcasted_iota(jnp.int32, (HALF, 128), 1) < HEAD_DIM
    keep = [low_half.astype(f32).astype(bf16), (~low_half).astype(f32).astype(bf16)]
    fill = [-keep[1], -keep[0]]
    extra_row = lax.broadcasted_iota(jnp.int32, (16, HALF), 0)

    def attend_back(seq, index):
        pair, block = index // blocks, index % blocks
        first = block * HALF
        lanes = slice(pair * 128, pair * 128 + 128)
        cols = tokens_at(first, 0, HALF)
        for odd in range(2):
            head = pair * 2 + odd
            own = slice(head * HEAD_DIM, (head + 1) * HEAD_DIM)
            key_rows = slice(width + own.start, width + own.stop)
            place = head * blocks + block
            high = dots[seq, 2 * head : 2 * head + 1, cols]
            rest = dots[seq, 2 * head + 1 : 2 * head + 2, cols]
            extra = jnp.where(extra_row == 0, high, jnp.where(extra_row == 1, rest, 0.0))
            extra = jnp.concatenate([extra, jnp.zeros((HEAD_DIM - 16, HALF), f32)], axis=0)
            grown = doT[seq, own, cols]
            stack = [grown, extra.astype(bf16)]
            if odd:
                stack = stack[::-1]
            stack = jnp.concatenate(stack, axis=0)
            side = vtok[seq, cols, lanes] * keep[odd] + fill[odd]
            for at in range(0, HALF, CHUNK):
                part = slice(at, at + CHUNK)
                grads = nn(side, stack[:, part])
                dsT[odd, :, part] = (pT[seq, place, :, part].astype(f32) * grads).astype(bf16)
                yield
            value_grad = nt(grown, pT[seq, place]).astype(bf16)
            yield
            key_grad = nt(qkT[seq, own, cols], dsT[odd]).astype(bf16)
            yield
            query_grad = (nn(qkT[seq, key_rows, cols], dsT[odd]) * scale).astype(bf16)
            yield
            doT[seq, own, cols] = value_grad
            qkT[seq, key_rows, cols] = key_grad
            qkT[seq, own, cols] = query_grad

    def joint_sums(seq, pair):
        for third in range(3):
            source = doT if third == 2 else qkT
            at = pair * 128 + (width if third == 1 else 0)
            lanes = slice(third * width + pair * 128, third * width + (pair + 1) * 128)
            gj[:, lanes] += nt(xT[seq], source[seq, at : at + 128, :])

    def together(*parts):
        parts = list(parts)
        while parts:
            for part in list(parts):
                if next(part, parts) is parts:
                    parts.remove(part)

    def chains(seq):
        def chain(side):
            chunk_count = length // CHUNK
            for index in range(side * chunk_count // 2, (side + 1) * chunk_count // 2):
                yield from dense(seq, side, index * CHUNK)

        return [chain(0), chain(1)]

    attend(0, {4: gather_b.third})
    gather_b.finish()
    unpack(
        held_b, 0, ((wo, wot, shards[1]), (we, wet, shards[2]), (wr, wrt, shards[3]))
    )
    together(*chains(0))
    weight_sums(0)

    def middle(seq, carry):
        attend(seq)
        together(*chains(seq))
        weight_sums(seq)
        return carry

    lax.fori_loop(1, count, middle, 0)

    def pack(reduce, sources):
        for device in range(devices):
            outer = device // inners
            pieces = []
            for ref in sources:
                depth = ref.shape[0] // devices
                pieces += column_blocks(ref[device * depth : (device + 1) * depth, :])
            packed = reduce.packed
            packed[outer % 2, outer // 2, device % inners] = padded_rows(pieces, packed.shape[3])

    sum_a, sum_b, sum_c = Reduce(peers, *reduce_a), Reduce(peers, *reduce_b), Reduce(peers, *reduce_c)
    pack(sum_a, (go.at[0:width], ge.at[0:width], gr.at[0:inner_width]))
    sum_a.first()

    def joint_columns(pair):
        return [
            gj.at[0:width, third * width + pair * 128 : third * width + (pair + 1) * 128]
            for third in range(3)
        ]

    def back_of(pair, steps):
        def back(seq, carry):
            for block in range(blocks):
                together(attend_back(seq, pair * blocks + block))
            joint_sums(seq, pair)
            for at, step in steps.items():

                @pl.when(seq == min(at, count - 1))
                def _():
                    step()

            return carry

        lax.fori_loop(0, count, back, 0)

    back_of(0, {1: sum_a.second})
    pack(sum_b, joint_columns(0))
    sum_b.first()
    back_of(1, {0: sum_a.third, 1: sum_b.second})
    rows = [
        gj[width : width + 1, 0:width],
        gj[width : width + 1, 2 * width : 3 * width],
        go[width : width + 1, :],
        jnp.zeros((2, width), f32),
        gr[inner_width : inner_width + 1, :],
        jnp.zeros((1, width), f32),
        accc[0:1, :],
    ]
    missing = 128 - sum(row.shape[0] for row in rows)
    columns = jnp.concatenate(rows + [jnp.zeros((missing, width), f32)], axis=0).T
    lanes = lax.broadcasted_iota(jnp.int32, (width, 128), 1)
    for at, place in ((6, 0), (3, width), (4, 2 * width)):
        total = jnp.sum(accb[place : place + width, :], axis=1, keepdims=True)
        columns = jnp.where(lanes == at, total, columns)
    wide = jnp.broadcast_to(ge[width : width + 1, :], (128, inner_width)).T
    for first in range(2):
        item = [wide[k * share : (k + 1) * share] for k in range(first, 2 * devices, 2)]
        columns = jnp.where(lanes == VECTORS + first, jnp.concatenate(item, axis=0), columns)
    bcol[0] = columns
    pack(sum_c, [bcol.at[0]] + joint_columns(1))
    sum_c.first()

    def tg_copies(seq):
        return [
            pltpu.make_async_copy(
                turn.at[tiles + tile, pl.ds(0, length)],
                tg_hbm.at[seq, :, pl.ds(tile * 128, 128)],
                tg_sem.at[tile],
            )
            for tile in range(tiles)
        ]

    def turn_back(tile, at, piece):
        turn[tile, HALF + at : HALF + at + CHUNK, :] = piece
        if at >= HALF:
            turn[tile, at - HALF : at - HALF + CHUNK, :] = piece

    def inputs_back(seq, carry):
        start = big_cell_start(seg_smem, seq, length)

        def give_back(tile, at):
            return turn[tile, pl.ds(HALF - start + at, CHUNK), :]

        def lay(index, at):
            for tile in range(tiles):
                lanes = slice(tile * 128, (tile + 1) * 128)
                turn_back(tile, at, xtok[seq, tokens_at(at), lanes].astype(f32))

        def give_out(index, at):
            for tile in range(tiles):
                lanes = slice(tile * 128, (tile + 1) * 128)
                xtok[seq, tokens_at(at), lanes] = give_back(tile, at).astype(bf16)

        chunks(lay)
        chunks(give_out)
        out_copy(seq).start()

        @pl.when(seq >= 1)
        def _():
            for copy in tg_copies(seq - 1):
                copy.wait()

        def one(index, at):
            rows = tokens_at(at)
            result = (
                nn(wj[:, 0 : 2 * width], qkT[seq, :, rows])
                + nn(wj[:, 2 * width : 3 * width], doT[seq, :, rows])
                + blow[seq, :, rows].astype(f32)
            ).T
            for tile in range(tiles):
                turn_back(tile, at, result[:, tile * 128 : (tile + 1) * 128])

        def give_grad(index, at):
            for tile in range(tiles):
                turn[tiles + tile, tokens_at(at), :] = give_back(tile, at)

        chunks(one)
        chunks(give_grad)
        for copy in tg_copies(seq):
            copy.start()

        @pl.when(seq == 0)
        def _():
            sum_b.third()
            sum_c.second()

        if count > 2:

            @pl.when(seq == 2)
            def _():
                sum_c.third()

        return carry

    lax.fori_loop(0, count, inputs_back, 0)
    if count <= 2:
        sum_c.third()
    fin_a[...] = sum_a.finish()
    fin_b[...] = sum_b.finish()
    fin_c[...] = sum_c.finish()
    for seq in range(count):
        out_copy(seq).wait()
    for copy in tg_copies(count - 1):
        copy.wait()


def run_layer(outers, inners, tokens, segment_ids, padding_mask, cotangent, shards):
    count, length, width = tokens.shape
    devices = outers * inners
    share = width // devices
    inner_width = shards[2].shape[1]
    tiles = width // 128
    chips = outers // 2
    blocks = length // HALF

    def rows_of(items):
        return sum(item.size // 128 for item in items)

    held_a = rounded_up(share + rows_of(shards[:1]), 16)
    held_b = rounded_up(rows_of(shards[1:4]), 16)
    dma = pltpu.SemaphoreType.DMA
    vmem = pltpu.VMEM
    shape = jax.ShapeDtypeStruct
    scratch = [vmem(item.shape, bf16) for item in shards]
    scratch += [
        vmem((2, length, width), bf16),
        vmem((2, length, width), bf16),
        vmem((count, length), jnp.int32),
        vmem((count, length), jnp.int32),
        pltpu.SMEM((count, length), jnp.int32),
        vmem((width, 3 * width), bf16),
        vmem((width, width), bf16),
        vmem((width, inner_width), bf16),
        vmem((inner_width, width), bf16),
        vmem((3 * width, width), bf16),
        vmem((width, width), bf16),
        vmem((inner_width, width), bf16),
        vmem((width, inner_width), bf16),
        vmem((3 * width, 128), f32),
        vmem((inner_width, 128), f32),
        vmem((6, width, 128), f32),
        vmem((8, width), f32),
        vmem((2 * tiles, length + HALF, 128), f32),
        vmem((count, length, width), bf16),
        vmem((count, width + 16, length), bf16),
        vmem((count, width, length), bf16),
        vmem((count, length, 128), bf16),
        vmem((count, HEAD_DIM, length), bf16),
        vmem((count, 2 * width, length), bf16),
        vmem((width, length), bf16),
        vmem((HEADS, length, 128), bf16),
        vmem((count, length, width), bf16),
        vmem((count, HEADS * blocks, HALF, HALF), bf16),
        vmem((8, length), f32),
        vmem((width + 16, length), bf16),
        vmem((2, width, CHUNK), f32),
        vmem((2, 8, CHUNK), f32),
        vmem((inner_width + 16, length), bf16),
        vmem((width, length), bf16),
        vmem((inner_width, length), bf16),
        vmem((width + 16, length), bf16),
        vmem((count, width, length), bf16),
        vmem((2, inner_width, CHUNK), f32),
        vmem((2, HALF, HALF), bf16),
        vmem((count, 2 * HEADS, length), f32),
        vmem((width + 16, 3 * width), f32),
        vmem((width + 16, width), f32),
        vmem((width + 16, inner_width), f32),
        vmem((inner_width + 16, width), f32),
        vmem((3 * width, 128), f32),
        vmem((16, width), f32),
        vmem((2, chips, inners, held_a, 128), bf16),
        dma((inners + 2 * chips,)),
        dma((inners + 2 * chips,)),
        vmem((2, chips, inners, held_b, 128), bf16),
        dma((inners + 2 * chips,)),
        dma((inners + 2 * chips,)),
    ]
    sums_b = rounded_up(3 * share, 16)
    sums_c = rounded_up(4 * share, 16)
    for rows in (held_b, sums_b, sums_c):
        scratch += reduce_scratch(outers, inners, rows)
    scratch += [dma((len(shards) + 3,)), dma((2, 2)), dma((count,)), dma((tiles,))]
    hbm = pl.BlockSpec(memory_space=pl.ANY)
    return pl.pallas_call(
        functools.partial(layer_kernel, outers, inners),
        in_specs=[hbm] * (4 + len(shards)),
        out_specs=[hbm, hbm] + [pl.BlockSpec(memory_space=pltpu.VMEM)] * 3,
        out_shape=[
            shape(tokens.shape, bf16),
            shape(tokens.shape, f32),
            shape((held_b, 128), f32),
            shape((sums_b, 128), f32),
            shape((sums_c, 128), f32),
        ],
        scratch_shapes=scratch,
        compiler_params=pltpu.CompilerParams(
            collective_id=0, has_side_effects=True, vmem_limit_bytes=64 * 1024 * 1024 - 65536
        ),
        name="layer",
    )(tokens, cotangent, segment_ids, padding_mask, *shards)


def finish_kernel(out_made, tg_made, fin_a, fin_b, fin_c, *refs):
    layer_out, tokens_grad, matrices, vectors = *refs[:2], refs[2:6], refs[6:-4]
    tg_held, out_held, arrive, leave = refs[-4:]
    count, length = layer_out.shape[:2]
    ways = ((tg_made, tg_held, tokens_grad), (out_made, out_held, layer_out))
    arrivals, leavings = [], []
    for seq in range(count):
        for part in range(2):
            rows = pl.ds(part * length // 2, length // 2)
            for k, (source, held, target) in enumerate(ways):
                spot = (k, seq, part)
                source, held, target = [ref.at[seq, rows] for ref in (source, held, target)]
                arrivals.append(pltpu.make_async_copy(source, held, arrive.at[spot]))
                leavings.append(pltpu.make_async_copy(held, target, leave.at[spot]))
    for copy in arrivals:
        copy.start()
    rows = vectors[0].shape[0]
    lines = fin_c[0:rows, :].T
    for at, ref in enumerate(vectors[:-1]):
        ref[...] = lines[at, :]
    vectors[-1][...] = jnp.concatenate([lines[VECTORS, :], lines[VECTORS + 1, :]])
    for third in range(3):
        for pair, (source, at) in enumerate(((fin_b, 0), (fin_c, rows))):
            column = (third * (HEADS // 2) + pair) * 128
            at += third * rows
            matrices[0][:, column : column + 128] = source[at : at + rows, :]
    at = 0
    for ref in matrices[1:]:
        depth = ref.shape[0]
        for column in range(0, ref.shape[1], 128):
            ref[:, column : column + 128] = fin_a[at : at + depth, :]
            at += depth
    for arrival, leaving in zip(arrivals, leavings):
        arrival.wait()
        leaving.start()
    for leaving in leavings:
        leaving.wait()


def finish(out_made, tg_made, fin_a, fin_b, fin_c, shards):
    hbm = pl.BlockSpec(memory_space=pl.ANY)
    vmem = pl.BlockSpec(memory_space=pltpu.VMEM)
    shape = jax.ShapeDtypeStruct
    return pl.pallas_call(
        finish_kernel,
        in_specs=[hbm, hbm] + [vmem] * 3,
        out_specs=[hbm, hbm] + [vmem] * len(shards),
        out_shape=[shape(out_made.shape, bf16), shape(tg_made.shape, f32)]
        + [shape(item.shape, f32) for item in shards],
        scratch_shapes=[
            pltpu.VMEM(tg_made.shape, f32),
            pltpu.VMEM(out_made.shape, bf16),
            pltpu.SemaphoreType.DMA((2, out_made.shape[0], 2)),
            pltpu.SemaphoreType.DMA((2, out_made.shape[0], 2)),
        ],
        compiler_params=pltpu.CompilerParams(vmem_limit_bytes=60 * 1024 * 1024),
        name="finish",
    )(out_made, tg_made, fin_a, fin_b, fin_c)


def on_device(
    outers,
    inners,
    tokens,
    segment_ids,
    padding_mask,
    joint_weight,
    query_bias,
    value_bias,
    output_weight,
    output_bias,
    first_gain,
    first_shift,
    expand_weight,
    expand_bias,
    reduce_weight,
    reduce_bias,
    second_gain,
    second_shift,
    cotangent,
):
    shards = (
        joint_weight,
        output_weight,
        expand_weight,
        reduce_weight,
        query_bias,
        value_bias,
        output_bias,
        first_gain,
        first_shift,
        reduce_bias,
        second_gain,
        second_shift,
        expand_bias,
    )
    turned = run_layer(outers, inners, tokens, segment_ids, padding_mask, cotangent, shards)
    layer_out, tokens_grad, *owned = finish(*turned, shards)
    gj, go, ge, gr, query, value, out, gain1, shift1, reduce, gain2, shift2, expand = owned
    return (
        layer_out,
        tokens_grad,
        gj,
        query,
        value,
        go,
        out,
        gain1,
        shift1,
        ge,
        expand,
        gr,
        reduce,
        gain2,
        shift2,
    )


def solution(mesh):
    rows = P(("outer", "inner"))
    rows2 = P(("outer", "inner"), None)
    rows3 = P(("outer", "inner"), None, None)
    weights = (rows2, rows, rows, rows2, rows, rows, rows, rows2, rows, rows2, rows, rows, rows)
    return jax.shard_map(
        functools.partial(on_device, mesh.shape["outer"], mesh.shape["inner"]),
        mesh=mesh,
        in_specs=(rows3, rows2, rows2) + weights + (rows3,),
        out_specs=(rows3, rows3) + weights,
        check_vma=False,
    )
```
